128 devices in a mesh: llm: 16 (over y, x), enc: 8 (over z, core).
Axes of the slice: x: 4, y: 4, z: 4, core: 2. Of those that a mesh axis runs over, the one named last changes fastest.
Arguments:
- patches: bfloat16 [16384, 1152], P(('llm', 'enc')), may hold values from -6 to 6
- image_seg: int32 [128, 1, 128], replicated, may hold values from 0 to 3, never falling along the last dimension, each value on 1 to 64 neighbouring positions
- owner_slot: int32 [128, 1], replicated, may hold values from 0 to 15, as said below
- place_start: int32 [128, 1], P(('llm', 'enc')), may hold values from 0 to 32, as said below
- text_embeds: bfloat16 [20480, 1280], P(('llm', 'enc')), may hold values from -6 to 6
- merged_grad: bfloat16 [20480, 1280], P(('llm', 'enc')), may hold values from -0.4375 to 0.4375
- w_patch: bfloat16 [1152, 1280], replicated, may hold values from -0.1875 to 0.1875
- w_qkv: bfloat16 [1280, 3840], replicated, may hold values from -1.118034 to 1.118034
- w_out: bfloat16 [1280, 1280], replicated, may hold values from -0.15625 to 0.15625
Outputs:
- merged: bfloat16 [20480, 1280], P(('llm', 'enc'))
- grad_patch: float32 [1152, 1280], P(None, ('llm', 'enc'))
- grad_out: float32 [1280, 1280], P(None, ('llm', 'enc'))
The draws below stay inside these ranges and needn't reach their ends.
Inputs may be any that keep to these rules, and one draw needn't show every extreme that they name: `image_seg`: within each sample's block of 128 rows, image numbers start at 0 and never fall. `owner_slot`: a value q + m names LLM rank q (device on the same enc index) and its placeholder block m; the samples of one device name distinct ranks; among the devices of one enc index every pair of rank and block is named exactly once. `place_start`: block m starts between m * 160 and m * 160 + 32.
All inputs are finite; a program needn't handle non-finite values.
Results may differ from the reference program's by a relative error of at most 0.014.
Values may be sent and summed in bfloat16 or wider, within the bound.
A program may use at most 128 MiB of HBM per device.

```python
import math
import jax
import jax.numpy as jnp
import numpy as np
from jax import lax

D = 1280
HEADS = 16
HEAD_DIM = 80
PIN = 1152
GROUP_ROWS = 128
GROUPS_DEV = 1
STRIDE = 160
IMG_GROUP = 4
SEG_MOST = 64
PATCH_DEV = 128
SEQ_DEV = 160
PATCHES = 16384
SEQ_ALL = 20480
N_LLM = 16
N_ENC = 8
DEVICES = 128


def column_owners(column_key):
    relabel_key, group_key, source_key, slot_key = jax.random.split(column_key, 4)
    relabel = jax.random.permutation(relabel_key, N_LLM)
    group_shift = jax.random.permutation(group_key, N_LLM)[:GROUPS_DEV]
    source_shift = jax.random.permutation(source_key, N_LLM)
    slot_order = jax.random.permutation(slot_key, GROUPS_DEV)
    target_rank = relabel[(source_shift[:, None] + group_shift[None, :]) % N_LLM]
    return target_rank * GROUPS_DEV + slot_order[None, :]


def draw_owner_slot(key, part):
    key = jax.random.fold_in(key, 5)
    per_column = jax.vmap(column_owners)(jax.random.split(key, N_ENC))
    return jnp.transpose(per_column, (1, 0, 2)).reshape(N_LLM * N_ENC, GROUPS_DEV).astype(jnp.int32)


def draw_place_start(key, part):
    key = jax.random.fold_in(key, 7)
    offsets = jax.random.randint(key, (DEVICES, GROUPS_DEV), 0, STRIDE - GROUP_ROWS + 1, dtype=jnp.int32)
    offsets = offsets.at[0, 0].set(0).at[0, GROUPS_DEV - 1].set(STRIDE - GROUP_ROWS)
    return offsets + STRIDE * jnp.arange(GROUPS_DEV, dtype=jnp.int32)[None, :]


def draw_w_qkv(key, part):
    key = jax.random.fold_in(key, 11)
    base_key = jax.random.fold_in(key, 0)
    limit = 40.0 * D ** (-0.5)
    base = jnp.clip(jax.random.normal(base_key, (D, 3 * D), jnp.float32), -6.0, 6.0) * D ** (-0.5)
    return jnp.clip(base, -limit, limit).astype(jnp.bfloat16)


def raised(result, stream_key, source, target, shards_of, factor):
    owner, partner = [(jnp.arange(result.shape[axis_at]) // (result.shape[axis_at] // shards_of)).reshape([-1 if axis == axis_at else 1 for axis in range(result.ndim)]) for axis_at in (source, target)]
    chosen = jax.random.permutation(stream_key, shards_of)[partner]
    strong = (owner == chosen) | (owner == (partner + shards_of // 2) % shards_of)
    return jnp.where(strong, factor * result, result)


def shard_levels(stream_key, extent, shards, smallest, high):
    loudness = 1.0
    for position, blocks in shards:
        steps = jax.random.uniform(jax.random.fold_in(jax.random.fold_in(stream_key, 6), position), (blocks,), jnp.float32, smallest / len(shards), high / len(shards))
        loudness = loudness * jnp.repeat(jnp.exp(steps), extent[position] // blocks).reshape((-1,) + (1,) * (len(extent) - 1 - position))
    return loudness


def profile(number_of, total, most, slope):
    portions = [(1 << 20) // math.isqrt(standing ** slope) + 1 for standing in range(2, number_of + 1)]
    spare, given = total - most - (number_of - 1), [1] * (number_of - 1)
    while spare > 0:
        free = [i for i in range(number_of - 1) if given[i] < most]
        mass, remaining = sum([portions[i] for i in free]), spare
        for i in free:
            more = min(most - given[i], max(1, remaining * portions[i] // mass), spare)
            given[i] = given[i] + more
            spare = spare - more
    return np.array([most] + given)


def ragged_sizes(stream_key, number_of, total, most, slope):
    if number_of == 2:
        one = jax.random.randint(stream_key, (), max(1, total - most), min(most, total - 1) + 1)
        return jnp.stack([one, total - one])
    tallies = jnp.asarray(profile(number_of, total, most, slope), jnp.int32)
    pairs = (number_of - 1) // 2
    giver, taker = tallies[1:1 + 2 * pairs:2], tallies[2:2 + 2 * pairs:2]
    room = jnp.minimum(giver - 1, most - taker)
    shifted = jax.random.randint(jax.random.fold_in(stream_key, 1), (pairs,), 0, 1 << 20) % (room + 1)
    tallies = tallies.at[1:1 + 2 * pairs:2].set(giver - shifted).at[2:2 + 2 * pairs:2].set(taker + shifted)
    return tallies[jax.random.permutation(jax.random.fold_in(stream_key, 2), number_of)]


def noise(key, shape, spread, most, pieces=(), kind=jnp.bfloat16):
    level = shard_levels(key, shape, pieces, -0.22, 0.18) if pieces else 1.0
    array = jax.random.normal(key, shape, jnp.float32) * spread * level
    return jnp.minimum(jnp.maximum(array, -most), most).astype(kind)


def bell_draw_with(own_key, dims, deviation, bound, cuts, heavy, kind=jnp.bfloat16):
    values = deviation * jax.random.normal(own_key, dims, jnp.float32)
    if cuts:
        values = values * shard_levels(own_key, dims, cuts, -0.22, 0.18)
    return jnp.clip(raised(values, jax.random.fold_in(own_key, 3), *heavy), -bound, bound).astype(kind)


def setup_inputs(seed: int = 0) -> dict:
    key_of = jax.random.split(jax.random.key(seed), 10)
    patches = noise(key_of[0], (PATCHES, PIN), 1.0, 6.0, ((0, 128),))
    image_seg = jax.vmap(lambda own: jnp.searchsorted(jnp.cumsum(ragged_sizes(own, IMG_GROUP, GROUP_ROWS, SEG_MOST, 2)), jnp.arange(GROUP_ROWS), side="right"))(jax.random.split(key_of[1], DEVICES * GROUPS_DEV)).reshape((DEVICES, GROUPS_DEV, GROUP_ROWS)).astype(jnp.int32)
    owner_slot = draw_owner_slot(jax.random.fold_in(key_of[9], 71), 0)
    place_start = draw_place_start(jax.random.fold_in(key_of[9], 71), 0)
    text_embeds = noise(key_of[4], (SEQ_ALL, D), 1.0, 6.0, ((0, 128),))
    merged_grad = bell_draw_with(key_of[5], (SEQ_ALL, D), ((DEVICES * PATCH_DEV) ** -0.5), 0.4375, ((0, 128),), (0, 1, 128, 5.5))
    w_patch = noise(key_of[6], (PIN, D), PIN ** -0.5, 0.1875)
    w_qkv = draw_w_qkv(jax.random.fold_in(key_of[9], 71), 0)
    w_out = noise(key_of[8], (D, D), D ** -0.5, 0.15625)
    return dict(patches=patches, image_seg=image_seg, owner_slot=owner_slot, place_start=place_start, text_embeds=text_embeds, merged_grad=merged_grad, w_patch=w_patch, w_qkv=w_qkv, w_out=w_out)


def layer_norm(values_in):
    average = lax.optimization_barrier(jnp.mean(values_in, axis=-1, keepdims=True))
    centred = values_in - average
    inverse_std = lax.rsqrt(lax.optimization_barrier(jnp.mean(centred * centred, axis=-1, keepdims=True)) + 1e-06)
    return (centred * inverse_std, inverse_std)

def split_heads(packed, blocks, length):
    return packed.reshape(blocks, length, HEADS, HEAD_DIM)

def attention_forward(qkv_low, segments):
    blocks, length = segments.shape
    widened = qkv_low.astype(jnp.float32)
    queries = split_heads(widened[:, :, :D], blocks, length)
    keys_all = split_heads(widened[:, :, D:2 * D], blocks, length)
    values_all = split_heads(widened[:, :, 2 * D:], blocks, length)
    scores = jnp.einsum('bqhe,bkhe->bhqk', queries, keys_all) * HEAD_DIM ** (-0.5)
    same_image = segments[:, None, :, None] == segments[:, None, None, :]
    scores = jnp.where(same_image, scores, jnp.float32(-1e+30))
    row_max = lax.optimization_barrier(jnp.max(scores, axis=-1, keepdims=True))
    weights = jnp.exp(scores - row_max)
    probability = weights / lax.optimization_barrier(jnp.sum(weights, axis=-1, keepdims=True))
    probs_low = probability.astype(jnp.bfloat16)
    attended = jnp.einsum('bhqk,bkhe->bqhe', probs_low.astype(jnp.float32), values_all)
    attn_cache = (queries, keys_all, values_all, probability, probs_low)
    return (attended.reshape(blocks, length, D).astype(jnp.bfloat16), attn_cache)

def attention_backward(attn_cache, grad_attended):
    queries, keys_all, values_all, probability, probs_low = attn_cache
    blocks, length = (grad_attended.shape[0], grad_attended.shape[1])
    grad_heads = split_heads(grad_attended.astype(jnp.float32), blocks, length)
    grad_prob = jnp.einsum('bqhe,bkhe->bhqk', grad_heads, values_all)
    grad_score = probability * (grad_prob - lax.optimization_barrier(jnp.sum(grad_prob * probability, axis=-1, keepdims=True)))
    score_low = lax.optimization_barrier((grad_score * HEAD_DIM ** (-0.5)).astype(jnp.bfloat16)).astype(jnp.float32)
    grad_query = jnp.einsum('bhqk,bkhe->bqhe', score_low, keys_all)
    grad_key = jnp.einsum('bhqk,bqhe->bkhe', score_low, queries)
    grad_value = jnp.einsum('bhqk,bqhe->bkhe', probs_low.astype(jnp.float32), grad_heads)
    joined = jnp.concatenate([grad_query.reshape(blocks, length, D), grad_key.reshape(blocks, length, D), grad_value.reshape(blocks, length, D)], axis=-1)
    return joined.astype(jnp.bfloat16)

def encode(patch_block, segments, w_patch, w_qkv, w_out):
    blocks, length = segments.shape
    patch_rows = patch_block.reshape(blocks * length, PIN)
    residual = jnp.dot(patch_rows, w_patch, preferred_element_type=jnp.float32)
    normed, inverse_std = layer_norm(residual)
    normed_low = normed.astype(jnp.bfloat16)
    qkv_low = jnp.dot(normed_low, w_qkv, preferred_element_type=jnp.float32).astype(jnp.bfloat16)
    attended, attn_cache = attention_forward(qkv_low.reshape(blocks, length, 3 * D), segments)
    attended_rows = attended.reshape(blocks * length, D)
    output = residual + jnp.dot(attended_rows, w_out, preferred_element_type=jnp.float32)
    stored = (patch_rows, normed, inverse_std, attended_rows, attn_cache)
    return (output.astype(jnp.bfloat16).reshape(blocks, length, D), stored)

def backprop(stored, upstream, w_qkv, w_out):
    patch_rows, normed, inverse_std, attended_rows, attn_cache = stored
    blocks = attn_cache[3].shape[0]
    length = attn_cache[3].shape[2]
    grad_out = jnp.dot(attended_rows.T, upstream, preferred_element_type=jnp.float32)
    grad_attended = jnp.dot(upstream, w_out.T, preferred_element_type=jnp.float32).astype(jnp.bfloat16)
    grad_qkv_low = attention_backward(attn_cache, grad_attended.reshape(blocks, length, D)).reshape(blocks * length, 3 * D)
    grad_normed = jnp.dot(grad_qkv_low, w_qkv.T, preferred_element_type=jnp.float32)
    mean_grad = lax.optimization_barrier(jnp.mean(grad_normed, axis=-1, keepdims=True))
    mean_cross = lax.optimization_barrier(jnp.mean(grad_normed * normed, axis=-1, keepdims=True))
    grad_residual = upstream.astype(jnp.float32) + inverse_std * (grad_normed - mean_grad - normed * mean_cross)
    grad_patch = jnp.dot(patch_rows.T, grad_residual.astype(jnp.bfloat16), preferred_element_type=jnp.float32)
    return (grad_patch, grad_out)

def reference(patches, image_seg, owner_slot, place_start, text_embeds, merged_grad, w_patch, w_qkv, w_out):
    devices = image_seg.shape[0]
    groups = image_seg.shape[1]
    length = image_seg.shape[2]
    device_ids = jnp.arange(devices, dtype=jnp.int32)
    target = owner_slot // groups * N_ENC + (device_ids % N_ENC)[:, None]
    slot_number = owner_slot % groups
    place_index = (target * groups + slot_number).reshape(-1).astype(jnp.int32)
    start_rows = place_start.reshape(-1)[place_index]
    positions = target.reshape(-1)[:, None] * SEQ_DEV + start_rows[:, None] + jnp.arange(length, dtype=jnp.int32)[None, :]
    positions = positions.astype(jnp.int32)
    upstream_all = merged_grad[positions.reshape(-1)].reshape(devices, groups, length, D)
    patch_groups = patches.reshape(devices, groups, length, PIN)

    def one_device(carry, item):
        patch_block, segments, upstream = item
        embedded, stored = encode(patch_block, segments, w_patch, w_qkv, w_out)
        parts = backprop(stored, upstream.reshape(groups * length, D), w_qkv, w_out)
        return ((carry[0] + parts[0], carry[1] + parts[1]), embedded)
    initial = (jnp.zeros((PIN, D), jnp.float32), jnp.zeros((D, D), jnp.float32))
    totals, embedded_all = lax.scan(one_device, initial, (patch_groups, image_seg, upstream_all))
    merged = text_embeds.at[positions.reshape(-1)].set(embedded_all.reshape(-1, D))
    return (merged, totals[0], totals[1])
```

```python
import jax
import jax.numpy as jnp
from jax import lax
from jax.experimental import pallas as pl
from jax.experimental.pallas import tpu as pltpu
from jax.sharding import PartitionSpec as P

D = 1280
HEADS = 16
HEAD_DIM = 80
PIN = 1152
ROWS = 128
SEQ = 160
N_LLM = 16
N_ENC = 8
HALF = 640
SCALE = HEAD_DIM ** (-0.5)
PART_COLS = ((0, 384), (384, 256))

BF = jnp.bfloat16
F32 = jnp.float32
MESH = pl.DeviceIdType.MESH
NN = (((1,), (0,)), ((), ()))
NT = (((1,), (1,)), ((), ()))
TN = (((0,), (0,)), ((), ()))


def mm(a, b, dims=NN):
    return lax.dot_general(a, b, dims, preferred_element_type=F32)


def iota(shape, axis):
    return lax.broadcasted_iota(jnp.int32, shape, axis)


def aligned(value, unit):
    return pl.multiple_of(value, unit)


def each(low, high, body):
    def step(i, carry):
        body(i)
        return carry

    lax.fori_loop(low, high, step, 0)


def head_window(j):
    first = 80 * j // 128 * 128
    last = -(-(80 * j + 80) // 128) * 128
    return first, last - first, 80 * j - first


def padded(rows, offset, width):
    pieces = []
    if offset:
        pieces.append(jnp.zeros((offset, ROWS), BF))
    pieces.append(rows)
    if width - offset - 80:
        pieces.append(jnp.zeros((width - offset - 80, ROWS), BF))
    return jnp.concatenate(pieces, axis=0)


def kernel(
    owner_ref, start_ref, seg_hbm, patches_hbm, text_hbm, mgrad_hbm, wp_hbm, wq_hbm, wo_hbm,
    merged_hbm, gpatch_ref, gout_ref,
    seg, pat, text, mgrad, wp, wq, wo,
    perm, sent1, recv1, sent2, emb_in, up, res, nlow, resT, qkv, qkvT, pT, plT, attT, att,
    upT, gaT, gqkvT, gnT, merged, uu, aa, gt, r1, s1, r2, s2, x3, r3,
    local_sem, ex_send, ex_recv, pair_send, pair_recv, p1_send, p1_recv, p2_send, p2_recv,
    p3_send, p3_recv,
):
    llm = lax.axis_index("llm")
    enc = lax.axis_index("enc")
    y, x = llm // 4, llm % 4
    core = enc % 2
    device = llm * N_ENC + enc
    start = start_ref[0, 0]

    def local(source, target, slot):
        return pltpu.make_async_copy(source, target, local_sem.at[slot])

    def remote(source, target, send, recv, to_llm, to_enc):
        return pltpu.make_async_remote_copy(
            src_ref=source, dst_ref=target, send_sem=send, recv_sem=recv,
            device_id=(to_llm, to_enc), device_id_type=MESH,
        )

    load_mgrad = local(mgrad_hbm, mgrad, 0)
    load_pat = local(patches_hbm, pat, 1)
    load_seg = local(seg_hbm.at[device], seg, 2)
    load_wp = local(wp_hbm, wp, 3)
    load_wq = [
        local(wq_hbm.at[:, pl.ds(D * i, D)], wq.at[:, pl.ds(D * i, D)], 4 + i) for i in range(3)
    ]
    load_wo = local(wo_hbm, wo, 7)
    load_text = local(text_hbm, text, 8)
    for load in (load_mgrad, load_pat, load_seg, load_wp, *load_wq, load_wo, load_text):
        load.start()

    barrier = pltpu.get_barrier_semaphore()

    def greet_llm(k):
        pl.semaphore_signal(
            barrier, inc=1, device_id=((llm + k) % N_LLM, enc), device_id_type=MESH
        )

    def greet_enc(k):
        pl.semaphore_signal(
            barrier, inc=1, device_id=(llm, (enc + k) % N_ENC), device_id_type=MESH
        )

    each(1, N_LLM, greet_llm)
    each(1, N_ENC, greet_enc)

    lane = iota((16, 256), 1)
    row = iota((16, 256), 0)

    def owner_rows(s):
        rank = owner_ref[0, s * N_ENC + enc]
        hit = (lane == rank * 16 + row).astype(F32)
        perm[pl.ds(aligned(s * 16, 16), 16), :] = hit.astype(BF)

    each(0, N_LLM, owner_rows)

    load_mgrad.wait()
    take = (iota((ROWS, SEQ), 1) == iota((ROWS, SEQ), 0) + start).astype(F32).astype(BF)
    sent1[0, :, :] = mm(take, mgrad[...]).astype(BF)

    pl.semaphore_wait(barrier, N_LLM - 1 + N_ENC - 1)

    def piece(ref, j):
        return ref.at[pl.ds(aligned(j // 2 * 16, 16), 16), pl.ds(aligned(j % 2 * HALF, 128), HALF)]

    def scatter(way, k):
        to = (llm + k) % N_LLM
        return remote(
            piece(sent1.at[way], to), recv1.at[way, pl.ds(aligned(llm * 16, 16), 16)],
            ex_send.at[way, 0, k], ex_recv.at[way, 0, k], to, enc,
        )

    def scatter_arrival(way, k):
        source = (llm + N_LLM - k) % N_LLM
        return remote(
            piece(sent1.at[way], llm), recv1.at[way, pl.ds(aligned(source * 16, 16), 16)],
            ex_send.at[way, 0, k], ex_recv.at[way, 0, k], (llm + k) % N_LLM, enc,
        )

    def deliver(way, target, k):
        to = (llm + k) % N_LLM
        return remote(
            sent2.at[way, pl.ds(aligned(to * 16, 16), 16)], piece(target, llm),
            ex_send.at[way, 1, k], ex_recv.at[way, 1, k], to, enc,
        )

    def deliver_arrival(way, target, k):
        source = (llm + N_LLM - k) % N_LLM
        return remote(
            sent2.at[way, pl.ds(aligned(llm * 16, 16), 16)], piece(target, source),
            ex_send.at[way, 1, k], ex_recv.at[way, 1, k], (llm + k) % N_LLM, enc,
        )

    def own_piece(ref):
        return ref[pl.ds(aligned(llm // 2 * 16, 16), 16), pl.ds(aligned(llm % 2 * HALF, 128), HALF)]

    def exchange_first(way):
        each(1, N_LLM, lambda k: scatter(way, k).start())
        recv1[way, pl.ds(aligned(llm * 16, 16), 16), :] = own_piece(sent1.at[way])

    def exchange_second(way, target, dims):
        each(1, N_LLM, lambda k: scatter_arrival(way, k).wait_recv())
        sent2[way, :, :] = mm(perm[...], recv1[way], dims).astype(BF)
        each(1, N_LLM, lambda k: deliver(way, target, k).start())
        target[pl.ds(aligned(llm // 2 * 16, 16), 16), pl.ds(aligned(llm % 2 * HALF, 128), HALF)] = (
            sent2[way, pl.ds(aligned(llm * 16, 16), 16), :]
        )

    def exchange_finish(way, target):
        each(1, N_LLM, lambda k: deliver_arrival(way, target, k).wait_recv())

    exchange_first(0)

    other = enc + 1 - 2 * core

    def to_pair(slot, source, target):
        return remote(source, target, pair_send.at[slot], pair_recv.at[slot], llm, other)

    load_pat.wait()
    pair_pat = to_pair(
        0, pat.at[:, pl.ds(aligned((1 - core) * 512, 128), HALF)], aa.at[1, pl.ds(ROWS, ROWS)]
    )
    pair_pat.start()
    aa[1, pl.ds(0, ROWS), :] = pat[:, pl.ds(aligned(core * 512, 128), HALF)]

    load_wp.wait()

    def project(i):
        columns = pl.ds(aligned(i * 256, 256), 256)
        res[:, columns] = mm(pat[...], wp[:, columns])

    each(0, 5, project)
    for i in range(4):
        rows = pl.ds(32 * i, 32)
        values = res[rows, :]
        centred = values - jnp.mean(values, axis=1, keepdims=True)
        inverse = lax.rsqrt(jnp.mean(centred * centred, axis=1, keepdims=True) + 1e-6)
        nlow[rows, :] = (centred * inverse).astype(BF)

    exchange_second(0, up, NN)

    def project_qkv(i):
        columns = pl.ds(aligned(i * 256, 256), 256)
        tile = mm(nlow[...], wq[:, columns]).astype(BF)
        qkv[:, columns] = tile
        qkvT[columns, :] = tile.T

    for i in range(3):
        load_wq[i].wait()
        each(5 * i, 5 * i + 5, project_qkv)

    load_seg.wait()
    one_hot = (iota((8, ROWS), 0) == seg[...]).astype(F32).astype(BF)
    same_image = mm(one_hot, one_hot, TN) > 0.5

    def forward_heads(g):
        base = g * HALF
        for j in range(8):
            first, width, offset = head_window(j)
            head = pl.ds(aligned(base + 80 * j, 16), 80)
            block = pl.ds(aligned((g * 8 + j) * ROWS, ROWS), ROWS)
            keys = qkv[:, pl.ds(aligned(D + base + first, 128), width)]
            scores = mm(keys, padded(qkvT[head, :], offset, width)) * SCALE
            scores = jnp.where(same_image, scores, -1e30)
            weights = jnp.exp(scores - jnp.max(scores, axis=0, keepdims=True))
            probability = weights / jnp.sum(weights, axis=0, keepdims=True)
            low = probability.astype(BF)
            pT[block, :] = probability
            plT[block, :] = low
            values = qkvT[pl.ds(aligned(2 * D + base + 80 * j, 16), 80), :]
            attT[head, :] = mm(values, low).astype(BF)

    each(0, 2, forward_heads)

    def turn_attended(i):
        block = pl.ds(aligned(i * 128, 128), 128)
        att[:, block] = attT[block, :].T

    each(0, 10, turn_attended)
    pair_att = to_pair(
        1, att.at[:, pl.ds(aligned((1 - core) * HALF, 128), HALF)], aa.at[0, pl.ds(ROWS, ROWS)]
    )
    pair_att.start()
    aa[0, pl.ds(0, ROWS), :] = att[:, pl.ds(aligned(core * HALF, 128), HALF)]

    exchange_finish(0, up)

    def turn_upstream(i):
        block = pl.ds(aligned(i * 128, 128), 128)
        upT[block, :] = up[:, block].T

    each(0, 10, turn_upstream)
    pair_up = to_pair(2, upT, uu.at[0, 1])
    pair_up.start()
    uu[0, 0, :, :] = upT[...]

    load_wo.wait()

    def project_out(i):
        columns = pl.ds(aligned(i * 256, 256), 256)
        sent1[1, :, columns] = (res[:, columns] + mm(att[...], wo[:, columns])).astype(BF)

    each(0, 5, project_out)
    exchange_first(1)

    def project_back(i):
        rows = pl.ds(aligned(i * 256, 256), 256)
        gaT[rows, :] = mm(wo[rows, :], upT[...]).astype(BF)

    each(0, 5, project_back)

    def gradient(grad):
        def block(b):
            rows = pl.ds(aligned(b * 80, 16), 80)
            total = mm(uu[grad, 0, rows, :], aa[grad, pl.ds(0, ROWS), :])
            total = total + mm(uu[grad, 1, rows, :], aa[grad, pl.ds(ROWS, ROWS), :])
            gt[grad, b // 4, b % 4] = total.astype(BF)

        each(0, 16, block)

    def first_copy(grad, part, along_y, k):
        first, width = PART_COLS[part]
        columns = pl.ds(first, width)
        if along_y:
            to = (y + k) % 4
            source, to_llm = gt.at[grad, to, :, :, columns], to * 4 + x
        else:
            to = (x + k) % 4
            source, to_llm = gt.at[grad, :, to, :, columns], y * 4 + to
        return remote(
            source, r1.at[grad, k - 1, :, :, columns],
            p1_send.at[grad, part, k - 1], p1_recv.at[grad, part, k - 1], to_llm, enc,
        )

    def second_copy(grad, part, along_y, k):
        first, width = PART_COLS[part]
        columns = pl.ds(first, width)
        if along_y:
            to = (y + k) % 4
            to_llm = to * 4 + x
        else:
            to = (x + k) % 4
            to_llm = y * 4 + to
        return remote(
            s1.at[grad, to, :, columns], r2.at[grad, k - 1, :, columns],
            p2_send.at[grad, part, k - 1], p2_recv.at[grad, part, k - 1], to_llm, enc,
        )

    def third_copy(grad, k):
        to = (enc + k) % N_ENC
        return remote(
            x3.at[grad, pl.ds(aligned(to * 16, 16), 16)], r3.at[grad, k - 1],
            p3_send.at[grad, k - 1], p3_recv.at[grad, k - 1], llm, to,
        )

    def by_core(run):
        @pl.when(core == 0)
        def _():
            run(True)

        @pl.when(core == 1)
        def _():
            run(False)

    def first_phase(grad):
        def run(straight):
            for k in range(1, 4):
                for part in range(2):
                    first_copy(grad, part, straight == (part == 0), k).start()

        by_core(run)

    def second_phase(grad):
        def run(straight):
            for part in range(2):
                first, width = PART_COLS[part]
                columns = pl.ds(first, width)
                along_y = straight == (part == 0)
                for k in range(1, 4):
                    first_copy(grad, part, along_y, k).wait_recv()

                def add(i, part=part, columns=columns, along_y=along_y):
                    own = gt[grad, y, i, :, columns] if along_y else gt[grad, i, x, :, columns]
                    total = own.astype(F32)
                    for k in range(3):
                        total = total + r1[grad, k, i, :, columns].astype(F32)
                    s1[grad, i, :, columns] = total.astype(BF)

                each(0, 4, add)
                for k in range(1, 4):
                    second_copy(grad, part, not along_y, k).start()

        by_core(run)

    def third_phase(grad):
        def run(straight):
            for part in range(2):
                first, width = PART_COLS[part]
                columns = pl.ds(first, width)
                along_y = straight != (part == 0)
                for k in range(1, 4):
                    second_copy(grad, part, along_y, k).wait_recv()
                total = s1[grad, y if along_y else x, :, columns].astype(F32)
                for k in range(3):
                    total = total + r2[grad, k, :, columns].astype(F32)
                s2[:, columns] = total.astype(BF)

        by_core(run)
        spread_row = iota((ROWS, 80), 0)
        spread = jnp.logical_and(
            iota((ROWS, 80), 1) == spread_row // 16 * 10 + spread_row % 16, spread_row % 16 < 10
        )
        x3[grad, :, :] = mm(spread.astype(F32).astype(BF), s2[...]).astype(BF)
        each(1, N_ENC, lambda k: third_copy(grad, k).start())

    def last_phase(grad, out_ref, shift):
        each(1, N_ENC, lambda k: third_copy(grad, k).wait_recv())
        mine = x3[grad, pl.ds(aligned(enc * 16, 16), 16), :].astype(F32)
        for k in (2, 4, 6):
            mine = mine + r3[grad, k - 1].astype(F32)
        theirs = r3[grad, 0].astype(F32)
        for k in (3, 5, 7):
            theirs = theirs + r3[grad, k - 1].astype(F32)
        out_ref[:, pl.ds(aligned(core * shift, 128), HALF)] = mine[:10, :]
        out_ref[:, pl.ds(aligned((1 - core) * shift, 128), HALF)] = theirs[:10, :]

    def finish_sends(grad):
        def run(straight):
            for part in range(2):
                along_y = straight == (part == 0)
                for k in range(1, 4):
                    first_copy(grad, part, along_y, k).wait_send()
                    second_copy(grad, part, not along_y, k).wait_send()

        by_core(run)
        each(1, N_ENC, lambda k: third_copy(grad, k).wait_send())

    pair_att.wait_recv()
    pair_up.wait_recv()
    gradient(0)
    first_phase(0)

    def backward_heads(g):
        base = g * HALF
        for j in range(8):
            first, width, offset = head_window(j)
            head = pl.ds(aligned(base + 80 * j, 16), 80)
            head_k = pl.ds(aligned(D + base + 80 * j, 16), 80)
            head_v = pl.ds(aligned(2 * D + base + 80 * j, 16), 80)
            block = pl.ds(aligned((g * 8 + j) * ROWS, ROWS), ROWS)
            values = qkv[:, pl.ds(aligned(2 * D + base + first, 128), width)]
            rows = gaT[head, :]
            grad_prob = mm(values, padded(rows, offset, width))
            probability = pT[block, :]
            weighted = jnp.sum(grad_prob * probability, axis=0, keepdims=True)
            low = (probability * (grad_prob - weighted) * SCALE).astype(BF)
            gqkvT[head, :] = mm(qkvT[head_k, :], low).astype(BF)
            gqkvT[head_k, :] = mm(qkvT[head, :], low, NT).astype(BF)
            gqkvT[head_v, :] = mm(rows, plT[block, :], NT).astype(BF)

    each(0, 2, backward_heads)

    exchange_second(1, emb_in, TN)
    second_phase(0)

    def turn_residual(i):
        block = pl.ds(aligned(i * 128, 128), 128)
        resT[block, :] = res[:, block].T

    each(0, 10, turn_residual)
    mean = jnp.sum(resT[...], axis=0, keepdims=True) * (1.0 / D)
    centred = resT[...] - mean
    inverse = lax.rsqrt(jnp.sum(centred * centred, axis=0, keepdims=True) * (1.0 / D) + 1e-6)

    def back_qkv(i, carry):
        rows = pl.ds(aligned(i * 256, 256), 256)
        tile = mm(wq[rows, :], gqkvT[...])
        gnT[rows, :] = tile
        normed = (resT[rows, :] - mean) * inverse
        return (
            carry[0] + jnp.sum(tile, axis=0, keepdims=True),
            carry[1] + jnp.sum(tile * normed, axis=0, keepdims=True),
        )

    zero = jnp.zeros((1, ROWS), F32)
    mean_grad, mean_cross = lax.fori_loop(0, 5, back_qkv, (zero, zero))
    mean_grad = mean_grad * (1.0 / D)
    mean_cross = mean_cross * (1.0 / D)

    third_phase(0)

    def residual_grad(i):
        rows = pl.ds(aligned(i * 256, 256), 256)
        normed = (resT[rows, :] - mean) * inverse
        total = upT[rows, :].astype(F32) + inverse * (
            gnT[rows, :] - mean_grad - normed * mean_cross
        )
        uu[1, 0, rows, :] = total.astype(BF)

    each(0, 5, residual_grad)
    pair_res = to_pair(3, uu.at[1, 0], uu.at[1, 1])
    pair_res.start()
    pair_pat.wait_recv()
    pair_res.wait_recv()
    gradient(1)
    first_phase(1)

    exchange_finish(1, emb_in)
    load_text.wait()
    position = iota((SEQ, ROWS), 0)
    put = (position == iota((SEQ, ROWS), 1) + start).astype(F32).astype(BF)

    def merge(i):
        columns = pl.ds(aligned(i * 256, 256), 256)
        placed = mm(put, emb_in[:, columns])
        place = iota((SEQ, 256), 0)
        inside = jnp.logical_and(place >= start, place < start + ROWS)
        merged[:, columns] = jnp.where(inside, placed, text[:, columns].astype(F32)).astype(BF)

    each(0, 5, merge)
    store_merged = local(merged, merged_hbm, 9)
    store_merged.start()
    last_phase(0, gout_ref, HALF)

    second_phase(1)
    third_phase(1)
    last_phase(1, gpatch_ref, 512)

    store_merged.wait()
    for pair in (pair_pat, pair_att, pair_up, pair_res):
        pair.wait_send()

    def finish_exchange(k):
        scatter(0, k).wait_send()
        scatter(1, k).wait_send()
        deliver(0, up, k).wait_send()
        deliver(1, emb_in, k).wait_send()

    each(1, N_LLM, finish_exchange)
    finish_sends(0)
    finish_sends(1)


def shards(
    patches, image_seg, owner_slot, place_start, text_embeds, merged_grad, w_patch, w_qkv, w_out
):
    smem = pl.BlockSpec(memory_space=pltpu.SMEM)
    anywhere = pl.BlockSpec(memory_space=pl.ANY)
    vmem = pl.BlockSpec(memory_space=pltpu.VMEM)
    dma = pltpu.SemaphoreType.DMA
    merged, grad_patch, grad_out = pl.pallas_call(
        kernel,
        out_shape=(
            jax.ShapeDtypeStruct((SEQ, D), BF),
            jax.ShapeDtypeStruct((10, PIN), F32),
            jax.ShapeDtypeStruct((10, D), F32),
        ),
        in_specs=[smem, smem] + [anywhere] * 7,
        out_specs=(anywhere, vmem, vmem),
        scratch_shapes=[
            pltpu.VMEM((1, ROWS), jnp.int32),
            pltpu.VMEM((ROWS, PIN), BF),
            pltpu.VMEM((SEQ, D), BF),
            pltpu.VMEM((SEQ, D), BF),
            pltpu.VMEM((PIN, D), BF),
            pltpu.VMEM((D, 3 * D), BF),
            pltpu.VMEM((D, D), BF),
            pltpu.VMEM((256, 256), BF),
            pltpu.VMEM((2, ROWS, D), BF),
            pltpu.VMEM((2, 256, HALF), BF),
            pltpu.VMEM((2, 256, HALF), BF),
            pltpu.VMEM((ROWS, D), BF),
            pltpu.VMEM((ROWS, D), BF),
            pltpu.VMEM((ROWS, D), F32),
            pltpu.VMEM((ROWS, D), BF),
            pltpu.VMEM((D, ROWS), F32),
            pltpu.VMEM((ROWS, 3 * D), BF),
            pltpu.VMEM((3 * D, ROWS), BF),
            pltpu.VMEM((HEADS * ROWS, ROWS), F32),
            pltpu.VMEM((HEADS * ROWS, ROWS), BF),
            pltpu.VMEM((D, ROWS), BF),
            pltpu.VMEM((ROWS, D), BF),
            pltpu.VMEM((D, ROWS), BF),
            pltpu.VMEM((D, ROWS), BF),
            pltpu.VMEM((3 * D, ROWS), BF),
            pltpu.VMEM((D, ROWS), F32),
            pltpu.VMEM((SEQ, D), BF),
            pltpu.VMEM((2, 2, D, ROWS), BF),
            pltpu.VMEM((2, 2 * ROWS, HALF), BF),
            pltpu.VMEM((2, 4, 4, 80, HALF), BF),
            pltpu.VMEM((2, 3, 4, 80, HALF), BF),
            pltpu.VMEM((2, 4, 80, HALF), BF),
            pltpu.VMEM((2, 3, 80, HALF), BF),
            pltpu.VMEM((80, HALF), BF),
            pltpu.VMEM((2, ROWS, HALF), BF),
            pltpu.VMEM((2, 7, 16, HALF), BF),
            dma((10,)),
            dma((2, 2, N_LLM)),
            dma((2, 2, N_LLM)),
            dma((4,)),
            dma((4,)),
            dma((2, 2, 3)),
            dma((2, 2, 3)),
            dma((2, 2, 3)),
            dma((2, 2, 3)),
            dma((2, 7)),
            dma((2, 7)),
        ],
        compiler_params=pltpu.CompilerParams(
            collective_id=0, has_side_effects=True, vmem_limit_bytes=56 * 1024 * 1024
        ),
    )(
        owner_slot.reshape(1, 128), place_start, image_seg, patches, text_embeds, merged_grad,
        w_patch, w_qkv, w_out,
    )
    return (merged, grad_patch.T, grad_out.T)


def solution(mesh):
    rows = P(("llm", "enc"), None)
    columns = P(None, ("llm", "enc"))
    return jax.shard_map(
        shards,
        mesh=mesh,
        in_specs=(rows, P(), P(), rows, rows, rows, P(), P(), P()),
        out_specs=(rows, columns, columns),
        check_vma=False,
    )
```

```python
import jax
import jax.numpy as jnp
from jax import lax
from jax.experimental import pallas as pl
from jax.experimental.pallas import tpu as pltpu
from jax.sharding import PartitionSpec as P

D = 1280
HEADS = 16
HEAD_DIM = 80
PIN = 1152
ROWS = 128
SEQ = 160
N_LLM = 16
N_ENC = 8
HALF = 640
SCALE = HEAD_DIM ** (-0.5)

OUT_PARTS = ((pl.ds(256, 384), 2), (pl.ds(0, 128), 0), (pl.ds(128, 128), 1))
OUT_STRAIGHT, OUT_CROSSED = pl.ds(0, 256), pl.ds(256, 384)
PATCH_PARTS = ((pl.ds(0, 256), 0), (pl.ds(256, 256), 1), (pl.ds(512, 128), 2))
PATCH_STRAIGHT, PATCH_CROSSED = pl.ds(0, 512), pl.ds(512, 128)

BF = jnp.bfloat16
F32 = jnp.float32
MESH = pl.DeviceIdType.MESH
NN = (((1,), (0,)), ((), ()))
NT = (((1,), (1,)), ((), ()))
TN = (((0,), (0,)), ((), ()))


def mm(a, b, dims=NN):
    return lax.dot_general(a, b, dims, preferred_element_type=F32)


def iota(shape, axis):
    return lax.broadcasted_iota(jnp.int32, shape, axis)


def aligned(value, unit):
    return pl.multiple_of(value, unit)


def each(low, high, body):
    def step(i, carry):
        body(i)
        return carry

    lax.fori_loop(low, high, step, 0)


def head_window(j):
    first = 80 * j // 128 * 128
    last = -(-(80 * j + 80) // 128) * 128
    return first, last - first, 80 * j - first


def padded(rows, offset, width):
    pieces = []
    if offset:
        pieces.append(jnp.zeros((offset, ROWS), BF))
    pieces.append(rows)
    if width - offset - 80:
        pieces.append(jnp.zeros((width - offset - 80, ROWS), BF))
    return jnp.concatenate(pieces, axis=0)


def kernel(
    owner_ref, start_ref, seg_hbm, patches_hbm, text_hbm, mgrad_hbm, wp_hbm, wq_hbm, wo_hbm,
    merged_hbm, gpatch_hbm, gout_hbm,
    seg, pat, text, mgrad, wp, wq, wo,
    perm, sent1, recv1, sent2, emb_in, up, res, nlow, resT, qkv, qkvT, pT, plT, attT, att,
    upT, gaT, gqkvT, gnT, merged, gpatch, gout, uu, aa, gt, r1, s1, r2, x3, r3, r4,
    local_sem, ex_send, ex_recv, pair_send, pair_recv, p1_send, p1_recv, p2_send, p2_recv,
    p3_send, p3_recv, p4_send, p4_recv,
):
    llm = lax.axis_index("llm")
    enc = lax.axis_index("enc")
    y, x = llm // 4, llm % 4
    z, core = enc // 2, enc % 2
    device = llm * N_ENC + enc
    start = start_ref[0, 0]
    arrivals, sends = {}, []

    def local(source, target, slot):
        return pltpu.make_async_copy(source, target, local_sem.at[slot])

    def remote(source, target, send, recv, to_llm, to_enc):
        return pltpu.make_async_remote_copy(
            src_ref=source, dst_ref=target, send_sem=send, recv_sem=recv,
            device_id=(to_llm, to_enc), device_id_type=MESH,
        )

    load_mgrad = local(mgrad_hbm, mgrad, 0)
    load_pat = local(patches_hbm, pat, 1)
    load_seg = local(seg_hbm.at[device], seg, 2)
    load_wp = local(wp_hbm, wp, 3)
    load_wq = [
        local(wq_hbm.at[:, pl.ds(D * i, D)], wq.at[:, pl.ds(D * i, D)], 4 + i) for i in range(3)
    ]
    load_wo = local(wo_hbm, wo, 7)
    load_text = local(text_hbm, text, 8)
    for load in (load_mgrad, load_pat, load_seg, load_wp, *load_wq, load_wo, load_text):
        load.start()

    barrier = pltpu.get_barrier_semaphore()

    def greet_llm(k):
        pl.semaphore_signal(
            barrier, inc=1, device_id=((llm + k) % N_LLM, enc), device_id_type=MESH
        )

    def greet_enc(k):
        pl.semaphore_signal(
            barrier, inc=1, device_id=(llm, (enc + k) % N_ENC), device_id_type=MESH
        )

    each(1, N_LLM, greet_llm)
    each(1, N_ENC, greet_enc)

    def greet_crossed(e):
        for to_llm, to_enc in ((y * 4 + z, e), (y * 4 + e // 2, x * 2 + e % 2)):
            @pl.when(jnp.logical_or(to_llm != llm, to_enc != enc))
            def _(to_llm=to_llm, to_enc=to_enc):
                pl.semaphore_signal(
                    barrier, inc=1, device_id=(to_llm, to_enc), device_id_type=MESH
                )

    each(0, N_ENC, greet_crossed)

    lane = iota((16, 256), 1)
    row = iota((16, 256), 0)

    def owner_rows(s):
        rank = owner_ref[0, s * N_ENC + enc]
        hit = (lane == rank * 16 + row).astype(F32)
        perm[pl.ds(aligned(s * 16, 16), 16), :] = hit.astype(BF)

    each(0, N_LLM, owner_rows)

    load_mgrad.wait()
    take = (iota((ROWS, SEQ), 1) == iota((ROWS, SEQ), 0) + start).astype(F32).astype(BF)
    sent1[0, :, :] = mm(take, mgrad[...]).astype(BF)

    pl.semaphore_wait(barrier, N_LLM - 1 + 3 * N_ENC - 1 - 2 * (x == z).astype(jnp.int32))

    def piece(ref, j):
        return ref.at[pl.ds(aligned(j // 2 * 16, 16), 16), pl.ds(aligned(j % 2 * HALF, 128), HALF)]

    def scatter(way, k):
        to = (llm + k) % N_LLM
        return remote(
            piece(sent1.at[way], to), recv1.at[way, pl.ds(aligned(llm * 16, 16), 16)],
            ex_send.at[way, 0, k], ex_recv.at[way, 0, k], to, enc,
        )

    def scatter_arrival(way, k):
        source = (llm + N_LLM - k) % N_LLM
        return remote(
            piece(sent1.at[way], llm), recv1.at[way, pl.ds(aligned(source * 16, 16), 16)],
            ex_send.at[way, 0, k], ex_recv.at[way, 0, k], (llm + k) % N_LLM, enc,
        )

    def deliver(way, target, k):
        to = (llm + k) % N_LLM
        return remote(
            sent2.at[way, pl.ds(aligned(to * 16, 16), 16)], piece(target, llm),
            ex_send.at[way, 1, k], ex_recv.at[way, 1, k], to, enc,
        )

    def deliver_arrival(way, target, k):
        source = (llm + N_LLM - k) % N_LLM
        return remote(
            sent2.at[way, pl.ds(aligned(llm * 16, 16), 16)], piece(target, source),
            ex_send.at[way, 1, k], ex_recv.at[way, 1, k], (llm + k) % N_LLM, enc,
        )

    def own_piece(ref):
        return ref[pl.ds(aligned(llm // 2 * 16, 16), 16), pl.ds(aligned(llm % 2 * HALF, 128), HALF)]

    def exchange_first(way):
        each(1, N_LLM, lambda k: scatter(way, k).start())
        arrivals["scatter", way] = lambda: each(
            1, N_LLM, lambda k: scatter_arrival(way, k).wait_recv()
        )
        sends.append(lambda: each(1, N_LLM, lambda k: scatter(way, k).wait_send()))
        recv1[way, pl.ds(aligned(llm * 16, 16), 16), :] = own_piece(sent1.at[way])

    def exchange_second(way, target, dims):
        arrivals.pop(("scatter", way))()
        sent2[way, :, :] = mm(perm[...], recv1[way], dims).astype(BF)
        each(1, N_LLM, lambda k: deliver(way, target, k).start())
        arrivals["deliver", way] = lambda: each(
            1, N_LLM, lambda k: deliver_arrival(way, target, k).wait_recv()
        )
        sends.append(lambda: each(1, N_LLM, lambda k: deliver(way, target, k).wait_send()))
        target[pl.ds(aligned(llm // 2 * 16, 16), 16), pl.ds(aligned(llm % 2 * HALF, 128), HALF)] = (
            sent2[way, pl.ds(aligned(llm * 16, 16), 16), :]
        )

    exchange_first(0)

    other = enc + 1 - 2 * core

    def to_pair(slot, source, target):
        copy = remote(source, target, pair_send.at[slot], pair_recv.at[slot], llm, other)
        copy.start()
        arrivals["pair", slot] = copy.wait_recv
        sends.append(copy.wait_send)

    load_pat.wait()
    to_pair(
        0, pat.at[:, pl.ds(aligned((1 - core) * 512, 128), HALF)], aa.at[1, pl.ds(ROWS, ROWS)]
    )
    aa[1, pl.ds(0, ROWS), :] = pat[:, pl.ds(aligned(core * 512, 128), HALF)]

    load_wp.wait()

    def project(i):
        columns = pl.ds(aligned(i * 256, 256), 256)
        res[:, columns] = mm(pat[...], wp[:, columns])

    each(0, 5, project)
    for i in range(4):
        rows = pl.ds(32 * i, 32)
        values = res[rows, :]
        centred = values - jnp.mean(values, axis=1, keepdims=True)
        inverse = lax.rsqrt(jnp.mean(centred * centred, axis=1, keepdims=True) + 1e-6)
        nlow[rows, :] = (centred * inverse).astype(BF)

    exchange_second(0, up, NN)

    def project_qkv(i):
        columns = pl.ds(aligned(i * 256, 256), 256)
        tile = mm(nlow[...], wq[:, columns]).astype(BF)
        qkv[:, columns] = tile
        qkvT[columns, :] = tile.T

    for i in range(3):
        load_wq[i].wait()
        each(5 * i, 5 * i + 5, project_qkv)

    load_seg.wait()
    one_hot = (iota((8, ROWS), 0) == seg[...]).astype(F32).astype(BF)
    same_image = mm(one_hot, one_hot, TN) > 0.5

    def forward_heads(g):
        base = g * HALF
        for j in range(8):
            first, width, offset = head_window(j)
            head = pl.ds(aligned(base + 80 * j, 16), 80)
            block = pl.ds(aligned((g * 8 + j) * ROWS, ROWS), ROWS)
            keys = qkv[:, pl.ds(aligned(D + base + first, 128), width)]
            scores = mm(keys, padded(qkvT[head, :], offset, width)) * SCALE
            scores = jnp.where(same_image, scores, -1e30)
            weights = jnp.exp(scores - jnp.max(scores, axis=0, keepdims=True))
            probability = weights / jnp.sum(weights, axis=0, keepdims=True)
            low = probability.astype(BF)
            pT[block, :] = probability
            plT[block, :] = low
            values = qkvT[pl.ds(aligned(2 * D + base + 80 * j, 16), 80), :]
            attT[head, :] = mm(values, low).astype(BF)

    each(0, 2, forward_heads)

    def turn_attended(i):
        block = pl.ds(aligned(i * 128, 128), 128)
        att[:, block] = attT[block, :].T

    each(0, 10, turn_attended)
    to_pair(
        1, att.at[:, pl.ds(aligned((1 - core) * HALF, 128), HALF)], aa.at[0, pl.ds(ROWS, ROWS)]
    )
    aa[0, pl.ds(0, ROWS), :] = att[:, pl.ds(aligned(core * HALF, 128), HALF)]

    arrivals.pop(("deliver", 0))()

    def turn_upstream(i):
        block = pl.ds(aligned(i * 128, 128), 128)
        upT[block, :] = up[:, block].T

    each(0, 10, turn_upstream)
    to_pair(2, upT, uu.at[0, :, pl.ds(ROWS, ROWS)])
    uu[0, :, pl.ds(0, ROWS)] = upT[...]

    load_wo.wait()

    def project_out(i):
        columns = pl.ds(aligned(i * 256, 256), 256)
        sent1[1, :, columns] = (res[:, columns] + mm(att[...], wo[:, columns])).astype(BF)

    each(0, 5, project_out)
    exchange_first(1)

    def project_back(i):
        rows = pl.ds(aligned(i * 256, 256), 256)
        gaT[rows, :] = mm(wo[rows, :], upT[...]).astype(BF)

    each(0, 5, project_back)

    def gradient(grad, part):
        columns, _ = part

        def block(b):
            rows = pl.ds(aligned(b * 320, 16), 320)
            total = mm(uu[grad, rows, :], aa[grad, :, columns])
            gt[grad, b, :, :, columns] = total.astype(BF).reshape(4, 80, columns.size)

        each(0, 4, block)

    def first_copy(grad, part, k):
        columns, kind = part
        if kind == 0:
            to = (y + k) % 4
            source, to_llm, to_enc = gt.at[grad, to, :, :, columns], to * 4 + x, enc
        elif kind == 1:
            to = (x + k) % 4
            source, to_llm, to_enc = gt.at[grad, :, to, :, columns], y * 4 + to, enc
        else:
            to = (z + k) % 4
            source, to_llm, to_enc = gt.at[grad, :, to, :, columns], llm, to * 2 + core
        return remote(
            source, r1.at[grad, k - 1, :, :, columns],
            p1_send.at[grad, kind, k - 1], p1_recv.at[grad, kind, k - 1], to_llm, to_enc,
        )

    def second_copy(grad, part, k):
        columns, kind = part
        if kind == 0:
            to = (x + k) % 4
            to_llm = y * 4 + to
        else:
            to = (y + k) % 4
            to_llm = to * 4 + x
        return remote(
            s1.at[grad, to, :, columns], r2.at[grad, k - 1, :, columns],
            p2_send.at[grad, kind, k - 1], p2_recv.at[grad, kind, k - 1], to_llm, enc,
        )

    def third_copy(grad, columns, k):
        to = (enc + k) % N_ENC
        return remote(
            x3.at[grad, pl.ds(aligned(to * 16, 16), 16), columns], r3.at[grad, k - 1, :, columns],
            p3_send.at[grad, k - 1], p3_recv.at[grad, k - 1], llm, to,
        )

    def cross_copy(grad, columns, e):
        slot = x * 2 + core
        return remote(
            x3.at[grad, pl.ds(aligned(e * 16, 16), 16), columns], r4.at[grad, slot, :, columns],
            p4_send.at[grad, e], p4_recv.at[grad, slot], y * 4 + z, e,
        )

    def cross_arrival(grad, columns, slot):
        return remote(
            x3.at[grad, pl.ds(0, 16), columns], r4.at[grad, slot, :, columns],
            p4_send.at[grad, 0], p4_recv.at[grad, slot], y * 4 + z, enc,
        )

    def first_phase(grad, part):
        _, kind = part
        for k in range(1, 4):
            first_copy(grad, part, k).start()
        arrivals["first", grad, kind] = lambda: [
            first_copy(grad, part, k).wait_recv() for k in range(1, 4)
        ]
        sends.append(lambda: [first_copy(grad, part, k).wait_send() for k in range(1, 4)])

    def second_phase(grad, part):
        columns, kind = part
        arrivals.pop(("first", grad, kind))()

        def add(i):
            if kind == 0:
                own = gt[grad, y, i, :, columns]
            else:
                own = gt[grad, i, x if kind == 1 else z, :, columns]
            total = own.astype(F32)
            for k in range(3):
                total = total + r1[grad, k, i, :, columns].astype(F32)
            s1[grad, i, :, columns] = total.astype(BF)

        each(0, 4, add)
        for k in range(1, 4):
            second_copy(grad, part, k).start()
        arrivals["second", grad, kind] = lambda: [
            second_copy(grad, part, k).wait_recv() for k in range(1, 4)
        ]
        sends.append(lambda: [second_copy(grad, part, k).wait_send() for k in range(1, 4)])

    spread_row = iota((ROWS, 80), 0)
    spread = jnp.logical_and(
        iota((ROWS, 80), 1) == spread_row // 16 * 10 + spread_row % 16, spread_row % 16 < 10
    )
    spread = spread.astype(F32).astype(BF)

    def third_sum(grad, part):
        columns, kind = part
        arrivals.pop(("second", grad, kind))()
        total = s1[grad, x if kind == 0 else y, :, columns].astype(F32)
        for k in range(3):
            total = total + r2[grad, k, :, columns].astype(F32)
        x3[grad, :, columns] = mm(spread, total.astype(BF)).astype(BF)

    def third_phase(grad, straight, crossed):
        each(1, N_ENC, lambda k: third_copy(grad, straight, k).start())

        def send(e):
            @pl.when(jnp.logical_or(x != z, e != enc))
            def _():
                cross_copy(grad, crossed, e).start()

        each(0, N_ENC, send)

        @pl.when(x == z)
        def _():
            r4[grad, pl.ds(x * 2 + core, 1), :, crossed] = x3[
                grad, pl.ds(aligned(enc * 16, 16), 16), crossed
            ].reshape(1, 16, crossed.size)

        def wait(slot):
            @pl.when(jnp.logical_or(x != z, slot != x * 2 + core))
            def _():
                cross_arrival(grad, crossed, slot).wait_recv()

        def left(e):
            @pl.when(jnp.logical_or(x != z, e != enc))
            def _():
                cross_copy(grad, crossed, e).wait_send()

        def arrived():
            each(1, N_ENC, lambda k: third_copy(grad, straight, k).wait_recv())
            each(0, N_ENC, wait)

        def sent():
            each(1, N_ENC, lambda k: third_copy(grad, straight, k).wait_send())
            each(0, N_ENC, left)

        arrivals["third", grad] = arrived
        sends.append(sent)

    def last_phase(grad, total, shift, straight, crossed):
        arrivals.pop(("third", grad))()
        mine = x3[grad, pl.ds(aligned(enc * 16, 16), 16), straight].astype(F32)
        for k in (2, 4, 6):
            mine = mine + r3[grad, k - 1, :, straight].astype(F32)
        theirs = r3[grad, 0, :, straight].astype(F32)
        for k in (3, 5, 7):
            theirs = theirs + r3[grad, k - 1, :, straight].astype(F32)
        for half, value in ((core, mine), (1 - core, theirs)):
            lanes = pl.ds(aligned(half * shift + straight.start, 128), straight.size)
            total[:, lanes] = value[:10, :]
        for half in range(2):
            value = r4[grad, half, :, crossed].astype(F32)
            for other_x in range(1, 4):
                value = value + r4[grad, other_x * 2 + half, :, crossed].astype(F32)
            total[:, pl.ds(half * shift + crossed.start, crossed.size)] = value[:10, :]

    arrivals.pop(("pair", 1))()
    arrivals.pop(("pair", 2))()
    for part in OUT_PARTS:
        gradient(0, part)
        first_phase(0, part)

    def backward_heads(g):
        base = g * HALF
        for j in range(8):
            first, width, offset = head_window(j)
            head = pl.ds(aligned(base + 80 * j, 16), 80)
            head_k = pl.ds(aligned(D + base + 80 * j, 16), 80)
            head_v = pl.ds(aligned(2 * D + base + 80 * j, 16), 80)
            block = pl.ds(aligned((g * 8 + j) * ROWS, ROWS), ROWS)
            values = qkv[:, pl.ds(aligned(2 * D + base + first, 128), width)]
            rows = gaT[head, :]
            grad_prob = mm(values, padded(rows, offset, width))
            probability = pT[block, :]
            weighted = jnp.sum(grad_prob * probability, axis=0, keepdims=True)
            low = (probability * (grad_prob - weighted) * SCALE).astype(BF)
            gqkvT[head, :] = mm(qkvT[head_k, :], low).astype(BF)
            gqkvT[head_k, :] = mm(qkvT[head, :], low, NT).astype(BF)
            gqkvT[head_v, :] = mm(rows, plT[block, :], NT).astype(BF)

    each(0, 2, backward_heads)

    exchange_second(1, emb_in, TN)

    def turn_residual(i):
        block = pl.ds(aligned(i * 128, 128), 128)
        resT[block, :] = res[:, block].T

    each(0, 10, turn_residual)
    mean = jnp.sum(resT[...], axis=0, keepdims=True) * (1.0 / D)
    centred = resT[...] - mean
    inverse = lax.rsqrt(jnp.sum(centred * centred, axis=0, keepdims=True) * (1.0 / D) + 1e-6)

    def back_qkv(i, carry):
        rows = pl.ds(aligned(i * 256, 256), 256)
        tile = mm(wq[rows, :], gqkvT[...])
        gnT[rows, :] = tile
        normed = (resT[rows, :] - mean) * inverse
        return (
            carry[0] + jnp.sum(tile, axis=0, keepdims=True),
            carry[1] + jnp.sum(tile * normed, axis=0, keepdims=True),
        )

    zero = jnp.zeros((1, ROWS), F32)
    mean_grad, mean_cross = lax.fori_loop(0, 5, back_qkv, (zero, zero))
    mean_grad = mean_grad * (1.0 / D)
    mean_cross = mean_cross * (1.0 / D)

    for part in OUT_PARTS[1:] + OUT_PARTS[:1]:
        second_phase(0, part)

    def residual_grad(i):
        rows = pl.ds(aligned(i * 256, 256), 256)
        normed = (resT[rows, :] - mean) * inverse
        total = upT[rows, :].astype(F32) + inverse * (
            gnT[rows, :] - mean_grad - normed * mean_cross
        )
        uu[1, rows, pl.ds(0, ROWS)] = total.astype(BF)

    each(0, 5, residual_grad)
    to_pair(3, uu.at[1, :, pl.ds(0, ROWS)], uu.at[1, :, pl.ds(ROWS, ROWS)])
    for part in OUT_PARTS:
        third_sum(0, part)
    third_phase(0, OUT_STRAIGHT, OUT_CROSSED)
    arrivals.pop(("pair", 0))()
    arrivals.pop(("pair", 3))()
    for part in PATCH_PARTS:
        gradient(1, part)
        first_phase(1, part)

    arrivals.pop(("deliver", 1))()
    load_text.wait()
    position = iota((SEQ, ROWS), 0)
    put = (position == iota((SEQ, ROWS), 1) + start).astype(F32).astype(BF)

    def merge(i):
        columns = pl.ds(aligned(i * 256, 256), 256)
        placed = mm(put, emb_in[:, columns])
        place = iota((SEQ, 256), 0)
        inside = jnp.logical_and(place >= start, place < start + ROWS)
        merged[:, columns] = jnp.where(inside, placed, text[:, columns].astype(F32)).astype(BF)

    each(0, 5, merge)
    store_merged = local(merged, merged_hbm, 9)
    store_merged.start()
    last_phase(0, gout, HALF, OUT_STRAIGHT, OUT_CROSSED)
    store_gout = local(gout, gout_hbm, 10)
    store_gout.start()

    for part in PATCH_PARTS:
        second_phase(1, part)
    for part in PATCH_PARTS:
        third_sum(1, part)
    third_phase(1, PATCH_STRAIGHT, PATCH_CROSSED)
    last_phase(1, gpatch, 512, PATCH_STRAIGHT, PATCH_CROSSED)
    store_gpatch = local(gpatch, gpatch_hbm, 11)
    store_gpatch.start()

    for sent in sends:
        sent()
    store_merged.wait()
    store_gout.wait()
    store_gpatch.wait()


def finish_kernel(a, b, c, a_out, b_out, c_out, sem):
    copies = [
        pltpu.make_async_copy(source, target, sem.at[i])
        for i, (source, target) in enumerate(((a, a_out), (b, b_out), (c, c_out)))
    ]
    for copy in copies:
        copy.start()
    for copy in copies:
        copy.wait()


def shards(
    patches, image_seg, owner_slot, place_start, text_embeds, merged_grad, w_patch, w_qkv, w_out
):
    smem = pl.BlockSpec(memory_space=pltpu.SMEM)
    anywhere = pl.BlockSpec(memory_space=pl.ANY)
    dma = pltpu.SemaphoreType.DMA
    merged, grad_patch, grad_out = pl.pallas_call(
        kernel,
        out_shape=(
            jax.ShapeDtypeStruct((SEQ, D), BF),
            jax.ShapeDtypeStruct((10, PIN), F32),
            jax.ShapeDtypeStruct((10, D), F32),
        ),
        in_specs=[smem, smem] + [anywhere] * 7,
        out_specs=(anywhere, anywhere, anywhere),
        scratch_shapes=[
            pltpu.VMEM((1, ROWS), jnp.int32),
            pltpu.VMEM((ROWS, PIN), BF),
            pltpu.VMEM((SEQ, D), BF),
            pltpu.VMEM((SEQ, D), BF),
            pltpu.VMEM((PIN, D), BF),
            pltpu.VMEM((D, 3 * D), BF),
            pltpu.VMEM((D, D), BF),
            pltpu.VMEM((256, 256), BF),
            pltpu.VMEM((2, ROWS, D), BF),
            pltpu.VMEM((2, 256, HALF), BF),
            pltpu.VMEM((2, 256, HALF), BF),
            pltpu.VMEM((ROWS, D), BF),
            pltpu.VMEM((ROWS, D), BF),
            pltpu.VMEM((ROWS, D), F32),
            pltpu.VMEM((ROWS, D), BF),
            pltpu.VMEM((D, ROWS), F32),
            pltpu.VMEM((ROWS, 3 * D), BF),
            pltpu.VMEM((3 * D, ROWS), BF),
            pltpu.VMEM((HEADS * ROWS, ROWS), F32),
            pltpu.VMEM((HEADS * ROWS, ROWS), BF),
            pltpu.VMEM((D, ROWS), BF),
            pltpu.VMEM((ROWS, D), BF),
            pltpu.VMEM((D, ROWS), BF),
            pltpu.VMEM((D, ROWS), BF),
            pltpu.VMEM((3 * D, ROWS), BF),
            pltpu.VMEM((D, ROWS), F32),
            pltpu.VMEM((SEQ, D), BF),
            pltpu.VMEM((10, PIN), F32),
            pltpu.VMEM((10, D), F32),
            pltpu.VMEM((2, D, 2 * ROWS), BF),
            pltpu.VMEM((2, 2 * ROWS, HALF), BF),
            pltpu.VMEM((2, 4, 4, 80, HALF), BF),
            pltpu.VMEM((2, 3, 4, 80, HALF), BF),
            pltpu.VMEM((2, 4, 80, HALF), BF),
            pltpu.VMEM((2, 3, 80, HALF), BF),
            pltpu.VMEM((2, ROWS, HALF), BF),
            pltpu.VMEM((2, 7, 16, HALF), BF),
            pltpu.VMEM((2, 8, 16, HALF), BF),
            dma((12,)),
            dma((2, 2, N_LLM)),
            dma((2, 2, N_LLM)),
            dma((4,)),
            dma((4,)),
            dma((2, 3, 3)),
            dma((2, 3, 3)),
            dma((2, 3, 3)),
            dma((2, 3, 3)),
            dma((2, 7)),
            dma((2, 7)),
            dma((2, 8)),
            dma((2, 8)),
        ],
        compiler_params=pltpu.CompilerParams(
            collective_id=0, has_side_effects=True, vmem_limit_bytes=56 * 1024 * 1024
        ),
    )(
        owner_slot.reshape(1, 128), place_start, image_seg, patches, text_embeds, merged_grad,
        w_patch, w_qkv, w_out,
    )
    merged, grad_patch, grad_out = pl.pallas_call(
        finish_kernel,
        out_shape=(
            jax.ShapeDtypeStruct((SEQ, D), BF),
            jax.ShapeDtypeStruct((10, PIN), F32),
            jax.ShapeDtypeStruct((10, D), F32),
        ),
        in_specs=[anywhere] * 3,
        out_specs=(anywhere, anywhere, anywhere),
        scratch_shapes=[dma((3,))],
    )(merged, grad_patch, grad_out)
    return (merged, grad_patch.T, grad_out.T)


def solution(mesh):
    rows = P(("llm", "enc"), None)
    columns = P(None, ("llm", "enc"))
    return jax.shard_map(
        shards,
        mesh=mesh,
        in_specs=(rows, P(), P(), rows, rows, rows, P(), P(), P()),
        out_specs=(rows, columns, columns),
        check_vma=False,
    )
```

```python
import jax
import jax.numpy as jnp
from jax import lax
from jax.experimental import pallas as pl
from jax.experimental.pallas import tpu as pltpu
from jax.sharding import PartitionSpec as P

D = 1280
HEADS = 16
HEAD_DIM = 80
PIN = 1152
ROWS = 128
SEQ = 160
N_LLM = 16
N_ENC = 8
HALF = 640
SCALE = HEAD_DIM ** (-0.5)

OUT_PARTS = ((pl.ds(256, 384), 2), (pl.ds(0, 128), 0), (pl.ds(128, 128), 1))
PATCH_PARTS = ((pl.ds(0, 256), 0), (pl.ds(256, 256), 1), (pl.ds(512, 128), 2))

BF = jnp.bfloat16
F32 = jnp.float32
MESH = pl.DeviceIdType.MESH
NN = (((1,), (0,)), ((), ()))
NT = (((1,), (1,)), ((), ()))
TN = (((0,), (0,)), ((), ()))


def mm(a, b, dims=NN):
    return lax.dot_general(a, b, dims, preferred_element_type=F32)


def iota(shape, axis):
    return lax.broadcasted_iota(jnp.int32, shape, axis)


def aligned(value, unit):
    return pl.multiple_of(value, unit)


def each(low, high, body):
    def step(i, carry):
        body(i)
        return carry

    lax.fori_loop(low, high, step, 0)


def head_window(j):
    first = 80 * j // 128 * 128
    last = -(-(80 * j + 80) // 128) * 128
    return first, last - first, 80 * j - first


def padded(rows, offset, width):
    pieces = []
    if offset:
        pieces.append(jnp.zeros((offset, ROWS), BF))
    pieces.append(rows)
    if width - offset - 80:
        pieces.append(jnp.zeros((width - offset - 80, ROWS), BF))
    return jnp.concatenate(pieces, axis=0)


def kernel(
    owner_ref, start_ref, seg_hbm, patches_hbm, text_hbm, mgrad_hbm, wp_hbm, wq_hbm, wo_hbm,
    merged_hbm, gpatch_hbm, gout_hbm,
    seg, pat, text, mgrad, wp, wq, wo,
    perm, sent1, recv1, sent2, emb_in, up, res, nlow, resT, qkv, qkvT, pT, plT, attT, att,
    upT, gaT, gqkvT, gnT, merged, gpatch, gout, uu, aa, gt, r1, s1, r2, crossing, s2, x3, r3,
    local_sem, ex_send, ex_recv, pair_send, pair_recv, p1_send, p1_recv, p2_send, p2_recv,
    p3_send, p3_recv, p4_send, p4_recv,
):
    llm = lax.axis_index("llm")
    enc = lax.axis_index("enc")
    y, x = llm // 4, llm % 4
    z, core = enc // 2, enc % 2
    device = llm * N_ENC + enc
    start = start_ref[0, 0]
    arrivals, sends = {}, []

    def local(source, target, slot):
        return pltpu.make_async_copy(source, target, local_sem.at[slot])

    def remote(source, target, send, recv, to_llm, to_enc):
        return pltpu.make_async_remote_copy(
            src_ref=source, dst_ref=target, send_sem=send, recv_sem=recv,
            device_id=(to_llm, to_enc), device_id_type=MESH,
        )

    load_mgrad = local(mgrad_hbm, mgrad, 0)
    load_pat = local(patches_hbm, pat, 1)
    load_seg = local(seg_hbm.at[device], seg, 2)
    load_wp = local(wp_hbm, wp, 3)
    load_wq = [
        local(wq_hbm.at[:, pl.ds(D * i, D)], wq.at[:, pl.ds(D * i, D)], 4 + i) for i in range(3)
    ]
    load_wo = local(wo_hbm, wo, 7)
    load_text = local(text_hbm, text, 8)
    for load in (load_mgrad, load_pat, load_seg, load_wp, *load_wq, load_wo, load_text):
        load.start()

    barrier = pltpu.get_barrier_semaphore()

    def greet_llm(k):
        pl.semaphore_signal(
            barrier, inc=1, device_id=((llm + k) % N_LLM, enc), device_id_type=MESH
        )

    def greet_enc(k):
        pl.semaphore_signal(
            barrier, inc=1, device_id=(llm, (enc + k) % N_ENC), device_id_type=MESH
        )

    each(1, N_LLM, greet_llm)
    each(1, N_ENC, greet_enc)

    @pl.when(x != z)
    def _():
        pl.semaphore_signal(
            barrier, inc=1, device_id=(y * 4 + z, x * 2 + core), device_id_type=MESH
        )

    lane = iota((16, 256), 1)
    row = iota((16, 256), 0)

    def owner_rows(s):
        rank = owner_ref[0, s * N_ENC + enc]
        hit = (lane == rank * 16 + row).astype(F32)
        perm[pl.ds(aligned(s * 16, 16), 16), :] = hit.astype(BF)

    each(0, N_LLM, owner_rows)

    load_mgrad.wait()
    take = (iota((ROWS, SEQ), 1) == iota((ROWS, SEQ), 0) + start).astype(F32).astype(BF)
    sent1[0, :, :] = mm(take, mgrad[...]).astype(BF)

    pl.semaphore_wait(barrier, N_LLM - 1 + N_ENC - 1 + (x != z).astype(jnp.int32))

    def piece(ref, j):
        return ref.at[pl.ds(aligned(j // 2 * 16, 16), 16), pl.ds(aligned(j % 2 * HALF, 128), HALF)]

    def scatter(way, k):
        to = (llm + k) % N_LLM
        return remote(
            piece(sent1.at[way], to), recv1.at[way, pl.ds(aligned(llm * 16, 16), 16)],
            ex_send.at[way, 0, k], ex_recv.at[way, 0, k], to, enc,
        )

    def scatter_arrival(way, k):
        source = (llm + N_LLM - k) % N_LLM
        return remote(
            piece(sent1.at[way], llm), recv1.at[way, pl.ds(aligned(source * 16, 16), 16)],
            ex_send.at[way, 0, k], ex_recv.at[way, 0, k], (llm + k) % N_LLM, enc,
        )

    def deliver(way, target, k):
        to = (llm + k) % N_LLM
        return remote(
            sent2.at[way, pl.ds(aligned(to * 16, 16), 16)], piece(target, llm),
            ex_send.at[way, 1, k], ex_recv.at[way, 1, k], to, enc,
        )

    def deliver_arrival(way, target, k):
        source = (llm + N_LLM - k) % N_LLM
        return remote(
            sent2.at[way, pl.ds(aligned(llm * 16, 16), 16)], piece(target, source),
            ex_send.at[way, 1, k], ex_recv.at[way, 1, k], (llm + k) % N_LLM, enc,
        )

    def own_piece(ref):
        return ref[pl.ds(aligned(llm // 2 * 16, 16), 16), pl.ds(aligned(llm % 2 * HALF, 128), HALF)]

    def exchange_first(way):
        each(1, N_LLM, lambda k: scatter(way, k).start())
        arrivals["scatter", way] = lambda: each(
            1, N_LLM, lambda k: scatter_arrival(way, k).wait_recv()
        )
        sends.append(lambda: each(1, N_LLM, lambda k: scatter(way, k).wait_send()))
        recv1[way, pl.ds(aligned(llm * 16, 16), 16), :] = own_piece(sent1.at[way])

    def exchange_second(way, target, dims):
        arrivals.pop(("scatter", way))()
        sent2[way, :, :] = mm(perm[...], recv1[way], dims).astype(BF)
        each(1, N_LLM, lambda k: deliver(way, target, k).start())
        arrivals["deliver", way] = lambda: each(
            1, N_LLM, lambda k: deliver_arrival(way, target, k).wait_recv()
        )
        sends.append(lambda: each(1, N_LLM, lambda k: deliver(way, target, k).wait_send()))
        target[pl.ds(aligned(llm // 2 * 16, 16), 16), pl.ds(aligned(llm % 2 * HALF, 128), HALF)] = (
            sent2[way, pl.ds(aligned(llm * 16, 16), 16), :]
        )

    exchange_first(0)

    other = enc + 1 - 2 * core

    def to_pair(slot, source, target):
        copy = remote(source, target, pair_send.at[slot], pair_recv.at[slot], llm, other)
        copy.start()
        arrivals["pair", slot] = copy.wait_recv
        sends.append(copy.wait_send)

    load_pat.wait()
    to_pair(
        0, pat.at[:, pl.ds(aligned((1 - core) * 512, 128), HALF)], aa.at[1, pl.ds(ROWS, ROWS)]
    )
    aa[1, pl.ds(0, ROWS), :] = pat[:, pl.ds(aligned(core * 512, 128), HALF)]

    load_wp.wait()

    def project(i):
        columns = pl.ds(aligned(i * 256, 256), 256)
        res[:, columns] = mm(pat[...], wp[:, columns])

    each(0, 5, project)
    for i in range(4):
        rows = pl.ds(32 * i, 32)
        values = res[rows, :]
        centred = values - jnp.mean(values, axis=1, keepdims=True)
        inverse = lax.rsqrt(jnp.mean(centred * centred, axis=1, keepdims=True) + 1e-6)
        nlow[rows, :] = (centred * inverse).astype(BF)

    def turn_residual(i):
        block = pl.ds(aligned(i * 128, 128), 128)
        resT[block, :] = res[:, block].T

    each(0, 10, turn_residual)
    mean = jnp.sum(resT[...], axis=0, keepdims=True) * (1.0 / D)
    centred = resT[...] - mean
    inverse = lax.rsqrt(jnp.sum(centred * centred, axis=0, keepdims=True) * (1.0 / D) + 1e-6)

    def project_qkv(i):
        columns = pl.ds(aligned(i * 256, 256), 256)
        tile = mm(nlow[...], wq[:, columns]).astype(BF)
        qkv[:, columns] = tile
        qkvT[columns, :] = tile.T

    for i in range(3):
        load_wq[i].wait()
        each(5 * i, 5 * i + 5, project_qkv)

    exchange_second(0, up, NN)

    load_seg.wait()
    one_hot = (iota((8, ROWS), 0) == seg[...]).astype(F32).astype(BF)
    same_image = mm(one_hot, one_hot, TN) > 0.5

    def forward_heads(g):
        base = g * HALF
        for j in range(8):
            first, width, offset = head_window(j)
            head = pl.ds(aligned(base + 80 * j, 16), 80)
            block = pl.ds(aligned((g * 8 + j) * ROWS, ROWS), ROWS)
            keys = qkv[:, pl.ds(aligned(D + base + first, 128), width)]
            scores = mm(keys, padded(qkvT[head, :], offset, width)) * SCALE
            scores = jnp.where(same_image, scores, -1e30)
            weights = jnp.exp(scores - jnp.max(scores, axis=0, keepdims=True))
            probability = weights / jnp.sum(weights, axis=0, keepdims=True)
            low = probability.astype(BF)
            pT[block, :] = probability
            plT[block, :] = low
            values = qkvT[pl.ds(aligned(2 * D + base + 80 * j, 16), 80), :]
            attT[head, :] = mm(values, low).astype(BF)

    each(0, 2, forward_heads)

    def turn_attended(i):
        block = pl.ds(aligned(i * 128, 128), 128)
        att[:, block] = attT[block, :].T

    each(0, 10, turn_attended)
    to_pair(
        1, att.at[:, pl.ds(aligned((1 - core) * HALF, 128), HALF)], aa.at[0, pl.ds(ROWS, ROWS)]
    )
    aa[0, pl.ds(0, ROWS), :] = att[:, pl.ds(aligned(core * HALF, 128), HALF)]

    arrivals.pop(("deliver", 0))()

    def turn_upstream(i):
        block = pl.ds(aligned(i * 128, 128), 128)
        upT[block, :] = up[:, block].T

    each(0, 10, turn_upstream)
    to_pair(2, upT, uu.at[0, :, pl.ds(ROWS, ROWS)])
    uu[0, :, pl.ds(0, ROWS)] = upT[...]

    load_wo.wait()

    def project_out(i):
        columns = pl.ds(aligned(i * 256, 256), 256)
        sent1[1, :, columns] = (res[:, columns] + mm(att[...], wo[:, columns])).astype(BF)

    each(0, 5, project_out)
    exchange_first(1)

    def project_back(i):
        rows = pl.ds(aligned(i * 256, 256), 256)
        gaT[rows, :] = mm(wo[rows, :], upT[...]).astype(BF)

    each(0, 5, project_back)

    def gradient(grad, part):
        columns, _ = part

        def block(b):
            rows = pl.ds(aligned(b * 320, 16), 320)
            total = mm(uu[grad, rows, :], aa[grad, :, columns])
            gt[grad, b, :, :, columns] = total.astype(BF).reshape(4, 80, columns.size)

        each(0, 4, block)

    def first_copy(grad, part, k):
        columns, kind = part
        if kind == 0:
            to = (y + k) % 4
            source, to_llm, to_enc = gt.at[grad, to, :, :, columns], to * 4 + x, enc
        elif kind == 1:
            to = (x + k) % 4
            source, to_llm, to_enc = gt.at[grad, :, to, :, columns], y * 4 + to, enc
        else:
            to = (z + k) % 4
            source, to_llm, to_enc = gt.at[grad, :, to, :, columns], llm, to * 2 + core
        return remote(
            source, r1.at[grad, k - 1, :, :, columns],
            p1_send.at[grad, kind, k - 1], p1_recv.at[grad, kind, k - 1], to_llm, to_enc,
        )

    def second_copy(grad, part, k):
        columns, kind = part
        if kind == 0:
            to = (x + k) % 4
            to_llm = y * 4 + to
        else:
            to = (y + k) % 4
            to_llm = to * 4 + x
        return remote(
            s1.at[grad, to, :, columns], r2.at[grad, k - 1, :, columns],
            p2_send.at[grad, kind, k - 1], p2_recv.at[grad, kind, k - 1], to_llm, enc,
        )

    def cross_copy(grad, part):
        columns, _ = part
        return remote(
            crossing.at[grad, :, columns], s2.at[grad, :, columns],
            p4_send.at[grad], p4_recv.at[grad], y * 4 + z, x * 2 + core,
        )

    def third_copy(grad, k):
        to = (enc + k) % N_ENC
        return remote(
            x3.at[grad, pl.ds(aligned(to * 16, 16), 16)], r3.at[grad, k - 1],
            p3_send.at[grad, k - 1], p3_recv.at[grad, k - 1], llm, to,
        )

    def first_phase(grad, part):
        _, kind = part
        for k in range(1, 4):
            first_copy(grad, part, k).start()
        arrivals["first", grad, kind] = lambda: [
            first_copy(grad, part, k).wait_recv() for k in range(1, 4)
        ]
        sends.append(lambda: [first_copy(grad, part, k).wait_send() for k in range(1, 4)])

    def second_phase(grad, part):
        columns, kind = part
        arrivals.pop(("first", grad, kind))()

        def add(i):
            if kind == 0:
                own = gt[grad, y, i, :, columns]
            else:
                own = gt[grad, i, x if kind == 1 else z, :, columns]
            total = own.astype(F32)
            for k in range(3):
                total = total + r1[grad, k, i, :, columns].astype(F32)
            s1[grad, i, :, columns] = total.astype(BF)

        each(0, 4, add)
        for k in range(1, 4):
            second_copy(grad, part, k).start()
        arrivals["second", grad, kind] = lambda: [
            second_copy(grad, part, k).wait_recv() for k in range(1, 4)
        ]
        sends.append(lambda: [second_copy(grad, part, k).wait_send() for k in range(1, 4)])

    spread_row = iota((ROWS, 80), 0)
    spread = jnp.logical_and(
        iota((ROWS, 80), 1) == spread_row // 16 * 10 + spread_row % 16, spread_row % 16 < 10
    )
    spread = spread.astype(F32).astype(BF)

    def third_sum(grad, part):
        columns, kind = part
        arrivals.pop(("second", grad, kind))()
        total = s1[grad, x if kind == 0 else y, :, columns].astype(F32)
        for k in range(3):
            total = total + r2[grad, k, :, columns].astype(F32)
        if kind < 2:
            s2[grad, :, columns] = total.astype(BF)
            return

        crossing[grad, :, columns] = total.astype(BF)

        def if_other(run):
            pl.when(x != z)(run)

        @pl.when(x == z)
        def _():
            s2[grad, :, columns] = crossing[grad, :, columns]

        if_other(lambda: cross_copy(grad, part).start())
        arrivals["cross", grad] = lambda: if_other(lambda: cross_copy(grad, part).wait_recv())
        sends.append(lambda: if_other(lambda: cross_copy(grad, part).wait_send()))

    def third_phase(grad):
        arrivals.pop(("cross", grad))()
        x3[grad, :, :] = mm(spread, s2[grad]).astype(BF)
        each(1, N_ENC, lambda k: third_copy(grad, k).start())
        arrivals["third", grad] = lambda: each(
            1, N_ENC, lambda k: third_copy(grad, k).wait_recv()
        )
        sends.append(lambda: each(1, N_ENC, lambda k: third_copy(grad, k).wait_send()))

    def last_phase(grad, total, shift):
        arrivals.pop(("third", grad))()
        mine = x3[grad, pl.ds(aligned(enc * 16, 16), 16), :].astype(F32)
        for k in (2, 4, 6):
            mine = mine + r3[grad, k - 1].astype(F32)
        theirs = r3[grad, 0].astype(F32)
        for k in (3, 5, 7):
            theirs = theirs + r3[grad, k - 1].astype(F32)
        total[:, pl.ds(aligned(core * shift, 128), HALF)] = mine[:10, :]
        total[:, pl.ds(aligned((1 - core) * shift, 128), HALF)] = theirs[:10, :]

    arrivals.pop(("pair", 1))()
    arrivals.pop(("pair", 2))()
    for part in OUT_PARTS:
        gradient(0, part)
        first_phase(0, part)

    def backward_heads(g):
        base = g * HALF
        for j in range(8):
            first, width, offset = head_window(j)
            head = pl.ds(aligned(base + 80 * j, 16), 80)
            head_k = pl.ds(aligned(D + base + 80 * j, 16), 80)
            head_v = pl.ds(aligned(2 * D + base + 80 * j, 16), 80)
            block = pl.ds(aligned((g * 8 + j) * ROWS, ROWS), ROWS)
            values = qkv[:, pl.ds(aligned(2 * D + base + first, 128), width)]
            rows = gaT[head, :]
            grad_prob = mm(values, padded(rows, offset, width))
            probability = pT[block, :]
            weighted = jnp.sum(grad_prob * probability, axis=0, keepdims=True)
            low = (probability * (grad_prob - weighted) * SCALE).astype(BF)
            gqkvT[head, :] = mm(qkvT[head_k, :], low).astype(BF)
            gqkvT[head_k, :] = mm(qkvT[head, :], low, NT).astype(BF)
            gqkvT[head_v, :] = mm(rows, plT[block, :], NT).astype(BF)

    each(0, 2, backward_heads)

    exchange_second(1, emb_in, TN)

    def back_qkv(i, carry):
        rows = pl.ds(aligned(i * 256, 256), 256)
        tile = mm(wq[rows, :], gqkvT[...])
        gnT[rows, :] = tile
        normed = (resT[rows, :] - mean) * inverse
        return (
            carry[0] + jnp.sum(tile, axis=0, keepdims=True),
            carry[1] + jnp.sum(tile * normed, axis=0, keepdims=True),
        )

    zero = jnp.zeros((1, ROWS), F32)
    mean_grad, mean_cross = lax.fori_loop(0, 5, back_qkv, (zero, zero))
    mean_grad = mean_grad * (1.0 / D)
    mean_cross = mean_cross * (1.0 / D)

    def residual_grad(i):
        rows = pl.ds(aligned(i * 256, 256), 256)
        normed = (resT[rows, :] - mean) * inverse
        total = upT[rows, :].astype(F32) + inverse * (
            gnT[rows, :] - mean_grad - normed * mean_cross
        )
        uu[1, rows, pl.ds(0, ROWS)] = total.astype(BF)

    each(0, 5, residual_grad)
    to_pair(3, uu.at[1, :, pl.ds(0, ROWS)], uu.at[1, :, pl.ds(ROWS, ROWS)])
    for part in OUT_PARTS[1:] + OUT_PARTS[:1]:
        second_phase(0, part)
    arrivals.pop(("pair", 0))()
    arrivals.pop(("pair", 3))()
    for part in PATCH_PARTS:
        gradient(1, part)
        first_phase(1, part)

    for part in OUT_PARTS:
        third_sum(0, part)

    arrivals.pop(("deliver", 1))()
    load_text.wait()
    position = iota((SEQ, ROWS), 0)
    put = (position == iota((SEQ, ROWS), 1) + start).astype(F32).astype(BF)

    def merge(i):
        columns = pl.ds(aligned(i * 256, 256), 256)
        placed = mm(put, emb_in[:, columns])
        place = iota((SEQ, 256), 0)
        inside = jnp.logical_and(place >= start, place < start + ROWS)
        merged[:, columns] = jnp.where(inside, placed, text[:, columns].astype(F32)).astype(BF)

    each(0, 5, merge)
    store_merged = local(merged, merged_hbm, 9)
    store_merged.start()
    third_phase(0)
    last_phase(0, gout, HALF)
    store_gout = local(gout, gout_hbm, 10)
    store_gout.start()

    for part in PATCH_PARTS[2:] + PATCH_PARTS[:2]:
        second_phase(1, part)
    for part in PATCH_PARTS[2:] + PATCH_PARTS[:2]:
        third_sum(1, part)
    third_phase(1)
    last_phase(1, gpatch, 512)
    store_gpatch = local(gpatch, gpatch_hbm, 11)
    store_gpatch.start()

    for sent in sends:
        sent()
    store_merged.wait()
    store_gout.wait()
    store_gpatch.wait()


def finish_kernel(a, b, c, a_out, b_out, c_out):
    a_out[...] = a[...]
    b_out[...] = b[...]
    c_out[...] = c[...]


def shards(
    patches, image_seg, owner_slot, place_start, text_embeds, merged_grad, w_patch, w_qkv, w_out
):
    smem = pl.BlockSpec(memory_space=pltpu.SMEM)
    anywhere = pl.BlockSpec(memory_space=pl.ANY)
    vmem = pl.BlockSpec(memory_space=pltpu.VMEM)
    dma = pltpu.SemaphoreType.DMA
    merged, grad_patch, grad_out = pl.pallas_call(
        kernel,
        out_shape=(
            jax.ShapeDtypeStruct((SEQ, D), BF),
            jax.ShapeDtypeStruct((10, PIN), F32),
            jax.ShapeDtypeStruct((10, D), F32),
        ),
        in_specs=[smem, smem] + [anywhere] * 7,
        out_specs=(anywhere, anywhere, anywhere),
        scratch_shapes=[
            pltpu.VMEM((1, ROWS), jnp.int32),
            pltpu.VMEM((ROWS, PIN), BF),
            pltpu.VMEM((SEQ, D), BF),
            pltpu.VMEM((SEQ, D), BF),
            pltpu.VMEM((PIN, D), BF),
            pltpu.VMEM((D, 3 * D), BF),
            pltpu.VMEM((D, D), BF),
            pltpu.VMEM((256, 256), BF),
            pltpu.VMEM((2, ROWS, D), BF),
            pltpu.VMEM((2, 256, HALF), BF),
            pltpu.VMEM((2, 256, HALF), BF),
            pltpu.VMEM((ROWS, D), BF),
            pltpu.VMEM((ROWS, D), BF),
            pltpu.VMEM((ROWS, D), F32),
            pltpu.VMEM((ROWS, D), BF),
            pltpu.VMEM((D, ROWS), F32),
            pltpu.VMEM((ROWS, 3 * D), BF),
            pltpu.VMEM((3 * D, ROWS), BF),
            pltpu.VMEM((HEADS * ROWS, ROWS), F32),
            pltpu.VMEM((HEADS * ROWS, ROWS), BF),
            pltpu.VMEM((D, ROWS), BF),
            pltpu.VMEM((ROWS, D), BF),
            pltpu.VMEM((D, ROWS), BF),
            pltpu.VMEM((D, ROWS), BF),
            pltpu.VMEM((3 * D, ROWS), BF),
            pltpu.VMEM((D, ROWS), F32),
            pltpu.VMEM((SEQ, D), BF),
            pltpu.VMEM((10, PIN), F32),
            pltpu.VMEM((10, D), F32),
            pltpu.VMEM((2, D, 2 * ROWS), BF),
            pltpu.VMEM((2, 2 * ROWS, HALF), BF),
            pltpu.VMEM((2, 4, 4, 80, HALF), BF),
            pltpu.VMEM((2, 3, 4, 80, HALF), BF),
            pltpu.VMEM((2, 4, 80, HALF), BF),
            pltpu.VMEM((2, 3, 80, HALF), BF),
            pltpu.VMEM((2, 80, HALF), BF),
            pltpu.VMEM((2, 80, HALF), BF),
            pltpu.VMEM((2, ROWS, HALF), BF),
            pltpu.VMEM((2, 7, 16, HALF), BF),
            dma((12,)),
            dma((2, 2, N_LLM)),
            dma((2, 2, N_LLM)),
            dma((4,)),
            dma((4,)),
            dma((2, 3, 3)),
            dma((2, 3, 3)),
            dma((2, 3, 3)),
            dma((2, 3, 3)),
            dma((2, 7)),
            dma((2, 7)),
            dma((2,)),
            dma((2,)),
        ],
        compiler_params=pltpu.CompilerParams(
            collective_id=0, has_side_effects=True, vmem_limit_bytes=56 * 1024 * 1024
        ),
    )(
        owner_slot.reshape(1, 128), place_start, image_seg, patches, text_embeds, merged_grad,
        w_patch, w_qkv, w_out,
    )
    merged, grad_patch, grad_out = pl.pallas_call(
        finish_kernel,
        out_shape=(
            jax.ShapeDtypeStruct((SEQ, D), BF),
            jax.ShapeDtypeStruct((10, PIN), F32),
            jax.ShapeDtypeStruct((10, D), F32),
        ),
        in_specs=[vmem] * 3,
        out_specs=(vmem, vmem, vmem),
    )(merged, grad_patch, grad_out)
    return (merged, grad_patch.T, grad_out.T)


def solution(mesh):
    rows = P(("llm", "enc"), None)
    columns = P(None, ("llm", "enc"))
    return jax.shard_map(
        shards,
        mesh=mesh,
        in_specs=(rows, P(), P(), rows, rows, rows, P(), P(), P()),
        out_specs=(rows, columns, columns),
        check_vma=False,
    )
```

```python
import jax
import jax.numpy as jnp
from jax import lax
from jax.experimental import pallas as pl
from jax.experimental.pallas import tpu as pltpu
from jax.sharding import PartitionSpec as P

D = 1280
HEADS = 16
HEAD_DIM = 80
PIN = 1152
ROWS = 128
SEQ = 160
N_LLM = 16
N_ENC = 8
HALF = 640
SCALE = HEAD_DIM ** (-0.5)

OUT_PARTS = ((pl.ds(256, 384), 2), (pl.ds(0, 128), 0), (pl.ds(128, 128), 1))
PATCH_PARTS = ((pl.ds(0, 256), 0), (pl.ds(256, 256), 1), (pl.ds(512, 128), 2))

BF = jnp.bfloat16
F32 = jnp.float32
MESH = pl.DeviceIdType.MESH
NN = (((1,), (0,)), ((), ()))
NT = (((1,), (1,)), ((), ()))
TN = (((0,), (0,)), ((), ()))


def mm(a, b, dims=NN):
    return lax.dot_general(a, b, dims, preferred_element_type=F32)


def iota(shape, axis):
    return lax.broadcasted_iota(jnp.int32, shape, axis)


def aligned(value, unit):
    return value if isinstance(value, int) else pl.multiple_of(value, unit)


def each(low, high, body):
    def step(i, carry):
        body(i)
        return carry

    lax.fori_loop(low, high, step, 0)


def head_window(j):
    first = 80 * j // 128 * 128
    last = -(-(80 * j + 80) // 128) * 128
    return first, last - first, 80 * j - first


def padded(rows, offset, width):
    pieces = []
    if offset:
        pieces.append(jnp.zeros((offset, ROWS), BF))
    pieces.append(rows)
    if width - offset - 80:
        pieces.append(jnp.zeros((width - offset - 80, ROWS), BF))
    return jnp.concatenate(pieces, axis=0)


def kernel(
    owner_ref, start_ref, seg_hbm, patches_hbm, text_hbm, mgrad_hbm, wp_hbm, wq_hbm, wo_hbm,
    merged_hbm, gpatch_hbm, gout_hbm,
    seg, pat, text, mgrad, wp, wq, wo,
    perm, sent1, recv1, sent2, emb_in, up, res, nlow, resT, qkv, qkvT, pT, plT, attT, att,
    upT, gaT, gqkvT, gnT, merged, gpatch, gout, uu, aa, gt, r1, s1, r2, crossing, s2, x3, r3,
    local_sem, ex_send, ex_recv, pair_send, pair_recv, p1_send, p1_recv, p2_send, p2_recv,
    p3_send, p3_recv, p4_send, p4_recv,
):
    llm = lax.axis_index("llm")
    enc = lax.axis_index("enc")
    y, x = llm // 4, llm % 4
    z, core = enc // 2, enc % 2
    device = llm * N_ENC + enc
    start = start_ref[0, 0]
    arrivals, sends = {}, []

    def local(source, target, slot):
        return pltpu.make_async_copy(source, target, local_sem.at[slot])

    def remote(source, target, send, recv, to_llm, to_enc):
        return pltpu.make_async_remote_copy(
            src_ref=source, dst_ref=target, send_sem=send, recv_sem=recv,
            device_id=(to_llm, to_enc), device_id_type=MESH,
        )

    load_mgrad = local(mgrad_hbm, mgrad, 0)
    load_pat = local(patches_hbm, pat, 1)
    load_seg = local(seg_hbm.at[device], seg, 2)
    load_wp = local(wp_hbm, wp, 3)
    load_wq = [
        local(wq_hbm.at[:, pl.ds(D * i, D)], wq.at[:, pl.ds(D * i, D)], 4 + i) for i in range(3)
    ]
    load_wo = local(wo_hbm, wo, 7)
    load_text = local(text_hbm, text, 8)
    for load in (load_mgrad, load_pat, load_seg, load_wp, *load_wq, load_wo, load_text):
        load.start()

    barrier = pltpu.get_barrier_semaphore()

    def greet_llm(k):
        pl.semaphore_signal(
            barrier, inc=1, device_id=((llm + k) % N_LLM, enc), device_id_type=MESH
        )

    def greet_enc(k):
        pl.semaphore_signal(
            barrier, inc=1, device_id=(llm, (enc + k) % N_ENC), device_id_type=MESH
        )

    each(1, N_LLM, greet_llm)
    each(1, N_ENC, greet_enc)

    @pl.when(x != z)
    def _():
        pl.semaphore_signal(
            barrier, inc=1, device_id=(y * 4 + z, x * 2 + core), device_id_type=MESH
        )

    lane = iota((16, 256), 1)
    row = iota((16, 256), 0)

    def owner_rows(s):
        rank = owner_ref[0, s * N_ENC + enc]
        hit = (lane == rank * 16 + row).astype(F32)
        perm[pl.ds(aligned(s * 16, 16), 16), :] = hit.astype(BF)

    each(0, N_LLM, owner_rows)

    load_mgrad.wait()
    take = (iota((ROWS, SEQ), 1) == iota((ROWS, SEQ), 0) + start).astype(F32).astype(BF)
    sent1[0, :, :] = mm(take, mgrad[...]).astype(BF)

    pl.semaphore_wait(barrier, N_LLM - 1 + N_ENC - 1 + (x != z).astype(jnp.int32))

    def piece(ref, j):
        return ref.at[pl.ds(aligned(j // 2 * 16, 16), 16), pl.ds(aligned(j % 2 * HALF, 128), HALF)]

    def scatter(way, k):
        to = (llm + k) % N_LLM
        return remote(
            piece(sent1.at[way], to), recv1.at[way, pl.ds(aligned(llm * 16, 16), 16)],
            ex_send.at[way, 0, k], ex_recv.at[way, 0, k], to, enc,
        )

    def scatter_arrival(way, k):
        source = (llm + N_LLM - k) % N_LLM
        return remote(
            piece(sent1.at[way], llm), recv1.at[way, pl.ds(aligned(source * 16, 16), 16)],
            ex_send.at[way, 0, k], ex_recv.at[way, 0, k], (llm + k) % N_LLM, enc,
        )

    def deliver(way, target, k):
        to = (llm + k) % N_LLM
        return remote(
            sent2.at[way, pl.ds(aligned(to * 16, 16), 16)], piece(target, llm),
            ex_send.at[way, 1, k], ex_recv.at[way, 1, k], to, enc,
        )

    def deliver_arrival(way, target, k):
        source = (llm + N_LLM - k) % N_LLM
        return remote(
            sent2.at[way, pl.ds(aligned(llm * 16, 16), 16)], piece(target, source),
            ex_send.at[way, 1, k], ex_recv.at[way, 1, k], (llm + k) % N_LLM, enc,
        )

    def own_piece(ref):
        return ref[pl.ds(aligned(llm // 2 * 16, 16), 16), pl.ds(aligned(llm % 2 * HALF, 128), HALF)]

    def exchange_first(way):
        each(1, N_LLM, lambda k: scatter(way, k).start())
        arrivals["scatter", way] = lambda: each(
            1, N_LLM, lambda k: scatter_arrival(way, k).wait_recv()
        )
        sends.append(lambda: each(1, N_LLM, lambda k: scatter(way, k).wait_send()))
        recv1[way, pl.ds(aligned(llm * 16, 16), 16), :] = own_piece(sent1.at[way])

    def exchange_second(way, target, dims):
        arrivals.pop(("scatter", way))()
        sent2[way, :, :] = mm(perm[...], recv1[way], dims).astype(BF)
        each(1, N_LLM, lambda k: deliver(way, target, k).start())
        arrivals["deliver", way] = lambda: each(
            1, N_LLM, lambda k: deliver_arrival(way, target, k).wait_recv()
        )
        sends.append(lambda: each(1, N_LLM, lambda k: deliver(way, target, k).wait_send()))
        target[pl.ds(aligned(llm // 2 * 16, 16), 16), pl.ds(aligned(llm % 2 * HALF, 128), HALF)] = (
            sent2[way, pl.ds(aligned(llm * 16, 16), 16), :]
        )

    exchange_first(0)

    other = enc + 1 - 2 * core

    def to_pair(slot, source, target):
        copy = remote(source, target, pair_send.at[slot], pair_recv.at[slot], llm, other)
        copy.start()
        arrivals["pair", slot] = copy.wait_recv
        sends.append(copy.wait_send)

    load_pat.wait()
    to_pair(
        0, pat.at[:, pl.ds(aligned((1 - core) * 512, 128), HALF)], aa.at[1, pl.ds(ROWS, ROWS)]
    )
    aa[1, pl.ds(0, ROWS), :] = pat[:, pl.ds(aligned(core * 512, 128), HALF)]

    load_wp.wait()

    for i in range(5):
        columns = pl.ds(256 * i, 256)
        res[:, columns] = mm(pat[...], wp[:, columns])
    for i in range(4):
        rows = pl.ds(32 * i, 32)
        values = res[rows, :]
        centred = values - jnp.mean(values, axis=1, keepdims=True)
        inverse = lax.rsqrt(jnp.mean(centred * centred, axis=1, keepdims=True) + 1e-6)
        nlow[rows, :] = (centred * inverse).astype(BF)

    for i in range(10):
        block = pl.ds(128 * i, 128)
        resT[block, :] = res[:, block].T
    mean = jnp.sum(resT[...], axis=0, keepdims=True) * (1.0 / D)
    centred = resT[...] - mean
    inverse = lax.rsqrt(jnp.sum(centred * centred, axis=0, keepdims=True) * (1.0 / D) + 1e-6)

    for i in range(15):
        if i % 5 == 0:
            load_wq[i // 5].wait()
        columns = pl.ds(256 * i, 256)
        tile = mm(nlow[...], wq[:, columns]).astype(BF)
        qkv[:, columns] = tile
        qkvT[columns, :] = tile.T

    exchange_second(0, up, NN)

    load_seg.wait()
    one_hot = (iota((8, ROWS), 0) == seg[...]).astype(F32).astype(BF)
    same_image = mm(one_hot, one_hot, TN) > 0.5

    def forward_heads(g):
        base = g * HALF
        for j in range(8):
            first, width, offset = head_window(j)
            head = pl.ds(aligned(base + 80 * j, 16), 80)
            block = pl.ds(aligned((g * 8 + j) * ROWS, ROWS), ROWS)
            keys = qkv[:, pl.ds(aligned(D + base + first, 128), width)]
            scores = mm(keys, padded(qkvT[head, :], offset, width)) * SCALE
            scores = jnp.where(same_image, scores, -1e30)
            weights = jnp.exp(scores - jnp.max(scores, axis=0, keepdims=True))
            probability = weights / jnp.sum(weights, axis=0, keepdims=True)
            low = probability.astype(BF)
            pT[block, :] = probability
            plT[block, :] = low
            values = qkvT[pl.ds(aligned(2 * D + base + 80 * j, 16), 80), :]
            attT[head, :] = mm(values, low).astype(BF)

    for g in range(2):
        forward_heads(g)

    for i in range(10):
        block = pl.ds(128 * i, 128)
        att[:, block] = attT[block, :].T
    to_pair(
        1, att.at[:, pl.ds(aligned((1 - core) * HALF, 128), HALF)], aa.at[0, pl.ds(ROWS, ROWS)]
    )
    aa[0, pl.ds(0, ROWS), :] = att[:, pl.ds(aligned(core * HALF, 128), HALF)]

    load_wo.wait()
    for i in range(5):
        columns = pl.ds(256 * i, 256)
        sent1[1, :, columns] = (res[:, columns] + mm(att[...], wo[:, columns])).astype(BF)
    exchange_first(1)

    arrivals.pop(("deliver", 0))()

    for i in range(10):
        block = pl.ds(128 * i, 128)
        upT[block, :] = up[:, block].T
    to_pair(2, upT, uu.at[0, :, pl.ds(ROWS, ROWS)])
    uu[0, :, pl.ds(0, ROWS)] = upT[...]

    for i in range(5):
        rows = pl.ds(256 * i, 256)
        gaT[rows, :] = mm(wo[rows, :], upT[...]).astype(BF)

    def gradient(grad, part):
        columns, _ = part

        total = mm(uu[grad], aa[grad, :, columns])
        gt[grad, :, :, :, columns] = total.astype(BF).reshape(4, 4, 80, columns.size)

    def first_copy(grad, part, k):
        columns, kind = part
        if kind == 0:
            to = (y + k) % 4
            source, to_llm, to_enc = gt.at[grad, to, :, :, columns], to * 4 + x, enc
        elif kind == 1:
            to = (x + k) % 4
            source, to_llm, to_enc = gt.at[grad, :, to, :, columns], y * 4 + to, enc
        else:
            to = (z + k) % 4
            source, to_llm, to_enc = gt.at[grad, :, to, :, columns], llm, to * 2 + core
        return remote(
            source, r1.at[grad, k - 1, :, :, columns],
            p1_send.at[grad, kind, k - 1], p1_recv.at[grad, kind, k - 1], to_llm, to_enc,
        )

    def second_copy(grad, part, k):
        columns, kind = part
        if kind == 0:
            to = (x + k) % 4
            to_llm = y * 4 + to
        else:
            to = (y + k) % 4
            to_llm = to * 4 + x
        return remote(
            s1.at[grad, to, :, columns], r2.at[grad, k - 1, :, columns],
            p2_send.at[grad, kind, k - 1], p2_recv.at[grad, kind, k - 1], to_llm, enc,
        )

    def cross_copy(grad, part):
        columns, _ = part
        return remote(
            crossing.at[grad, :, columns], s2.at[grad, :, columns],
            p4_send.at[grad], p4_recv.at[grad], y * 4 + z, x * 2 + core,
        )

    def third_copy(grad, k):
        to = (enc + k) % N_ENC
        return remote(
            x3.at[grad, pl.ds(aligned(to * 16, 16), 16)], r3.at[grad, k - 1],
            p3_send.at[grad, k - 1], p3_recv.at[grad, k - 1], llm, to,
        )

    def first_phase(grad, part):
        _, kind = part
        for k in range(1, 4):
            first_copy(grad, part, k).start()
        arrivals["first", grad, kind] = lambda: [
            first_copy(grad, part, k).wait_recv() for k in range(1, 4)
        ]
        sends.append(lambda: [first_copy(grad, part, k).wait_send() for k in range(1, 4)])

    def second_phase(grad, part):
        columns, kind = part
        arrivals.pop(("first", grad, kind))()

        def add(i):
            if kind == 0:
                own = gt[grad, y, i, :, columns]
            else:
                own = gt[grad, i, x if kind == 1 else z, :, columns]
            total = own.astype(F32)
            for k in range(3):
                total = total + r1[grad, k, i, :, columns].astype(F32)
            s1[grad, i, :, columns] = total.astype(BF)

        each(0, 4, add)
        for k in range(1, 4):
            second_copy(grad, part, k).start()
        arrivals["second", grad, kind] = lambda: [
            second_copy(grad, part, k).wait_recv() for k in range(1, 4)
        ]
        sends.append(lambda: [second_copy(grad, part, k).wait_send() for k in range(1, 4)])

    spread_row = iota((ROWS, 80), 0)
    spread = jnp.logical_and(
        iota((ROWS, 80), 1) == spread_row // 16 * 10 + spread_row % 16, spread_row % 16 < 10
    )
    spread = spread.astype(F32).astype(BF)

    def third_sum(grad, part):
        columns, kind = part
        arrivals.pop(("second", grad, kind))()
        total = s1[grad, x if kind == 0 else y, :, columns].astype(F32)
        for k in range(3):
            total = total + r2[grad, k, :, columns].astype(F32)
        if kind < 2:
            s2[grad, :, columns] = total.astype(BF)
            return

        crossing[grad, :, columns] = total.astype(BF)

        def if_other(run):
            pl.when(x != z)(run)

        @pl.when(x == z)
        def _():
            s2[grad, :, columns] = crossing[grad, :, columns]

        if_other(lambda: cross_copy(grad, part).start())
        arrivals["cross", grad] = lambda: if_other(lambda: cross_copy(grad, part).wait_recv())
        sends.append(lambda: if_other(lambda: cross_copy(grad, part).wait_send()))

    def third_phase(grad):
        arrivals.pop(("cross", grad))()
        x3[grad, :, :] = mm(spread, s2[grad]).astype(BF)
        each(1, N_ENC, lambda k: third_copy(grad, k).start())
        arrivals["third", grad] = lambda: each(
            1, N_ENC, lambda k: third_copy(grad, k).wait_recv()
        )
        sends.append(lambda: each(1, N_ENC, lambda k: third_copy(grad, k).wait_send()))

    def last_phase(grad, total, shift):
        arrivals.pop(("third", grad))()
        mine = x3[grad, pl.ds(aligned(enc * 16, 16), 16), :].astype(F32)
        for k in (2, 4, 6):
            mine = mine + r3[grad, k - 1].astype(F32)
        theirs = r3[grad, 0].astype(F32)
        for k in (3, 5, 7):
            theirs = theirs + r3[grad, k - 1].astype(F32)
        total[:, pl.ds(aligned(core * shift, 128), HALF)] = mine[:10, :]
        total[:, pl.ds(aligned((1 - core) * shift, 128), HALF)] = theirs[:10, :]

    arrivals.pop(("pair", 1))()
    arrivals.pop(("pair", 2))()
    for part in OUT_PARTS:
        gradient(0, part)
        first_phase(0, part)

    def backward_heads(g):
        base = g * HALF
        for j in range(8):
            first, width, offset = head_window(j)
            head = pl.ds(aligned(base + 80 * j, 16), 80)
            head_k = pl.ds(aligned(D + base + 80 * j, 16), 80)
            head_v = pl.ds(aligned(2 * D + base + 80 * j, 16), 80)
            block = pl.ds(aligned((g * 8 + j) * ROWS, ROWS), ROWS)
            values = qkv[:, pl.ds(aligned(2 * D + base + first, 128), width)]
            rows = gaT[head, :]
            grad_prob = mm(values, padded(rows, offset, width))
            probability = pT[block, :]
            weighted = jnp.sum(grad_prob * probability, axis=0, keepdims=True)
            low = (probability * (grad_prob - weighted) * SCALE).astype(BF)
            gqkvT[head, :] = mm(qkvT[head_k, :], low).astype(BF)
            gqkvT[head_k, :] = mm(qkvT[head, :], low, NT).astype(BF)
            gqkvT[head_v, :] = mm(rows, plT[block, :], NT).astype(BF)

    for g in range(2):
        backward_heads(g)

    exchange_second(1, emb_in, TN)

    mean_grad = jnp.zeros((1, ROWS), F32)
    mean_cross = jnp.zeros((1, ROWS), F32)
    for i in range(5):
        rows = pl.ds(256 * i, 256)
        tile = mm(wq[rows, :], gqkvT[...])
        gnT[rows, :] = tile
        normed = (resT[rows, :] - mean) * inverse
        mean_grad = mean_grad + jnp.sum(tile, axis=0, keepdims=True)
        mean_cross = mean_cross + jnp.sum(tile * normed, axis=0, keepdims=True)
    mean_grad = mean_grad * (1.0 / D)
    mean_cross = mean_cross * (1.0 / D)

    for i in range(5):
        rows = pl.ds(256 * i, 256)
        normed = (resT[rows, :] - mean) * inverse
        total = upT[rows, :].astype(F32) + inverse * (
            gnT[rows, :] - mean_grad - normed * mean_cross
        )
        uu[1, rows, pl.ds(0, ROWS)] = total.astype(BF)
    to_pair(3, uu.at[1, :, pl.ds(0, ROWS)], uu.at[1, :, pl.ds(ROWS, ROWS)])
    for part in OUT_PARTS[1:] + OUT_PARTS[:1]:
        second_phase(0, part)
    arrivals.pop(("pair", 0))()
    arrivals.pop(("pair", 3))()
    for part in PATCH_PARTS:
        gradient(1, part)
        first_phase(1, part)

    for part in OUT_PARTS:
        third_sum(0, part)

    arrivals.pop(("deliver", 1))()
    load_text.wait()
    position = iota((SEQ, ROWS), 0)
    put = (position == iota((SEQ, ROWS), 1) + start).astype(F32).astype(BF)

    place = iota((SEQ, 256), 0)
    inside = jnp.logical_and(place >= start, place < start + ROWS)
    for i in range(5):
        columns = pl.ds(256 * i, 256)
        placed = mm(put, emb_in[:, columns])
        merged[:, columns] = jnp.where(inside, placed, text[:, columns].astype(F32)).astype(BF)
    store_merged = local(merged, merged_hbm, 9)
    store_merged.start()
    third_phase(0)

    for part in PATCH_PARTS[2:] + PATCH_PARTS[:2]:
        second_phase(1, part)
    last_phase(0, gout, HALF)
    store_gout = local(gout, gout_hbm, 10)
    store_gout.start()
    for part in PATCH_PARTS[2:] + PATCH_PARTS[:2]:
        third_sum(1, part)
    third_phase(1)
    last_phase(1, gpatch, 512)
    store_gpatch = local(gpatch, gpatch_hbm, 11)
    store_gpatch.start()

    for sent in sends:
        sent()
    store_merged.wait()
    store_gout.wait()
    store_gpatch.wait()


def finish_kernel(a, b, c, a_out, b_out, c_out):
    a_out[...] = a[...]
    b_out[...] = b[...]
    c_out[...] = c[...]


def shards(
    patches, image_seg, owner_slot, place_start, text_embeds, merged_grad, w_patch, w_qkv, w_out
):
    smem = pl.BlockSpec(memory_space=pltpu.SMEM)
    anywhere = pl.BlockSpec(memory_space=pl.ANY)
    vmem = pl.BlockSpec(memory_space=pltpu.VMEM)
    dma = pltpu.SemaphoreType.DMA
    merged, grad_patch, grad_out = pl.pallas_call(
        kernel,
        out_shape=(
            jax.ShapeDtypeStruct((SEQ, D), BF),
            jax.ShapeDtypeStruct((10, PIN), F32),
            jax.ShapeDtypeStruct((10, D), F32),
        ),
        in_specs=[smem, smem] + [anywhere] * 7,
        out_specs=(anywhere, anywhere, anywhere),
        scratch_shapes=[
            pltpu.VMEM((1, ROWS), jnp.int32),
            pltpu.VMEM((ROWS, PIN), BF),
            pltpu.VMEM((SEQ, D), BF),
            pltpu.VMEM((SEQ, D), BF),
            pltpu.VMEM((PIN, D), BF),
            pltpu.VMEM((D, 3 * D), BF),
            pltpu.VMEM((D, D), BF),
            pltpu.VMEM((256, 256), BF),
            pltpu.VMEM((2, ROWS, D), BF),
            pltpu.VMEM((2, 256, HALF), BF),
            pltpu.VMEM((2, 256, HALF), BF),
            pltpu.VMEM((ROWS, D), BF),
            pltpu.VMEM((ROWS, D), BF),
            pltpu.VMEM((ROWS, D), F32),
            pltpu.VMEM((ROWS, D), BF),
            pltpu.VMEM((D, ROWS), F32),
            pltpu.VMEM((ROWS, 3 * D), BF),
            pltpu.VMEM((3 * D, ROWS), BF),
            pltpu.VMEM((HEADS * ROWS, ROWS), F32),
            pltpu.VMEM((HEADS * ROWS, ROWS), BF),
            pltpu.VMEM((D, ROWS), BF),
            pltpu.VMEM((ROWS, D), BF),
            pltpu.VMEM((D, ROWS), BF),
            pltpu.VMEM((D, ROWS), BF),
            pltpu.VMEM((3 * D, ROWS), BF),
            pltpu.VMEM((D, ROWS), F32),
            pltpu.VMEM((SEQ, D), BF),
            pltpu.VMEM((10, PIN), F32),
            pltpu.VMEM((10, D), F32),
            pltpu.VMEM((2, D, 2 * ROWS), BF),
            pltpu.VMEM((2, 2 * ROWS, HALF), BF),
            pltpu.VMEM((2, 4, 4, 80, HALF), BF),
            pltpu.VMEM((2, 3, 4, 80, HALF), BF),
            pltpu.VMEM((2, 4, 80, HALF), BF),
            pltpu.VMEM((2, 3, 80, HALF), BF),
            pltpu.VMEM((2, 80, HALF), BF),
            pltpu.VMEM((2, 80, HALF), BF),
            pltpu.VMEM((2, ROWS, HALF), BF),
            pltpu.VMEM((2, 7, 16, HALF), BF),
            dma((12,)),
            dma((2, 2, N_LLM)),
            dma((2, 2, N_LLM)),
            dma((4,)),
            dma((4,)),
            dma((2, 3, 3)),
            dma((2, 3, 3)),
            dma((2, 3, 3)),
            dma((2, 3, 3)),
            dma((2, 7)),
            dma((2, 7)),
            dma((2,)),
            dma((2,)),
        ],
        compiler_params=pltpu.CompilerParams(
            collective_id=0, has_side_effects=True, vmem_limit_bytes=56 * 1024 * 1024
        ),
    )(
        owner_slot.reshape(1, 128), place_start, image_seg, patches, text_embeds, merged_grad,
        w_patch, w_qkv, w_out,
    )
    merged, grad_patch, grad_out = pl.pallas_call(
        finish_kernel,
        out_shape=(
            jax.ShapeDtypeStruct((SEQ, D), BF),
            jax.ShapeDtypeStruct((10, PIN), F32),
            jax.ShapeDtypeStruct((10, D), F32),
        ),
        in_specs=[vmem] * 3,
        out_specs=(vmem, vmem, vmem),
    )(merged, grad_patch, grad_out)
    return (merged, grad_patch.T, grad_out.T)


def solution(mesh):
    rows = P(("llm", "enc"), None)
    columns = P(None, ("llm", "enc"))
    return jax.shard_map(
        shards,
        mesh=mesh,
        in_specs=(rows, P(), P(), rows, rows, rows, P(), P(), P()),
        out_specs=(rows, columns, columns),
        check_vma=False,
    )
```

```python
import jax
import jax.numpy as jnp
from jax import lax
from jax.experimental import pallas as pl
from jax.experimental.pallas import tpu as pltpu
from jax.sharding import PartitionSpec as P

D = 1280
HEADS = 16
HEAD_DIM = 80
PIN = 1152
ROWS = 128
SEQ = 160
N_LLM = 16
N_ENC = 8
HALF = 640
SCALE = HEAD_DIM ** (-0.5)

OUT_PARTS = ((pl.ds(256, 384), 2), (pl.ds(0, 128), 0), (pl.ds(128, 128), 1))
PATCH_PARTS = ((pl.ds(0, 256), 0), (pl.ds(256, 256), 1), (pl.ds(512, 128), 2))

BF = jnp.bfloat16
F32 = jnp.float32
MESH = pl.DeviceIdType.MESH
NN = (((1,), (0,)), ((), ()))
NT = (((1,), (1,)), ((), ()))
TN = (((0,), (0,)), ((), ()))


def mm(a, b, dims=NN):
    return lax.dot_general(a, b, dims, preferred_element_type=F32)


def iota(shape, axis):
    return lax.broadcasted_iota(jnp.int32, shape, axis)


def aligned(value, unit):
    return value if isinstance(value, int) else pl.multiple_of(value, unit)


def each(low, high, body):
    for i in range(low, high):
        body(i)


def head_window(j):
    first = 80 * j // 128 * 128
    last = -(-(80 * j + 80) // 128) * 128
    return first, last - first, 80 * j - first


def padded(rows, offset, width):
    pieces = []
    if offset:
        pieces.append(jnp.zeros((offset, ROWS), BF))
    pieces.append(rows)
    if width - offset - 80:
        pieces.append(jnp.zeros((width - offset - 80, ROWS), BF))
    return jnp.concatenate(pieces, axis=0)


def kernel(
    owner_ref, start_ref, seg_hbm, patches_hbm, text_hbm, mgrad_hbm, wp_hbm, wq_hbm, wo_hbm,
    merged_hbm, gpatch_hbm, gout_hbm,
    seg, pat, text, mgrad, wp, wq, wo,
    perm, sent1, recv1, sent2, emb_in, up, res, nlow, resT, qkv, qkvT, pT, plT, attT, att,
    upT, gaT, gqkvT, gnT, merged, gpatch, gout, uu, aa, gt, r1, s1, r2, crossing, s2, x3, r3,
    local_sem, ex_send, ex_recv, pair_send, pair_recv, p1_send, p1_recv, p2_send, p2_recv,
    p3_send, p3_recv, p4_send, p4_recv,
):
    llm = lax.axis_index("llm")
    enc = lax.axis_index("enc")
    y, x = llm // 4, llm % 4
    z, core = enc // 2, enc % 2
    device = llm * N_ENC + enc
    start = start_ref[0, 0]
    arrivals, sends = {}, []

    def local(source, target, slot):
        return pltpu.make_async_copy(source, target, local_sem.at[slot])

    def remote(source, target, send, recv, to_llm, to_enc):
        return pltpu.make_async_remote_copy(
            src_ref=source, dst_ref=target, send_sem=send, recv_sem=recv,
            device_id=(to_llm, to_enc), device_id_type=MESH,
        )

    load_mgrad = local(mgrad_hbm, mgrad, 0)
    load_pat = local(patches_hbm, pat, 1)
    load_seg = local(seg_hbm.at[device], seg, 2)
    load_wp = local(wp_hbm, wp, 3)
    load_wq = [
        local(wq_hbm.at[:, pl.ds(D * i, D)], wq.at[:, pl.ds(D * i, D)], 4 + i) for i in range(3)
    ]
    load_wo = local(wo_hbm, wo, 7)
    load_text = local(text_hbm, text, 8)
    for load in (load_mgrad, load_pat, load_seg, load_wp, *load_wq, load_wo, load_text):
        load.start()

    barrier = pltpu.get_barrier_semaphore()

    def greet_llm(k):
        pl.semaphore_signal(
            barrier, inc=1, device_id=((llm + k) % N_LLM, enc), device_id_type=MESH
        )

    def greet_enc(k):
        pl.semaphore_signal(
            barrier, inc=1, device_id=(llm, (enc + k) % N_ENC), device_id_type=MESH
        )

    each(1, N_LLM, greet_llm)
    each(1, N_ENC, greet_enc)

    @pl.when(x != z)
    def _():
        pl.semaphore_signal(
            barrier, inc=1, device_id=(y * 4 + z, x * 2 + core), device_id_type=MESH
        )

    lane = iota((16, 256), 1)
    row = iota((16, 256), 0)

    def owner_rows(s):
        rank = owner_ref[0, s * N_ENC + enc]
        hit = (lane == rank * 16 + row).astype(F32)
        perm[pl.ds(aligned(s * 16, 16), 16), :] = hit.astype(BF)

    each(0, N_LLM, owner_rows)

    load_mgrad.wait()
    take = (iota((ROWS, SEQ), 1) == iota((ROWS, SEQ), 0) + start).astype(F32).astype(BF)
    sent1[0, :, :] = mm(take, mgrad[...]).astype(BF)

    pl.semaphore_wait(barrier, N_LLM - 1 + N_ENC - 1 + (x != z).astype(jnp.int32))

    def piece(ref, j):
        return ref.at[pl.ds(aligned(j // 2 * 16, 16), 16), pl.ds(aligned(j % 2 * HALF, 128), HALF)]

    def scatter(way, k):
        to = (llm + k) % N_LLM
        return remote(
            piece(sent1.at[way], to), recv1.at[way, pl.ds(aligned(llm * 16, 16), 16)],
            ex_send.at[way, 0, k], ex_recv.at[way, 0, k], to, enc,
        )

    def scatter_arrival(way, k):
        source = (llm + N_LLM - k) % N_LLM
        return remote(
            piece(sent1.at[way], llm), recv1.at[way, pl.ds(aligned(source * 16, 16), 16)],
            ex_send.at[way, 0, k], ex_recv.at[way, 0, k], (llm + k) % N_LLM, enc,
        )

    def deliver(way, target, k):
        to = (llm + k) % N_LLM
        return remote(
            sent2.at[way, pl.ds(aligned(to * 16, 16), 16)], piece(target, llm),
            ex_send.at[way, 1, k], ex_recv.at[way, 1, k], to, enc,
        )

    def deliver_arrival(way, target, k):
        source = (llm + N_LLM - k) % N_LLM
        return remote(
            sent2.at[way, pl.ds(aligned(llm * 16, 16), 16)], piece(target, source),
            ex_send.at[way, 1, k], ex_recv.at[way, 1, k], (llm + k) % N_LLM, enc,
        )

    def own_piece(ref):
        return ref[pl.ds(aligned(llm // 2 * 16, 16), 16), pl.ds(aligned(llm % 2 * HALF, 128), HALF)]

    def exchange_first(way):
        each(1, N_LLM, lambda k: scatter(way, k).start())
        arrivals["scatter", way] = lambda: each(
            1, N_LLM, lambda k: scatter_arrival(way, k).wait_recv()
        )
        sends.append(lambda: each(1, N_LLM, lambda k: scatter(way, k).wait_send()))
        recv1[way, pl.ds(aligned(llm * 16, 16), 16), :] = own_piece(sent1.at[way])

    def exchange_second(way, target, dims):
        arrivals.pop(("scatter", way))()
        sent2[way, :, :] = mm(perm[...], recv1[way], dims).astype(BF)
        each(1, N_LLM, lambda k: deliver(way, target, k).start())
        arrivals["deliver", way] = lambda: each(
            1, N_LLM, lambda k: deliver_arrival(way, target, k).wait_recv()
        )
        sends.append(lambda: each(1, N_LLM, lambda k: deliver(way, target, k).wait_send()))
        target[pl.ds(aligned(llm // 2 * 16, 16), 16), pl.ds(aligned(llm % 2 * HALF, 128), HALF)] = (
            sent2[way, pl.ds(aligned(llm * 16, 16), 16), :]
        )

    exchange_first(0)

    other = enc + 1 - 2 * core

    def to_pair(slot, source, target):
        copy = remote(source, target, pair_send.at[slot], pair_recv.at[slot], llm, other)
        copy.start()
        arrivals["pair", slot] = copy.wait_recv
        sends.append(copy.wait_send)

    load_pat.wait()
    to_pair(
        0, pat.at[:, pl.ds(aligned((1 - core) * 512, 128), HALF)], aa.at[1, pl.ds(ROWS, ROWS)]
    )
    aa[1, pl.ds(0, ROWS), :] = pat[:, pl.ds(aligned(core * 512, 128), HALF)]

    load_wp.wait()

    for i in range(5):
        columns = pl.ds(256 * i, 256)
        res[:, columns] = mm(pat[...], wp[:, columns])
    for i in range(4):
        rows = pl.ds(32 * i, 32)
        values = res[rows, :]
        centred = values - jnp.mean(values, axis=1, keepdims=True)
        inverse = lax.rsqrt(jnp.mean(centred * centred, axis=1, keepdims=True) + 1e-6)
        nlow[rows, :] = (centred * inverse).astype(BF)

    for i in range(10):
        block = pl.ds(128 * i, 128)
        resT[block, :] = res[:, block].T
    mean = jnp.sum(resT[...], axis=0, keepdims=True) * (1.0 / D)
    centred = resT[...] - mean
    inverse = lax.rsqrt(jnp.sum(centred * centred, axis=0, keepdims=True) * (1.0 / D) + 1e-6)

    for i in range(15):
        if i % 5 == 0:
            load_wq[i // 5].wait()
        columns = pl.ds(256 * i, 256)
        tile = mm(nlow[...], wq[:, columns]).astype(BF)
        qkv[:, columns] = tile
        qkvT[columns, :] = tile.T

    exchange_second(0, up, NN)

    load_seg.wait()
    one_hot = (iota((8, ROWS), 0) == seg[...]).astype(F32).astype(BF)
    same_image = mm(one_hot, one_hot, TN) > 0.5

    def forward_heads(g):
        base = g * HALF
        for j in range(8):
            first, width, offset = head_window(j)
            head = pl.ds(aligned(base + 80 * j, 16), 80)
            block = pl.ds(aligned((g * 8 + j) * ROWS, ROWS), ROWS)
            keys = qkv[:, pl.ds(aligned(D + base + first, 128), width)]
            scores = mm(keys, padded(qkvT[head, :], offset, width)) * SCALE
            scores = jnp.where(same_image, scores, -1e30)
            weights = jnp.exp(scores - jnp.max(scores, axis=0, keepdims=True))
            probability = weights / jnp.sum(weights, axis=0, keepdims=True)
            low = probability.astype(BF)
            pT[block, :] = probability
            plT[block, :] = low
            values = qkvT[pl.ds(aligned(2 * D + base + 80 * j, 16), 80), :]
            attT[head, :] = mm(values, low).astype(BF)

    for g in range(2):
        forward_heads(g)

    for i in range(10):
        block = pl.ds(128 * i, 128)
        att[:, block] = attT[block, :].T
    to_pair(
        1, att.at[:, pl.ds(aligned((1 - core) * HALF, 128), HALF)], aa.at[0, pl.ds(ROWS, ROWS)]
    )
    aa[0, pl.ds(0, ROWS), :] = att[:, pl.ds(aligned(core * HALF, 128), HALF)]

    load_wo.wait()
    for i in range(5):
        columns = pl.ds(256 * i, 256)
        sent1[1, :, columns] = (res[:, columns] + mm(att[...], wo[:, columns])).astype(BF)
    exchange_first(1)

    arrivals.pop(("deliver", 0))()

    for i in range(10):
        block = pl.ds(128 * i, 128)
        upT[block, :] = up[:, block].T
    to_pair(2, upT, uu.at[0, :, pl.ds(ROWS, ROWS)])
    uu[0, :, pl.ds(0, ROWS)] = upT[...]

    for i in range(5):
        rows = pl.ds(256 * i, 256)
        gaT[rows, :] = mm(wo[rows, :], upT[...]).astype(BF)

    def gradient(grad, part):
        columns, _ = part

        total = mm(uu[grad], aa[grad, :, columns])
        gt[grad, :, :, :, columns] = total.astype(BF).reshape(4, 4, 80, columns.size)

    def first_copy(grad, part, k):
        columns, kind = part
        if kind == 0:
            to = (y + k) % 4
            source, to_llm, to_enc = gt.at[grad, to, :, :, columns], to * 4 + x, enc
        elif kind == 1:
            to = (x + k) % 4
            source, to_llm, to_enc = gt.at[grad, :, to, :, columns], y * 4 + to, enc
        else:
            to = (z + k) % 4
            source, to_llm, to_enc = gt.at[grad, :, to, :, columns], llm, to * 2 + core
        return remote(
            source, r1.at[grad, k - 1, :, :, columns],
            p1_send.at[grad, kind, k - 1], p1_recv.at[grad, kind, k - 1], to_llm, to_enc,
        )

    def second_copy(grad, part, k):
        columns, kind = part
        if kind == 0:
            to = (x + k) % 4
            to_llm = y * 4 + to
        else:
            to = (y + k) % 4
            to_llm = to * 4 + x
        return remote(
            s1.at[grad, to, :, columns], r2.at[grad, k - 1, :, columns],
            p2_send.at[grad, kind, k - 1], p2_recv.at[grad, kind, k - 1], to_llm, enc,
        )

    def cross_copy(grad, part):
        columns, _ = part
        return remote(
            crossing.at[grad, :, columns], s2.at[grad, :, columns],
            p4_send.at[grad], p4_recv.at[grad], y * 4 + z, x * 2 + core,
        )

    def third_copy(grad, k):
        to = (enc + k) % N_ENC
        return remote(
            x3.at[grad, pl.ds(aligned(to * 16, 16), 16)], r3.at[grad, k - 1],
            p3_send.at[grad, k - 1], p3_recv.at[grad, k - 1], llm, to,
        )

    def first_phase(grad, part):
        _, kind = part
        for k in range(1, 4):
            first_copy(grad, part, k).start()
        arrivals["first", grad, kind] = lambda: [
            first_copy(grad, part, k).wait_recv() for k in range(1, 4)
        ]
        sends.append(lambda: [first_copy(grad, part, k).wait_send() for k in range(1, 4)])

    def second_phase(grad, part):
        columns, kind = part
        arrivals.pop(("first", grad, kind))()

        def add(i):
            if kind == 0:
                own = gt[grad, y, i, :, columns]
            else:
                own = gt[grad, i, x if kind == 1 else z, :, columns]
            total = own.astype(F32)
            for k in range(3):
                total = total + r1[grad, k, i, :, columns].astype(F32)
            s1[grad, i, :, columns] = total.astype(BF)

        each(0, 4, add)
        for k in range(1, 4):
            second_copy(grad, part, k).start()
        arrivals["second", grad, kind] = lambda: [
            second_copy(grad, part, k).wait_recv() for k in range(1, 4)
        ]
        sends.append(lambda: [second_copy(grad, part, k).wait_send() for k in range(1, 4)])

    spread_row = iota((ROWS, 80), 0)
    spread = jnp.logical_and(
        iota((ROWS, 80), 1) == spread_row // 16 * 10 + spread_row % 16, spread_row % 16 < 10
    )
    spread = spread.astype(F32).astype(BF)

    def third_sum(grad, part):
        columns, kind = part
        arrivals.pop(("second", grad, kind))()
        total = s1[grad, x if kind == 0 else y, :, columns].astype(F32)
        for k in range(3):
            total = total + r2[grad, k, :, columns].astype(F32)
        if kind < 2:
            s2[grad, :, columns] = total.astype(BF)
            return

        crossing[grad, :, columns] = total.astype(BF)

        def if_other(run):
            pl.when(x != z)(run)

        @pl.when(x == z)
        def _():
            s2[grad, :, columns] = crossing[grad, :, columns]

        if_other(lambda: cross_copy(grad, part).start())
        arrivals["cross", grad] = lambda: if_other(lambda: cross_copy(grad, part).wait_recv())
        sends.append(lambda: if_other(lambda: cross_copy(grad, part).wait_send()))

    def third_phase(grad):
        arrivals.pop(("cross", grad))()
        x3[grad, :, :] = mm(spread, s2[grad]).astype(BF)
        each(1, N_ENC, lambda k: third_copy(grad, k).start())
        arrivals["third", grad] = lambda: each(
            1, N_ENC, lambda k: third_copy(grad, k).wait_recv()
        )
        sends.append(lambda: each(1, N_ENC, lambda k: third_copy(grad, k).wait_send()))

    def last_phase(grad, total, shift):
        arrivals.pop(("third", grad))()
        mine = x3[grad, pl.ds(aligned(enc * 16, 16), 16), :].astype(F32)
        for k in (2, 4, 6):
            mine = mine + r3[grad, k - 1].astype(F32)
        theirs = r3[grad, 0].astype(F32)
        for k in (3, 5, 7):
            theirs = theirs + r3[grad, k - 1].astype(F32)
        total[:, pl.ds(aligned(core * shift, 128), HALF)] = mine[:10, :]
        total[:, pl.ds(aligned((1 - core) * shift, 128), HALF)] = theirs[:10, :]

    arrivals.pop(("pair", 1))()
    arrivals.pop(("pair", 2))()
    for part in OUT_PARTS:
        gradient(0, part)
        first_phase(0, part)

    def backward_heads(g):
        base = g * HALF
        for j in range(8):
            first, width, offset = head_window(j)
            head = pl.ds(aligned(base + 80 * j, 16), 80)
            head_k = pl.ds(aligned(D + base + 80 * j, 16), 80)
            head_v = pl.ds(aligned(2 * D + base + 80 * j, 16), 80)
            block = pl.ds(aligned((g * 8 + j) * ROWS, ROWS), ROWS)
            values = qkv[:, pl.ds(aligned(2 * D + base + first, 128), width)]
            rows = gaT[head, :]
            grad_prob = mm(values, padded(rows, offset, width))
            probability = pT[block, :]
            weighted = jnp.sum(grad_prob * probability, axis=0, keepdims=True)
            low = (probability * (grad_prob - weighted) * SCALE).astype(BF)
            gqkvT[head, :] = mm(qkvT[head_k, :], low).astype(BF)
            gqkvT[head_k, :] = mm(qkvT[head, :], low, NT).astype(BF)
            gqkvT[head_v, :] = mm(rows, plT[block, :], NT).astype(BF)

    for g in range(2):
        backward_heads(g)

    exchange_second(1, emb_in, TN)

    mean_grad = jnp.zeros((1, ROWS), F32)
    mean_cross = jnp.zeros((1, ROWS), F32)
    for i in range(5):
        rows = pl.ds(256 * i, 256)
        tile = mm(wq[rows, :], gqkvT[...])
        gnT[rows, :] = tile
        normed = (resT[rows, :] - mean) * inverse
        mean_grad = mean_grad + jnp.sum(tile, axis=0, keepdims=True)
        mean_cross = mean_cross + jnp.sum(tile * normed, axis=0, keepdims=True)
    mean_grad = mean_grad * (1.0 / D)
    mean_cross = mean_cross * (1.0 / D)

    for i in range(5):
        rows = pl.ds(256 * i, 256)
        normed = (resT[rows, :] - mean) * inverse
        total = upT[rows, :].astype(F32) + inverse * (
            gnT[rows, :] - mean_grad - normed * mean_cross
        )
        uu[1, rows, pl.ds(0, ROWS)] = total.astype(BF)
    to_pair(3, uu.at[1, :, pl.ds(0, ROWS)], uu.at[1, :, pl.ds(ROWS, ROWS)])
    for part in OUT_PARTS[1:]:
        second_phase(0, part)
    arrivals.pop(("pair", 0))()
    arrivals.pop(("pair", 3))()
    for part in PATCH_PARTS:
        gradient(1, part)
        first_phase(1, part)

    for part in OUT_PARTS[1:]:
        third_sum(0, part)

    arrivals.pop(("deliver", 1))()
    load_text.wait()
    position = iota((SEQ, ROWS), 0)
    put = (position == iota((SEQ, ROWS), 1) + start).astype(F32).astype(BF)

    place = iota((SEQ, 256), 0)
    inside = jnp.logical_and(place >= start, place < start + ROWS)
    for i in range(5):
        columns = pl.ds(256 * i, 256)
        placed = mm(put, emb_in[:, columns])
        merged[:, columns] = jnp.where(inside, placed, text[:, columns].astype(F32)).astype(BF)
    store_merged = local(merged, merged_hbm, 9)
    store_merged.start()
    second_phase(0, OUT_PARTS[0])

    for part in PATCH_PARTS[2:] + PATCH_PARTS[:2]:
        second_phase(1, part)
    third_sum(0, OUT_PARTS[0])
    for part in PATCH_PARTS[2:] + PATCH_PARTS[:2]:
        third_sum(1, part)
    third_phase(0)
    third_phase(1)
    last_phase(0, gout, HALF)
    store_gout = local(gout, gout_hbm, 10)
    store_gout.start()
    last_phase(1, gpatch, 512)
    store_gpatch = local(gpatch, gpatch_hbm, 11)
    store_gpatch.start()

    for sent in sends:
        sent()
    store_merged.wait()
    store_gout.wait()
    store_gpatch.wait()


def finish_kernel(a, b, c, a_out, b_out, c_out):
    a_out[...] = a[...]
    b_out[...] = b[...]
    c_out[...] = c[...]


def shards(
    patches, image_seg, owner_slot, place_start, text_embeds, merged_grad, w_patch, w_qkv, w_out
):
    smem = pl.BlockSpec(memory_space=pltpu.SMEM)
    anywhere = pl.BlockSpec(memory_space=pl.ANY)
    vmem = pl.BlockSpec(memory_space=pltpu.VMEM)
    dma = pltpu.SemaphoreType.DMA
    merged, grad_patch, grad_out = pl.pallas_call(
        kernel,
        out_shape=(
            jax.ShapeDtypeStruct((SEQ, D), BF),
            jax.ShapeDtypeStruct((10, PIN), F32),
            jax.ShapeDtypeStruct((10, D), F32),
        ),
        in_specs=[smem, smem] + [anywhere] * 7,
        out_specs=(anywhere, anywhere, anywhere),
        scratch_shapes=[
            pltpu.VMEM((1, ROWS), jnp.int32),
            pltpu.VMEM((ROWS, PIN), BF),
            pltpu.VMEM((SEQ, D), BF),
            pltpu.VMEM((SEQ, D), BF),
            pltpu.VMEM((PIN, D), BF),
            pltpu.VMEM((D, 3 * D), BF),
            pltpu.VMEM((D, D), BF),
            pltpu.VMEM((256, 256), BF),
            pltpu.VMEM((2, ROWS, D), BF),
            pltpu.VMEM((2, 256, HALF), BF),
            pltpu.VMEM((2, 256, HALF), BF),
            pltpu.VMEM((ROWS, D), BF),
            pltpu.VMEM((ROWS, D), BF),
            pltpu.VMEM((ROWS, D), F32),
            pltpu.VMEM((ROWS, D), BF),
            pltpu.VMEM((D, ROWS), F32),
            pltpu.VMEM((ROWS, 3 * D), BF),
            pltpu.VMEM((3 * D, ROWS), BF),
            pltpu.VMEM((HEADS * ROWS, ROWS), F32),
            pltpu.VMEM((HEADS * ROWS, ROWS), BF),
            pltpu.VMEM((D, ROWS), BF),
            pltpu.VMEM((ROWS, D), BF),
            pltpu.VMEM((D, ROWS), BF),
            pltpu.VMEM((D, ROWS), BF),
            pltpu.VMEM((3 * D, ROWS), BF),
            pltpu.VMEM((D, ROWS), F32),
            pltpu.VMEM((SEQ, D), BF),
            pltpu.VMEM((10, PIN), F32),
            pltpu.VMEM((10, D), F32),
            pltpu.VMEM((2, D, 2 * ROWS), BF),
            pltpu.VMEM((2, 2 * ROWS, HALF), BF),
            pltpu.VMEM((2, 4, 4, 80, HALF), BF),
            pltpu.VMEM((2, 3, 4, 80, HALF), BF),
            pltpu.VMEM((2, 4, 80, HALF), BF),
            pltpu.VMEM((2, 3, 80, HALF), BF),
            pltpu.VMEM((2, 80, HALF), BF),
            pltpu.VMEM((2, 80, HALF), BF),
            pltpu.VMEM((2, ROWS, HALF), BF),
            pltpu.VMEM((2, 7, 16, HALF), BF),
            dma((12,)),
            dma((2, 2, N_LLM)),
            dma((2, 2, N_LLM)),
            dma((4,)),
            dma((4,)),
            dma((2, 3, 3)),
            dma((2, 3, 3)),
            dma((2, 3, 3)),
            dma((2, 3, 3)),
            dma((2, 7)),
            dma((2, 7)),
            dma((2,)),
            dma((2,)),
        ],
        compiler_params=pltpu.CompilerParams(
            collective_id=0, has_side_effects=True, vmem_limit_bytes=56 * 1024 * 1024
        ),
    )(
        owner_slot.reshape(1, 128), place_start, image_seg, patches, text_embeds, merged_grad,
        w_patch, w_qkv, w_out,
    )
    merged, grad_patch, grad_out = pl.pallas_call(
        finish_kernel,
        out_shape=(
            jax.ShapeDtypeStruct((SEQ, D), BF),
            jax.ShapeDtypeStruct((10, PIN), F32),
            jax.ShapeDtypeStruct((10, D), F32),
        ),
        in_specs=[vmem] * 3,
        out_specs=(vmem, vmem, vmem),
    )(merged, grad_patch, grad_out)
    return (merged, grad_patch.T, grad_out.T)


def solution(mesh):
    rows = P(("llm", "enc"), None)
    columns = P(None, ("llm", "enc"))
    return jax.shard_map(
        shards,
        mesh=mesh,
        in_specs=(rows, P(), P(), rows, rows, rows, P(), P(), P()),
        out_specs=(rows, columns, columns),
        check_vma=False,
    )
```

```python
import jax
import jax.numpy as jnp
from jax import lax
from jax.experimental import pallas as pl
from jax.experimental.pallas import tpu as pltpu
from jax.sharding import PartitionSpec as P

D = 1280
HEADS = 16
HEAD_DIM = 80
PIN = 1152
ROWS = 128
SEQ = 160
N_LLM = 16
N_ENC = 8
HALF = 640
SCALE = HEAD_DIM ** (-0.5)

OUT_PARTS = (
    ((pl.ds(384, 256), 2), (pl.ds(0, 256), 0), (pl.ds(256, 128), 1)),
    ((pl.ds(384, 256), 2), (pl.ds(0, 128), 0), (pl.ds(128, 256), 1)),
)
PATCH_PARTS = (
    ((pl.ds(384, 128), 2), (pl.ds(0, 256), 0), (pl.ds(256, 128), 1)),
    ((pl.ds(384, 256), 2), (pl.ds(0, 128), 0), (pl.ds(128, 256), 1)),
)
PARTS = (OUT_PARTS, PATCH_PARTS)
DOT_LANES = (pl.ds(384, 256), pl.ds(0, 256), pl.ds(256, 128))

BF = jnp.bfloat16
F32 = jnp.float32
MESH = pl.DeviceIdType.MESH
NN = (((1,), (0,)), ((), ()))
NT = (((1,), (1,)), ((), ()))
TN = (((0,), (0,)), ((), ()))


def mm(a, b, dims=NN):
    return lax.dot_general(a, b, dims, preferred_element_type=F32)


def iota(shape, axis):
    return lax.broadcasted_iota(jnp.int32, shape, axis)


def aligned(value, unit):
    return value if isinstance(value, int) else pl.multiple_of(value, unit)


def each(low, high, body):
    for i in range(low, high):
        body(i)


def head_window(j):
    first = 80 * j // 128 * 128
    last = -(-(80 * j + 80) // 128) * 128
    return first, last - first, 80 * j - first


def padded(rows, offset, width):
    pieces = []
    if offset:
        pieces.append(jnp.zeros((offset, ROWS), BF))
    pieces.append(rows)
    if width - offset - 80:
        pieces.append(jnp.zeros((width - offset - 80, ROWS), BF))
    return jnp.concatenate(pieces, axis=0)


def kernel(
    owner_hbm, start_hbm, seg_hbm, patches_hbm, text_hbm, mgrad_hbm, wp_hbm, wq_hbm, wo_hbm,
    merged_hbm, gpatch_hbm, gout_hbm,
    owner, first_row, seg, pat, text, mgrad, wp, wq, wo,
    perm, sent1, recv1, sent2, emb_in, up, res, nlow, resT, qkv, qkvT, pT, plT, attT, att,
    upT, gaT, gqkvT, gnT, merged, gpatch, gout, uu, aa, gt, r1, s1, r2, crossing, s2, x3, r3,
    local_sem, ex_send, ex_recv, pair_send, pair_recv, p1_send, p1_recv, p2_send, p2_recv,
    p3_send, p3_recv, p4_send, p4_recv,
):
    llm = lax.axis_index("llm")
    enc = lax.axis_index("enc")
    y, x = llm // 4, llm % 4
    z, core = enc // 2, enc % 2
    device = llm * N_ENC + enc
    arrivals, sends = {}, []

    def local(source, target, slot):
        return pltpu.make_async_copy(source, target, local_sem.at[slot])

    def remote(source, target, send, recv, to_llm, to_enc):
        return pltpu.make_async_remote_copy(
            src_ref=source, dst_ref=target, send_sem=send, recv_sem=recv,
            device_id=(to_llm, to_enc), device_id_type=MESH,
        )

    load_owner = local(owner_hbm, owner, 12)
    load_start = local(start_hbm, first_row, 13)
    load_mgrad = local(mgrad_hbm, mgrad, 0)
    load_pat = local(patches_hbm, pat, 1)
    load_seg = local(seg_hbm.at[device], seg, 2)
    load_wp = local(wp_hbm, wp, 3)
    load_wq = [
        local(wq_hbm.at[:, pl.ds(D * i, D)], wq.at[:, pl.ds(D * i, D)], 4 + i) for i in range(3)
    ]
    load_wo = local(wo_hbm, wo, 7)
    load_text = local(text_hbm, text, 8)
    for load in (load_owner, load_start, load_mgrad, load_pat, load_seg, load_wp, *load_wq, load_wo, load_text):
        load.start()

    barrier = pltpu.get_barrier_semaphore()

    def greet_llm(k):
        pl.semaphore_signal(
            barrier, inc=1, device_id=((llm + k) % N_LLM, enc), device_id_type=MESH
        )

    def greet_enc(k):
        pl.semaphore_signal(
            barrier, inc=1, device_id=(llm, (enc + k) % N_ENC), device_id_type=MESH
        )

    each(1, N_LLM, greet_llm)
    each(1, N_ENC, greet_enc)

    @pl.when(x != z)
    def _():
        pl.semaphore_signal(
            barrier, inc=1, device_id=(y * 4 + z, x * 2 + core), device_id_type=MESH
        )

    load_owner.wait()
    load_start.wait()
    start = first_row[0, 0]
    lane = iota((16, 256), 1)
    row = iota((16, 256), 0)

    def owner_rows(s):
        rank = owner[0, s * N_ENC + enc]
        hit = (lane == rank * 16 + row).astype(F32)
        perm[pl.ds(aligned(s * 16, 16), 16), :] = hit.astype(BF)

    each(0, N_LLM, owner_rows)

    load_mgrad.wait()
    take = (iota((ROWS, SEQ), 1) == iota((ROWS, SEQ), 0) + start).astype(F32).astype(BF)
    sent1[0, :, :] = mm(take, mgrad[...]).astype(BF)

    pl.semaphore_wait(barrier, N_LLM - 1 + N_ENC - 1 + (x != z).astype(jnp.int32))

    def piece(ref, j):
        return ref.at[pl.ds(aligned(j // 2 * 16, 16), 16), pl.ds(aligned(j % 2 * HALF, 128), HALF)]

    def scatter(way, k):
        to = (llm + k) % N_LLM
        return remote(
            piece(sent1.at[way], to), recv1.at[way, pl.ds(aligned(llm * 16, 16), 16)],
            ex_send.at[way, 0, k], ex_recv.at[way, 0, k], to, enc,
        )

    def scatter_arrival(way, k):
        source = (llm + N_LLM - k) % N_LLM
        return remote(
            piece(sent1.at[way], llm), recv1.at[way, pl.ds(aligned(source * 16, 16), 16)],
            ex_send.at[way, 0, k], ex_recv.at[way, 0, k], (llm + k) % N_LLM, enc,
        )

    def deliver(way, target, k):
        to = (llm + k) % N_LLM
        return remote(
            sent2.at[way, pl.ds(aligned(to * 16, 16), 16)], piece(target, llm),
            ex_send.at[way, 1, k], ex_recv.at[way, 1, k], to, enc,
        )

    def deliver_arrival(way, target, k):
        source = (llm + N_LLM - k) % N_LLM
        return remote(
            sent2.at[way, pl.ds(aligned(llm * 16, 16), 16)], piece(target, source),
            ex_send.at[way, 1, k], ex_recv.at[way, 1, k], (llm + k) % N_LLM, enc,
        )

    def own_piece(ref):
        return ref[pl.ds(aligned(llm // 2 * 16, 16), 16), pl.ds(aligned(llm % 2 * HALF, 128), HALF)]

    def exchange_first(way):
        each(1, N_LLM, lambda k: scatter(way, k).start())
        arrivals["scatter", way] = lambda: each(
            1, N_LLM, lambda k: scatter_arrival(way, k).wait_recv()
        )
        sends.append(lambda: each(1, N_LLM, lambda k: scatter(way, k).wait_send()))
        recv1[way, pl.ds(aligned(llm * 16, 16), 16), :] = own_piece(sent1.at[way])

    def exchange_second(way, target, dims):
        arrivals.pop(("scatter", way))()
        sent2[way, :, :] = mm(perm[...], recv1[way], dims).astype(BF)
        each(1, N_LLM, lambda k: deliver(way, target, k).start())
        arrivals["deliver", way] = lambda: each(
            1, N_LLM, lambda k: deliver_arrival(way, target, k).wait_recv()
        )
        sends.append(lambda: each(1, N_LLM, lambda k: deliver(way, target, k).wait_send()))
        target[pl.ds(aligned(llm // 2 * 16, 16), 16), pl.ds(aligned(llm % 2 * HALF, 128), HALF)] = (
            sent2[way, pl.ds(aligned(llm * 16, 16), 16), :]
        )

    exchange_first(0)
    other = enc + 1 - 2 * core

    def to_pair(slot, source, target):
        copy = remote(source, target, pair_send.at[slot], pair_recv.at[slot], llm, other)
        copy.start()
        arrivals["pair", slot] = copy.wait_recv
        sends.append(copy.wait_send)

    load_pat.wait()
    to_pair(
        0, pat.at[:, pl.ds(aligned((1 - core) * 512, 128), HALF)], aa.at[1, pl.ds(ROWS, ROWS)]
    )
    aa[1, pl.ds(0, ROWS), :] = pat[:, pl.ds(aligned(core * 512, 128), HALF)]

    load_wp.wait()

    for i in range(5):
        columns = pl.ds(256 * i, 256)
        res[:, columns] = mm(pat[...], wp[:, columns])
    for i in range(4):
        rows = pl.ds(32 * i, 32)
        values = res[rows, :]
        centred = values - jnp.mean(values, axis=1, keepdims=True)
        inverse = lax.rsqrt(jnp.mean(centred * centred, axis=1, keepdims=True) + 1e-6)
        nlow[rows, :] = (centred * inverse).astype(BF)

    for i in range(10):
        block = pl.ds(128 * i, 128)
        resT[block, :] = res[:, block].T
    mean = jnp.sum(resT[...], axis=0, keepdims=True) * (1.0 / D)
    centred = resT[...] - mean
    inverse = lax.rsqrt(jnp.sum(centred * centred, axis=0, keepdims=True) * (1.0 / D) + 1e-6)

    for i in range(15):
        if i % 5 == 0:
            load_wq[i // 5].wait()
        columns = pl.ds(256 * i, 256)
        tile = mm(nlow[...], wq[:, columns]).astype(BF)
        qkv[:, columns] = tile
        qkvT[columns, :] = tile.T

    exchange_second(0, up, NN)

    load_seg.wait()
    one_hot = (iota((8, ROWS), 0) == seg[...]).astype(F32).astype(BF)
    same_image = mm(one_hot, one_hot, TN) > 0.5

    def forward_heads(g):
        base = g * HALF
        for j in range(8):
            first, width, offset = head_window(j)
            head = pl.ds(aligned(base + 80 * j, 16), 80)
            block = pl.ds(aligned((g * 8 + j) * ROWS, ROWS), ROWS)
            keys = qkv[:, pl.ds(aligned(D + base + first, 128), width)]
            scores = mm(keys, padded(qkvT[head, :], offset, width)) * SCALE
            scores = jnp.where(same_image, scores, -1e30)
            weights = jnp.exp(scores - jnp.max(scores, axis=0, keepdims=True))
            probability = weights / jnp.sum(weights, axis=0, keepdims=True)
            low = probability.astype(BF)
            pT[block, :] = probability
            plT[block, :] = low
            values = qkvT[pl.ds(aligned(2 * D + base + 80 * j, 16), 80), :]
            attT[head, :] = mm(values, low).astype(BF)

    for g in range(2):
        forward_heads(g)

    for i in range(10):
        block = pl.ds(128 * i, 128)
        att[:, block] = attT[block, :].T
    to_pair(
        1, att.at[:, pl.ds(aligned((1 - core) * HALF, 128), HALF)], aa.at[0, pl.ds(ROWS, ROWS)]
    )
    aa[0, pl.ds(0, ROWS), :] = att[:, pl.ds(aligned(core * HALF, 128), HALF)]

    load_wo.wait()
    for i in range(5):
        columns = pl.ds(256 * i, 256)
        sent1[1, :, columns] = (res[:, columns] + mm(att[...], wo[:, columns])).astype(BF)

    arrivals.pop(("deliver", 0))()

    for i in range(10):
        block = pl.ds(128 * i, 128)
        upT[block, :] = up[:, block].T
    to_pair(2, upT, uu.at[0, :, pl.ds(ROWS, ROWS)])
    exchange_first(1)
    uu[0, :, pl.ds(0, ROWS)] = upT[...]

    for i in range(5):
        rows = pl.ds(256 * i, 256)
        gaT[rows, :] = mm(wo[rows, :], upT[...]).astype(BF)

    def by_core(run):
        for c in range(2):
            pl.when(core == c)(lambda c=c: run(c))

    def gradient(grad, index):
        columns = DOT_LANES[index]
        total = mm(uu[grad], aa[grad, :, columns])
        gt[grad, :, :, :, columns] = total.astype(BF).reshape(4, 4, 80, columns.size)

    def first_copy(grad, part, k):
        columns, kind = part
        if kind == 0:
            to = (y + k) % 4
            source, to_llm, to_enc = gt.at[grad, to, :, :, columns], to * 4 + x, enc
        elif kind == 1:
            to = (x + k) % 4
            source, to_llm, to_enc = gt.at[grad, :, to, :, columns], y * 4 + to, enc
        else:
            to = (z + k) % 4
            source, to_llm, to_enc = gt.at[grad, :, to, :, columns], llm, to * 2 + core
        return remote(
            source, r1.at[grad, k - 1, :, :, columns],
            p1_send.at[grad, kind, k - 1], p1_recv.at[grad, kind, k - 1], to_llm, to_enc,
        )

    def second_copy(grad, part, k):
        columns, kind = part
        if kind == 0:
            to = (x + k) % 4
            to_llm = y * 4 + to
        else:
            to = (y + k) % 4
            to_llm = to * 4 + x
        return remote(
            s1.at[grad, to, :, columns], r2.at[grad, k - 1, :, columns],
            p2_send.at[grad, kind, k - 1], p2_recv.at[grad, kind, k - 1], to_llm, enc,
        )

    def cross_copy(grad, part):
        columns, _ = part
        return remote(
            crossing.at[grad, :, columns], s2.at[grad, :, columns],
            p4_send.at[grad], p4_recv.at[grad], y * 4 + z, x * 2 + core,
        )

    def third_copy(grad, k):
        to = (enc + k) % N_ENC
        return remote(
            x3.at[grad, pl.ds(aligned(to * 16, 16), 16)], r3.at[grad, k - 1],
            p3_send.at[grad, k - 1], p3_recv.at[grad, k - 1], llm, to,
        )

    def three(grad, index, copy, act):
        def run(c):
            for k in range(1, 4):
                getattr(copy(grad, PARTS[grad][c][index], k), act)()

        by_core(run)

    def first_phase(grad, index):
        three(grad, index, first_copy, "start")
        arrivals["first", grad, index] = lambda: three(grad, index, first_copy, "wait_recv")
        sends.append(lambda: three(grad, index, first_copy, "wait_send"))

    def second_phase(grad, index):
        arrivals.pop(("first", grad, index))()

        def run(c):
            columns, kind = PARTS[grad][c][index]
            for i in range(4):
                if kind == 0:
                    own = gt[grad, y, i, :, columns]
                else:
                    own = gt[grad, i, x if kind == 1 else z, :, columns]
                total = own.astype(F32)
                for k in range(3):
                    total = total + r1[grad, k, i, :, columns].astype(F32)
                s1[grad, i, :, columns] = total.astype(BF)

        by_core(run)
        three(grad, index, second_copy, "start")
        arrivals["second", grad, index] = lambda: three(grad, index, second_copy, "wait_recv")
        sends.append(lambda: three(grad, index, second_copy, "wait_send"))

    spread_row = iota((ROWS, 80), 0)
    spread = jnp.logical_and(
        iota((ROWS, 80), 1) == spread_row // 16 * 10 + spread_row % 16, spread_row % 16 < 10
    )
    spread = spread.astype(F32).astype(BF)

    def cross(grad, act):
        def run(c):
            getattr(cross_copy(grad, PARTS[grad][c][0]), act)()

        pl.when(x != z)(lambda: by_core(run))

    def third_sum(grad, index):
        arrivals.pop(("second", grad, index))()

        def run(c):
            columns, kind = PARTS[grad][c][index]
            total = s1[grad, x if kind == 0 else y, :, columns].astype(F32)
            for k in range(3):
                total = total + r2[grad, k, :, columns].astype(F32)
            if kind < 2:
                s2[grad, :, columns] = total.astype(BF)
                return

            crossing[grad, :, columns] = total.astype(BF)

            @pl.when(x == z)
            def _():
                s2[grad, :, columns] = crossing[grad, :, columns]

        by_core(run)
        if index == 0:
            cross(grad, "start")
            arrivals["cross", grad] = lambda: cross(grad, "wait_recv")
            sends.append(lambda: cross(grad, "wait_send"))

    def third_phase(grad):
        arrivals.pop(("cross", grad))()
        x3[grad, :, :] = mm(spread, s2[grad]).astype(BF)
        each(1, N_ENC, lambda k: third_copy(grad, k).start())
        arrivals["third", grad] = lambda: each(
            1, N_ENC, lambda k: third_copy(grad, k).wait_recv()
        )
        sends.append(lambda: each(1, N_ENC, lambda k: third_copy(grad, k).wait_send()))

    def last_phase(grad, total, shift):
        arrivals.pop(("third", grad))()
        mine = x3[grad, pl.ds(aligned(enc * 16, 16), 16), :].astype(F32)
        for k in (2, 4, 6):
            mine = mine + r3[grad, k - 1].astype(F32)
        theirs = r3[grad, 0].astype(F32)
        for k in (3, 5, 7):
            theirs = theirs + r3[grad, k - 1].astype(F32)

        def put_halves(c):
            total[:, pl.ds(0, HALF)] = (mine if c == 0 else theirs)[:10, :]
            total[:, pl.ds(shift, HALF)] = (theirs if c == 0 else mine)[:10, :]

        by_core(put_halves)

    @pl.when(core == 0)
    def _():
        s2[1, :, pl.ds(512, 128)] = jnp.zeros((80, 128), BF)

    arrivals.pop(("pair", 1))()
    arrivals.pop(("pair", 2))()
    for index in range(3):
        gradient(0, index)
        first_phase(0, index)

    def backward_heads(g):
        base = g * HALF
        for j in range(8):
            first, width, offset = head_window(j)
            head = pl.ds(aligned(base + 80 * j, 16), 80)
            head_k = pl.ds(aligned(D + base + 80 * j, 16), 80)
            head_v = pl.ds(aligned(2 * D + base + 80 * j, 16), 80)
            block = pl.ds(aligned((g * 8 + j) * ROWS, ROWS), ROWS)
            values = qkv[:, pl.ds(aligned(2 * D + base + first, 128), width)]
            rows = gaT[head, :]
            grad_prob = mm(values, padded(rows, offset, width))
            probability = pT[block, :]
            weighted = jnp.sum(grad_prob * probability, axis=0, keepdims=True)
            low = (probability * (grad_prob - weighted) * SCALE).astype(BF)
            gqkvT[head, :] = mm(qkvT[head_k, :], low).astype(BF)
            gqkvT[head_k, :] = mm(qkvT[head, :], low, NT).astype(BF)
            gqkvT[head_v, :] = mm(rows, plT[block, :], NT).astype(BF)

    for g in range(2):
        backward_heads(g)


    mean_grad = jnp.zeros((1, ROWS), F32)
    mean_cross = jnp.zeros((1, ROWS), F32)
    for i in range(5):
        rows = pl.ds(256 * i, 256)
        tile = mm(wq[rows, :], gqkvT[...])
        gnT[rows, :] = tile
        normed = (resT[rows, :] - mean) * inverse
        mean_grad = mean_grad + jnp.sum(tile, axis=0, keepdims=True)
        mean_cross = mean_cross + jnp.sum(tile * normed, axis=0, keepdims=True)
    exchange_second(1, emb_in, TN)
    mean_grad = mean_grad * (1.0 / D)
    mean_cross = mean_cross * (1.0 / D)

    for i in range(5):
        rows = pl.ds(256 * i, 256)
        normed = (resT[rows, :] - mean) * inverse
        total = upT[rows, :].astype(F32) + inverse * (
            gnT[rows, :] - mean_grad - normed * mean_cross
        )
        uu[1, rows, pl.ds(0, ROWS)] = total.astype(BF)
    to_pair(3, uu.at[1, :, pl.ds(0, ROWS)], uu.at[1, :, pl.ds(ROWS, ROWS)])
    second_phase(0, 1)
    second_phase(0, 2)
    arrivals.pop(("pair", 0))()
    arrivals.pop(("pair", 3))()
    for index in range(3):
        gradient(1, index)
        first_phase(1, index)

    third_sum(0, 1)
    third_sum(0, 2)

    arrivals.pop(("deliver", 1))()
    load_text.wait()
    position = iota((SEQ, ROWS), 0)
    put = (position == iota((SEQ, ROWS), 1) + start).astype(F32).astype(BF)

    place = iota((SEQ, 256), 0)
    inside = jnp.logical_and(place >= start, place < start + ROWS)
    for i in range(5):
        columns = pl.ds(256 * i, 256)
        placed = mm(put, emb_in[:, columns])
        merged[:, columns] = jnp.where(inside, placed, text[:, columns].astype(F32)).astype(BF)
    store_merged = local(merged, merged_hbm, 9)
    store_merged.start()
    second_phase(0, 0)
    second_phase(1, 0)
    second_phase(1, 1)
    second_phase(1, 2)
    third_sum(0, 0)
    third_sum(1, 0)
    third_phase(0)
    third_sum(1, 1)
    third_sum(1, 2)
    third_phase(1)
    last_phase(0, gout, HALF)
    store_gout = local(gout, gout_hbm, 10)
    store_gout.start()
    last_phase(1, gpatch, 512)
    store_gpatch = local(gpatch, gpatch_hbm, 11)
    store_gpatch.start()

    for sent in sends:
        sent()
    store_merged.wait()
    store_gout.wait()
    store_gpatch.wait()


def finish_kernel(a, b, c, a_out, b_out, c_out):
    a_out[...] = a[...]
    b_out[...] = b[...]
    c_out[...] = c[...]


def shards(
    patches, image_seg, owner_slot, place_start, text_embeds, merged_grad, w_patch, w_qkv, w_out
):
    anywhere = pl.BlockSpec(memory_space=pl.ANY)
    vmem = pl.BlockSpec(memory_space=pltpu.VMEM)
    dma = pltpu.SemaphoreType.DMA
    merged, grad_patch, grad_out = pl.pallas_call(
        kernel,
        out_shape=(
            jax.ShapeDtypeStruct((SEQ, D), BF),
            jax.ShapeDtypeStruct((10, PIN), F32),
            jax.ShapeDtypeStruct((10, D), F32),
        ),
        in_specs=[anywhere] * 9,
        out_specs=(anywhere, anywhere, anywhere),
        scratch_shapes=[
            pltpu.SMEM((1, ROWS), jnp.int32),
            pltpu.SMEM((1, 1), jnp.int32),
            pltpu.VMEM((1, ROWS), jnp.int32),
            pltpu.VMEM((ROWS, PIN), BF),
            pltpu.VMEM((SEQ, D), BF),
            pltpu.VMEM((SEQ, D), BF),
            pltpu.VMEM((PIN, D), BF),
            pltpu.VMEM((D, 3 * D), BF),
            pltpu.VMEM((D, D), BF),
            pltpu.VMEM((256, 256), BF),
            pltpu.VMEM((2, ROWS, D), BF),
            pltpu.VMEM((2, 256, HALF), BF),
            pltpu.VMEM((2, 256, HALF), BF),
            pltpu.VMEM((ROWS, D), BF),
            pltpu.VMEM((ROWS, D), BF),
            pltpu.VMEM((ROWS, D), F32),
            pltpu.VMEM((ROWS, D), BF),
            pltpu.VMEM((D, ROWS), F32),
            pltpu.VMEM((ROWS, 3 * D), BF),
            pltpu.VMEM((3 * D, ROWS), BF),
            pltpu.VMEM((HEADS * ROWS, ROWS), F32),
            pltpu.VMEM((HEADS * ROWS, ROWS), BF),
            pltpu.VMEM((D, ROWS), BF),
            pltpu.VMEM((ROWS, D), BF),
            pltpu.VMEM((D, ROWS), BF),
            pltpu.VMEM((D, ROWS), BF),
            pltpu.VMEM((3 * D, ROWS), BF),
            pltpu.VMEM((D, ROWS), F32),
            pltpu.VMEM((SEQ, D), BF),
            pltpu.VMEM((10, PIN), F32),
            pltpu.VMEM((10, D), F32),
            pltpu.VMEM((2, D, 2 * ROWS), BF),
            pltpu.VMEM((2, 2 * ROWS, HALF), BF),
            pltpu.VMEM((2, 4, 4, 80, HALF), BF),
            pltpu.VMEM((2, 3, 4, 80, HALF), BF),
            pltpu.VMEM((2, 4, 80, HALF), BF),
            pltpu.VMEM((2, 3, 80, HALF), BF),
            pltpu.VMEM((2, 80, HALF), BF),
            pltpu.VMEM((2, 80, HALF), BF),
            pltpu.VMEM((2, ROWS, HALF), BF),
            pltpu.VMEM((2, 7, 16, HALF), BF),
            dma((14,)),
            dma((2, 2, N_LLM)),
            dma((2, 2, N_LLM)),
            dma((4,)),
            dma((4,)),
            dma((2, 3, 3)),
            dma((2, 3, 3)),
            dma((2, 3, 3)),
            dma((2, 3, 3)),
            dma((2, 7)),
            dma((2, 7)),
            dma((2,)),
            dma((2,)),
        ],
        compiler_params=pltpu.CompilerParams(
            collective_id=0, has_side_effects=True, vmem_limit_bytes=56 * 1024 * 1024
        ),
    )(
        owner_slot.reshape(1, 128), place_start, image_seg, patches, text_embeds, merged_grad,
        w_patch, w_qkv, w_out,
    )
    merged, grad_patch, grad_out = pl.pallas_call(
        finish_kernel,
        out_shape=(
            jax.ShapeDtypeStruct((SEQ, D), BF),
            jax.ShapeDtypeStruct((10, PIN), F32),
            jax.ShapeDtypeStruct((10, D), F32),
        ),
        in_specs=[vmem] * 3,
        out_specs=(vmem, vmem, vmem),
    )(merged, grad_patch, grad_out)
    return (merged, grad_patch.T, grad_out.T)


def solution(mesh):
    rows = P(("llm", "enc"), None)
    columns = P(None, ("llm", "enc"))
    return jax.shard_map(
        shards,
        mesh=mesh,
        in_specs=(rows, P(), P(), rows, rows, rows, P(), P(), P()),
        out_specs=(rows, columns, columns),
        check_vma=False,
    )
```

```python
import jax
import jax.numpy as jnp
from jax import lax
from jax.experimental import pallas as pl
from jax.experimental.pallas import tpu as pltpu
from jax.sharding import PartitionSpec as P

D = 1280
HEADS = 16
HEAD_DIM = 80
PIN = 1152
ROWS = 128
SEQ = 160
N_LLM = 16
N_ENC = 8
HALF = 640
SCALE = HEAD_DIM ** (-0.5)

OUT_PARTS = (
    ((pl.ds(384, 256), 2), (pl.ds(0, 256), 0), (pl.ds(256, 128), 1)),
    ((pl.ds(384, 256), 3), (pl.ds(0, 128), 0), (pl.ds(128, 256), 1)),
)
PATCH_PARTS = (
    ((pl.ds(384, 128), 2), (pl.ds(0, 256), 0), (pl.ds(256, 128), 1)),
    ((pl.ds(384, 256), 3), (pl.ds(0, 128), 0), (pl.ds(128, 256), 1)),
)
PARTS = (OUT_PARTS, PATCH_PARTS)
DOT_LANES = (pl.ds(384, 256), pl.ds(0, 256), pl.ds(256, 128))

BF = jnp.bfloat16
F32 = jnp.float32
MESH = pl.DeviceIdType.MESH
NN = (((1,), (0,)), ((), ()))
NT = (((1,), (1,)), ((), ()))
TN = (((0,), (0,)), ((), ()))


def mm(a, b, dims=NN):
    return lax.dot_general(a, b, dims, preferred_element_type=F32)


def iota(shape, axis):
    return lax.broadcasted_iota(jnp.int32, shape, axis)


def aligned(value, unit):
    return value if isinstance(value, int) else pl.multiple_of(value, unit)


def each(low, high, body):
    for i in range(low, high):
        body(i)


def head_window(j):
    first = 80 * j // 128 * 128
    last = -(-(80 * j + 80) // 128) * 128
    return first, last - first, 80 * j - first


def padded(rows, offset, width):
    pieces = []
    if offset:
        pieces.append(jnp.zeros((offset, ROWS), BF))
    pieces.append(rows)
    if width - offset - 80:
        pieces.append(jnp.zeros((width - offset - 80, ROWS), BF))
    return jnp.concatenate(pieces, axis=0)


def kernel(
    owner_hbm, start_hbm, seg_hbm, patches_hbm, text_hbm, mgrad_hbm, wp_hbm, wq_hbm, wo_hbm,
    merged_hbm, gpatch_hbm, gout_hbm,
    owner, first_row, seg, pat, text, mgrad, wp, wq, wo,
    perm, sent1, recv1, sent2, emb_in, up, res, nlow, resT, qkv, qkvT, pT, probs, attT, att,
    upT, gaT, gqkvT, gnT, merged, gpatch, gout, uu, aa, gt, r1, s1, r2, crossing, s2, x3, r3,
    local_sem, ex_send, ex_recv, pair_send, pair_recv, p1_send, p1_recv, p2_send, p2_recv,
    p3_send, p3_recv, p4_send, p4_recv,
):
    llm = lax.axis_index("llm")
    enc = lax.axis_index("enc")
    y, x = llm // 4, llm % 4
    z, core = enc // 2, enc % 2
    device = llm * N_ENC + enc
    arrivals, sends = {}, []

    def local(source, target, slot):
        return pltpu.make_async_copy(source, target, local_sem.at[slot])

    def remote(source, target, send, recv, to_llm, to_enc):
        return pltpu.make_async_remote_copy(
            src_ref=source, dst_ref=target, send_sem=send, recv_sem=recv,
            device_id=(to_llm, to_enc), device_id_type=MESH,
        )

    load_owner = local(owner_hbm, owner, 12)
    load_start = local(start_hbm, first_row, 13)
    load_mgrad = local(mgrad_hbm, mgrad, 0)
    load_pat = local(patches_hbm, pat, 1)
    load_seg = local(seg_hbm.at[device], seg, 2)
    load_wp = local(wp_hbm, wp, 3)
    load_wq = [
        local(wq_hbm.at[:, pl.ds(D * i, D)], wq.at[:, pl.ds(D * i, D)], 4 + i) for i in range(3)
    ]
    load_wo = local(wo_hbm, wo, 7)
    load_text = local(text_hbm, text, 8)
    for load in (load_owner, load_start, load_mgrad, load_pat, load_seg, load_wp, *load_wq, load_wo, load_text):
        load.start()

    barrier = pltpu.get_barrier_semaphore()

    def greet_llm(k):
        pl.semaphore_signal(
            barrier, inc=1, device_id=((llm + k) % N_LLM, enc), device_id_type=MESH
        )

    def greet_enc(k):
        pl.semaphore_signal(
            barrier, inc=1, device_id=(llm, (enc + k) % N_ENC), device_id_type=MESH
        )

    each(1, N_LLM, greet_llm)
    each(1, N_ENC, greet_enc)

    turned = jnp.where(core == 0, x, y)
    mate_llm, mate_enc = jnp.where(core == 0, y * 4 + z, z * 4 + x), turned * 2 + core

    @pl.when(turned != z)
    def _():
        pl.semaphore_signal(
            barrier, inc=1, device_id=(mate_llm, mate_enc), device_id_type=MESH
        )

    load_owner.wait()
    load_start.wait()
    start = first_row[0, 0]
    lane = iota((16, 256), 1)
    row = iota((16, 256), 0)

    def owner_rows(s):
        rank = owner[0, s * N_ENC + enc]
        hit = (lane == rank * 16 + row).astype(F32)
        perm[pl.ds(aligned(s * 16, 16), 16), :] = hit.astype(BF)

    each(0, N_LLM, owner_rows)

    load_mgrad.wait()
    take = (iota((ROWS, SEQ), 1) == iota((ROWS, SEQ), 0) + start).astype(F32).astype(BF)
    sent1[0, :, :] = mm(take, mgrad[...]).astype(BF)

    pl.semaphore_wait(barrier, N_LLM - 1 + N_ENC - 1 + (turned != z).astype(jnp.int32))

    def piece(ref, j):
        return ref.at[pl.ds(aligned(j // 2 * 16, 16), 16), pl.ds(aligned(j % 2 * HALF, 128), HALF)]

    def scatter(way, k):
        to = (llm + k) % N_LLM
        return remote(
            piece(sent1.at[way], to), recv1.at[way, pl.ds(aligned(llm * 16, 16), 16)],
            ex_send.at[way, 0, k], ex_recv.at[way, 0, k], to, enc,
        )

    def scatter_arrival(way, k):
        source = (llm + N_LLM - k) % N_LLM
        return remote(
            piece(sent1.at[way], llm), recv1.at[way, pl.ds(aligned(source * 16, 16), 16)],
            ex_send.at[way, 0, k], ex_recv.at[way, 0, k], (llm + k) % N_LLM, enc,
        )

    def deliver(way, target, k):
        to = (llm + k) % N_LLM
        return remote(
            sent2.at[way, pl.ds(aligned(to * 16, 16), 16)], piece(target, llm),
            ex_send.at[way, 1, k], ex_recv.at[way, 1, k], to, enc,
        )

    def deliver_arrival(way, target, k):
        source = (llm + N_LLM - k) % N_LLM
        return remote(
            sent2.at[way, pl.ds(aligned(llm * 16, 16), 16)], piece(target, source),
            ex_send.at[way, 1, k], ex_recv.at[way, 1, k], (llm + k) % N_LLM, enc,
        )

    def own_piece(ref):
        return ref[pl.ds(aligned(llm // 2 * 16, 16), 16), pl.ds(aligned(llm % 2 * HALF, 128), HALF)]

    def exchange_first(way):
        each(1, N_LLM, lambda k: scatter(way, k).start())
        arrivals["scatter", way] = lambda: each(
            1, N_LLM, lambda k: scatter_arrival(way, k).wait_recv()
        )
        sends.append(lambda: each(1, N_LLM, lambda k: scatter(way, k).wait_send()))
        recv1[way, pl.ds(aligned(llm * 16, 16), 16), :] = own_piece(sent1.at[way])

    def exchange_second(way, target, dims):
        arrivals.pop(("scatter", way))()
        sent2[way, :, :] = mm(perm[...], recv1[way], dims).astype(BF)
        each(1, N_LLM, lambda k: deliver(way, target, k).start())
        arrivals["deliver", way] = lambda: each(
            1, N_LLM, lambda k: deliver_arrival(way, target, k).wait_recv()
        )
        sends.append(lambda: each(1, N_LLM, lambda k: deliver(way, target, k).wait_send()))
        target[pl.ds(aligned(llm // 2 * 16, 16), 16), pl.ds(aligned(llm % 2 * HALF, 128), HALF)] = (
            sent2[way, pl.ds(aligned(llm * 16, 16), 16), :]
        )

    exchange_first(0)
    other = enc + 1 - 2 * core

    def to_pair(slot, source, target):
        copy = remote(source, target, pair_send.at[slot], pair_recv.at[slot], llm, other)
        copy.start()
        arrivals["pair", slot] = copy.wait_recv
        sends.append(copy.wait_send)

    load_pat.wait()
    to_pair(
        0, pat.at[:, pl.ds(aligned((1 - core) * 512, 128), HALF)], aa.at[1, pl.ds(ROWS, ROWS)]
    )
    aa[1, pl.ds(0, ROWS), :] = pat[:, pl.ds(aligned(core * 512, 128), HALF)]

    load_wp.wait()

    for i in range(5):
        columns = pl.ds(256 * i, 256)
        res[:, columns] = mm(pat[...], wp[:, columns])
    for i in range(4):
        rows = pl.ds(32 * i, 32)
        values = res[rows, :]
        centred = values - jnp.mean(values, axis=1, keepdims=True)
        inverse = lax.rsqrt(jnp.mean(centred * centred, axis=1, keepdims=True) + 1e-6)
        nlow[rows, :] = (centred * inverse).astype(BF)

    for i in range(10):
        block = pl.ds(128 * i, 128)
        resT[block, :] = res[:, block].T
    mean = jnp.sum(resT[...], axis=0, keepdims=True) * (1.0 / D)
    centred = resT[...] - mean
    inverse = lax.rsqrt(jnp.sum(centred * centred, axis=0, keepdims=True) * (1.0 / D) + 1e-6)

    for i in range(15):
        if i % 5 == 0:
            load_wq[i // 5].wait()
        columns = pl.ds(256 * i, 256)
        tile = mm(nlow[...], wq[:, columns]).astype(BF)
        qkv[:, columns] = tile
        qkvT[columns, :] = tile.T

    exchange_second(0, up, NN)

    load_seg.wait()
    one_hot = (iota((8, ROWS), 0) == seg[...]).astype(F32).astype(BF)
    same_image = mm(one_hot, one_hot, TN) > 0.5

    def forward_heads(g):
        base = g * HALF
        for j in range(8):
            first, width, offset = head_window(j)
            head = pl.ds(aligned(base + 80 * j, 16), 80)
            block = pl.ds(aligned((g * 8 + j) * ROWS, ROWS), ROWS)
            keys = qkv[:, pl.ds(aligned(D + base + first, 128), width)]
            scores = mm(keys, padded(qkvT[head, :], offset, width)) * SCALE
            scores = jnp.where(same_image, scores, -1e30)
            weights = jnp.exp(scores - jnp.max(scores, axis=0, keepdims=True))
            probability = weights / jnp.sum(weights, axis=0, keepdims=True)
            low = probability.astype(BF)
            pT[block, :] = probability
            probs[block, :] = low.T
            values = qkvT[pl.ds(aligned(2 * D + base + 80 * j, 16), 80), :]
            attT[head, :] = mm(values, low).astype(BF)

    for g in range(2):
        forward_heads(g)

    for i in range(10):
        block = pl.ds(128 * i, 128)
        att[:, block] = attT[block, :].T
    to_pair(
        1, att.at[:, pl.ds(aligned((1 - core) * HALF, 128), HALF)], aa.at[0, pl.ds(ROWS, ROWS)]
    )
    aa[0, pl.ds(0, ROWS), :] = att[:, pl.ds(aligned(core * HALF, 128), HALF)]

    load_wo.wait()
    for i in range(5):
        columns = pl.ds(256 * i, 256)
        sent1[1, :, columns] = (res[:, columns] + mm(att[...], wo[:, columns])).astype(BF)

    arrivals.pop(("deliver", 0))()

    for i in range(10):
        block = pl.ds(128 * i, 128)
        upT[block, :] = up[:, block].T
    to_pair(2, upT, uu.at[0, :, pl.ds(ROWS, ROWS)])
    exchange_first(1)
    uu[0, :, pl.ds(0, ROWS)] = upT[...]

    for i in range(5):
        rows = pl.ds(256 * i, 256)
        gaT[rows, :] = mm(wo[rows, :], upT[...]).astype(BF)

    def by_core(run):
        for c in range(2):
            pl.when(core == c)(lambda c=c: run(c))

    def gradient(grad, index):
        columns = DOT_LANES[index]
        total = mm(uu[grad], aa[grad, :, columns])
        gt[grad, :, :, :, columns] = total.astype(BF).reshape(4, 4, 80, columns.size)

    def first_copy(grad, part, k):
        columns, kind = part
        if kind == 0:
            to = (y + k) % 4
            source, to_llm, to_enc = gt.at[grad, to, :, :, columns], to * 4 + x, enc
        elif kind == 1:
            to = (x + k) % 4
            source, to_llm, to_enc = gt.at[grad, :, to, :, columns], y * 4 + to, enc
        else:
            to = (z + k) % 4
            source = gt.at[grad, :, to, :, columns] if kind == 2 else gt.at[grad, to, :, :, columns]
            to_llm, to_enc = llm, to * 2 + core
        return remote(
            source, r1.at[grad, k - 1, :, :, columns],
            p1_send.at[grad, min(kind, 2), k - 1], p1_recv.at[grad, min(kind, 2), k - 1], to_llm, to_enc,
        )

    def second_copy(grad, part, k):
        columns, kind = part
        if kind in (0, 3):
            to = (x + k) % 4
            to_llm = y * 4 + to
        else:
            to = (y + k) % 4
            to_llm = to * 4 + x
        return remote(
            s1.at[grad, to, :, columns], r2.at[grad, k - 1, :, columns],
            p2_send.at[grad, min(kind, 2), k - 1], p2_recv.at[grad, min(kind, 2), k - 1], to_llm, enc,
        )

    def cross_copy(grad, part):
        columns, _ = part
        return remote(
            crossing.at[grad, :, columns], s2.at[grad, :, columns],
            p4_send.at[grad], p4_recv.at[grad], mate_llm, mate_enc,
        )

    def third_copy(grad, k):
        to = (enc + k) % N_ENC
        return remote(
            x3.at[grad, pl.ds(aligned(to * 16, 16), 16)], r3.at[grad, k - 1],
            p3_send.at[grad, k - 1], p3_recv.at[grad, k - 1], llm, to,
        )

    def three(grad, index, copy, act):
        def run(c):
            for k in range(1, 4):
                getattr(copy(grad, PARTS[grad][c][index], k), act)()

        by_core(run)

    def first_phase(grad, index):
        three(grad, index, first_copy, "start")
        arrivals["first", grad, index] = lambda: three(grad, index, first_copy, "wait_recv")
        sends.append(lambda: three(grad, index, first_copy, "wait_send"))

    def second_phase(grad, index):
        arrivals.pop(("first", grad, index))()

        def run(c):
            columns, kind = PARTS[grad][c][index]
            for i in range(4):
                if kind in (0, 3):
                    own = gt[grad, z if kind else y, i, :, columns]
                else:
                    own = gt[grad, i, x if kind == 1 else z, :, columns]
                total = own.astype(F32)
                for k in range(3):
                    total = total + r1[grad, k, i, :, columns].astype(F32)
                s1[grad, i, :, columns] = total.astype(BF)

        by_core(run)
        three(grad, index, second_copy, "start")
        arrivals["second", grad, index] = lambda: three(grad, index, second_copy, "wait_recv")
        sends.append(lambda: three(grad, index, second_copy, "wait_send"))

    spread_row = iota((ROWS, 80), 0)
    spread = jnp.logical_and(
        iota((ROWS, 80), 1) == spread_row // 16 * 10 + spread_row % 16, spread_row % 16 < 10
    )
    spread = spread.astype(F32).astype(BF)

    def cross(grad, act):
        def run(c):
            getattr(cross_copy(grad, PARTS[grad][c][0]), act)()

        pl.when(turned != z)(lambda: by_core(run))

    def third_sum(grad, index):
        arrivals.pop(("second", grad, index))()

        def run(c):
            columns, kind = PARTS[grad][c][index]
            total = s1[grad, x if kind in (0, 3) else y, :, columns].astype(F32)
            for k in range(3):
                total = total + r2[grad, k, :, columns].astype(F32)
            if kind < 2:
                s2[grad, :, columns] = total.astype(BF)
                return

            crossing[grad, :, columns] = total.astype(BF)

            @pl.when(turned == z)
            def _():
                s2[grad, :, columns] = crossing[grad, :, columns]

        by_core(run)
        if index == 0:
            cross(grad, "start")
            arrivals["cross", grad] = lambda: cross(grad, "wait_recv")
            sends.append(lambda: cross(grad, "wait_send"))

    def third_phase(grad):
        arrivals.pop(("cross", grad))()
        x3[grad, :, :] = mm(spread, s2[grad]).astype(BF)
        each(1, N_ENC, lambda k: third_copy(grad, k).start())
        arrivals["third", grad] = lambda: each(
            1, N_ENC, lambda k: third_copy(grad, k).wait_recv()
        )
        sends.append(lambda: each(1, N_ENC, lambda k: third_copy(grad, k).wait_send()))

    def last_phase(grad, total, shift):
        arrivals.pop(("third", grad))()
        mine = x3[grad, pl.ds(aligned(enc * 16, 16), 16), :].astype(F32)
        for k in (2, 4, 6):
            mine = mine + r3[grad, k - 1].astype(F32)
        theirs = r3[grad, 0].astype(F32)
        for k in (3, 5, 7):
            theirs = theirs + r3[grad, k - 1].astype(F32)

        def put_halves(c):
            total[:, pl.ds(0, HALF)] = (mine if c == 0 else theirs)[:10, :]
            total[:, pl.ds(shift, HALF)] = (theirs if c == 0 else mine)[:10, :]

        by_core(put_halves)

    @pl.when(core == 0)
    def _():
        s2[1, :, pl.ds(512, 128)] = jnp.zeros((80, 128), BF)

    arrivals.pop(("pair", 1))()
    arrivals.pop(("pair", 2))()
    for index in range(3):
        gradient(0, index)
        first_phase(0, index)

    def backward_heads(g):
        base = g * HALF
        for j in range(8):
            first, width, offset = head_window(j)
            head = pl.ds(aligned(base + 80 * j, 16), 80)
            head_k = pl.ds(aligned(D + base + 80 * j, 16), 80)
            head_v = pl.ds(aligned(2 * D + base + 80 * j, 16), 80)
            block = pl.ds(aligned((g * 8 + j) * ROWS, ROWS), ROWS)
            values = qkv[:, pl.ds(aligned(2 * D + base + first, 128), width)]
            rows = gaT[head, :]
            grad_prob = mm(values, padded(rows, offset, width))
            probability = pT[block, :]
            weighted = jnp.sum(grad_prob * probability, axis=0, keepdims=True)
            low = (probability * (grad_prob - weighted) * SCALE).astype(BF)
            gqkvT[head, :] = mm(qkvT[head_k, :], low).astype(BF)
            gqkvT[head_k, :] = mm(qkvT[head, :], low, NT).astype(BF)
            gqkvT[head_v, :] = mm(rows, probs[block, :]).astype(BF)

    for g in range(2):
        backward_heads(g)


    mean_grad = jnp.zeros((1, ROWS), F32)
    mean_cross = jnp.zeros((1, ROWS), F32)
    for i in range(5):
        rows = pl.ds(256 * i, 256)
        tile = mm(wq[rows, :], gqkvT[...])
        gnT[rows, :] = tile
        normed = (resT[rows, :] - mean) * inverse
        mean_grad = mean_grad + jnp.sum(tile, axis=0, keepdims=True)
        mean_cross = mean_cross + jnp.sum(tile * normed, axis=0, keepdims=True)
    exchange_second(1, emb_in, TN)
    mean_grad = mean_grad * (1.0 / D)
    mean_cross = mean_cross * (1.0 / D)

    for i in range(5):
        rows = pl.ds(256 * i, 256)
        normed = (resT[rows, :] - mean) * inverse
        total = upT[rows, :].astype(F32) + inverse * (
            gnT[rows, :] - mean_grad - normed * mean_cross
        )
        uu[1, rows, pl.ds(0, ROWS)] = total.astype(BF)
    to_pair(3, uu.at[1, :, pl.ds(0, ROWS)], uu.at[1, :, pl.ds(ROWS, ROWS)])
    second_phase(0, 1)
    second_phase(0, 2)
    arrivals.pop(("pair", 0))()
    arrivals.pop(("pair", 3))()
    for index in range(3):
        gradient(1, index)
        first_phase(1, index)

    third_sum(0, 1)
    third_sum(0, 2)

    arrivals.pop(("deliver", 1))()
    load_text.wait()
    position = iota((SEQ, ROWS), 0)
    put = (position == iota((SEQ, ROWS), 1) + start).astype(F32).astype(BF)

    place = iota((SEQ, 256), 0)
    inside = jnp.logical_and(place >= start, place < start + ROWS)
    for i in range(5):
        columns = pl.ds(256 * i, 256)
        placed = mm(put, emb_in[:, columns])
        merged[:, columns] = jnp.where(inside, placed, text[:, columns].astype(F32)).astype(BF)
    store_merged = local(merged, merged_hbm, 9)
    store_merged.start()
    second_phase(0, 0)
    second_phase(1, 0)
    second_phase(1, 1)
    second_phase(1, 2)
    third_sum(0, 0)
    third_sum(1, 0)
    third_phase(0)
    third_sum(1, 1)
    third_sum(1, 2)
    third_phase(1)
    last_phase(0, gout, HALF)
    store_gout = local(gout, gout_hbm, 10)
    store_gout.start()
    last_phase(1, gpatch, 512)
    store_gpatch = local(gpatch, gpatch_hbm, 11)
    store_gpatch.start()

    for sent in sends:
        sent()
    store_merged.wait()
    store_gout.wait()
    store_gpatch.wait()


def finish_kernel(a, b, c, a_out, b_out, c_out):
    a_out[...] = a[...]
    b_out[...] = b[...]
    c_out[...] = c[...]


def shards(
    patches, image_seg, owner_slot, place_start, text_embeds, merged_grad, w_patch, w_qkv, w_out
):
    anywhere = pl.BlockSpec(memory_space=pl.ANY)
    vmem = pl.BlockSpec(memory_space=pltpu.VMEM)
    dma = pltpu.SemaphoreType.DMA
    merged, grad_patch, grad_out = pl.pallas_call(
        kernel,
        out_shape=(
            jax.ShapeDtypeStruct((SEQ, D), BF),
            jax.ShapeDtypeStruct((10, PIN), F32),
            jax.ShapeDtypeStruct((10, D), F32),
        ),
        in_specs=[anywhere] * 9,
        out_specs=(anywhere, anywhere, anywhere),
        scratch_shapes=[
            pltpu.SMEM((1, ROWS), jnp.int32),
            pltpu.SMEM((1, 1), jnp.int32),
            pltpu.VMEM((1, ROWS), jnp.int32),
            pltpu.VMEM((ROWS, PIN), BF),
            pltpu.VMEM((SEQ, D), BF),
            pltpu.VMEM((SEQ, D), BF),
            pltpu.VMEM((PIN, D), BF),
            pltpu.VMEM((D, 3 * D), BF),
            pltpu.VMEM((D, D), BF),
            pltpu.VMEM((256, 256), BF),
            pltpu.VMEM((2, ROWS, D), BF),
            pltpu.VMEM((2, 256, HALF), BF),
            pltpu.VMEM((2, 256, HALF), BF),
            pltpu.VMEM((ROWS, D), BF),
            pltpu.VMEM((ROWS, D), BF),
            pltpu.VMEM((ROWS, D), F32),
            pltpu.VMEM((ROWS, D), BF),
            pltpu.VMEM((D, ROWS), F32),
            pltpu.VMEM((ROWS, 3 * D), BF),
            pltpu.VMEM((3 * D, ROWS), BF),
            pltpu.VMEM((HEADS * ROWS, ROWS), F32),
            pltpu.VMEM((HEADS * ROWS, ROWS), BF),
            pltpu.VMEM((D, ROWS), BF),
            pltpu.VMEM((ROWS, D), BF),
            pltpu.VMEM((D, ROWS), BF),
            pltpu.VMEM((D, ROWS), BF),
            pltpu.VMEM((3 * D, ROWS), BF),
            pltpu.VMEM((D, ROWS), F32),
            pltpu.VMEM((SEQ, D), BF),
            pltpu.VMEM((10, PIN), F32),
            pltpu.VMEM((10, D), F32),
            pltpu.VMEM((2, D, 2 * ROWS), BF),
            pltpu.VMEM((2, 2 * ROWS, HALF), BF),
            pltpu.VMEM((2, 4, 4, 80, HALF), BF),
            pltpu.VMEM((2, 3, 4, 80, HALF), BF),
            pltpu.VMEM((2, 4, 80, HALF), BF),
            pltpu.VMEM((2, 3, 80, HALF), BF),
            pltpu.VMEM((2, 80, HALF), BF),
            pltpu.VMEM((2, 80, HALF), BF),
            pltpu.VMEM((2, ROWS, HALF), BF),
            pltpu.VMEM((2, 7, 16, HALF), BF),
            dma((14,)),
            dma((2, 2, N_LLM)),
            dma((2, 2, N_LLM)),
            dma((4,)),
            dma((4,)),
            dma((2, 3, 3)),
            dma((2, 3, 3)),
            dma((2, 3, 3)),
            dma((2, 3, 3)),
            dma((2, 7)),
            dma((2, 7)),
            dma((2,)),
            dma((2,)),
        ],
        compiler_params=pltpu.CompilerParams(
            collective_id=0, has_side_effects=True, vmem_limit_bytes=56 * 1024 * 1024
        ),
    )(
        owner_slot.reshape(1, 128), place_start, image_seg, patches, text_embeds, merged_grad,
        w_patch, w_qkv, w_out,
    )
    merged, grad_patch, grad_out = pl.pallas_call(
        finish_kernel,
        out_shape=(
            jax.ShapeDtypeStruct((SEQ, D), BF),
            jax.ShapeDtypeStruct((10, PIN), F32),
            jax.ShapeDtypeStruct((10, D), F32),
        ),
        in_specs=[vmem] * 3,
        out_specs=(vmem, vmem, vmem),
    )(merged, grad_patch, grad_out)
    return (merged, grad_patch.T, grad_out.T)


def solution(mesh):
    rows = P(("llm", "enc"), None)
    columns = P(None, ("llm", "enc"))
    return jax.shard_map(
        shards,
        mesh=mesh,
        in_specs=(rows, P(), P(), rows, rows, rows, P(), P(), P()),
        out_specs=(rows, columns, columns),
        check_vma=False,
    )
```

```python
import jax
import jax.numpy as jnp
from jax import lax
from jax.experimental import pallas as pl
from jax.experimental.pallas import tpu as pltpu
from jax.sharding import PartitionSpec as P

D = 1280
HEADS = 16
HEAD_DIM = 80
PIN = 1152
ROWS = 128
SEQ = 160
N_LLM = 16
N_ENC = 8
HALF = 640
SCALE = HEAD_DIM ** (-0.5)

OUT_PARTS = (
    ((pl.ds(384, 256), 2), (pl.ds(0, 256), 0), (pl.ds(256, 128), 1)),
    ((pl.ds(384, 256), 3), (pl.ds(0, 128), 0), (pl.ds(128, 256), 1)),
)
PATCH_PARTS = (
    ((pl.ds(384, 128), 2), (pl.ds(0, 256), 0), (pl.ds(256, 128), 1)),
    ((pl.ds(384, 256), 3), (pl.ds(0, 128), 0), (pl.ds(128, 256), 1)),
)
PARTS = (OUT_PARTS, PATCH_PARTS)
PEERS = (10, 6, 9, 11, 14, 2, 5, 7, 8, 13, 15, 1, 3, 4, 12)
DOT_LANES = (pl.ds(384, 256), pl.ds(0, 256), pl.ds(256, 128))

BF = jnp.bfloat16
F32 = jnp.float32
MESH = pl.DeviceIdType.MESH
NN = (((1,), (0,)), ((), ()))
NT = (((1,), (1,)), ((), ()))
TN = (((0,), (0,)), ((), ()))


def mm(a, b, dims=NN):
    return lax.dot_general(a, b, dims, preferred_element_type=F32)


def iota(shape, axis):
    return lax.broadcasted_iota(jnp.int32, shape, axis)


def aligned(value, unit):
    return value if isinstance(value, int) else pl.multiple_of(value, unit)


def each(low, high, body):
    for i in range(low, high):
        body(i)


def each_peer(body):
    for k in PEERS:
        body(k)


def head_window(j):
    first = 80 * j // 128 * 128
    last = -(-(80 * j + 80) // 128) * 128
    return first, last - first, 80 * j - first


def padded(rows, offset, width):
    pieces = []
    if offset:
        pieces.append(jnp.zeros((offset, ROWS), BF))
    pieces.append(rows)
    if width - offset - 80:
        pieces.append(jnp.zeros((width - offset - 80, ROWS), BF))
    return jnp.concatenate(pieces, axis=0)


def kernel(
    owner_hbm, start_hbm, seg_hbm, patches_hbm, text_hbm, mgrad_hbm, wp_hbm, wq_hbm, wo_hbm,
    merged_hbm, gpatch_hbm, gout_hbm,
    owner, first_row, seg, pat, text, mgrad, wp, wq, wo,
    perm, sent1, recv1, sent2, emb_in, up, res, nlow, resT, qkv, qkvT, pT, probs, attT, att,
    upT, gaT, gqkvT, gnT, merged, gpatch, gout, uu, aa, gt, r1, s1, r2, crossing, s2, x3, r3,
    local_sem, ex_send, ex_recv, pair_send, pair_recv, p1_send, p1_recv, p2_send, p2_recv,
    p3_send, p3_recv, p4_send, p4_recv,
):
    llm = lax.axis_index("llm")
    enc = lax.axis_index("enc")
    y, x = llm // 4, llm % 4
    z, core = enc // 2, enc % 2
    device = llm * N_ENC + enc
    arrivals, sends = {}, []

    def local(source, target, slot):
        return pltpu.make_async_copy(source, target, local_sem.at[slot])

    def remote(source, target, send, recv, to_llm, to_enc):
        return pltpu.make_async_remote_copy(
            src_ref=source, dst_ref=target, send_sem=send, recv_sem=recv,
            device_id=(to_llm, to_enc), device_id_type=MESH,
        )

    load_owner = local(owner_hbm, owner, 12)
    load_start = local(start_hbm, first_row, 13)
    load_mgrad = local(mgrad_hbm, mgrad, 0)
    load_pat = local(patches_hbm, pat, 1)
    load_seg = local(seg_hbm.at[device], seg, 2)
    load_wp = local(wp_hbm, wp, 3)
    load_wq = [
        local(wq_hbm.at[:, pl.ds(D * i, D)], wq.at[:, pl.ds(D * i, D)], 4 + i) for i in range(3)
    ]
    load_wo = local(wo_hbm, wo, 7)
    load_text = local(text_hbm, text, 8)
    for load in (load_owner, load_start, load_mgrad, load_pat, load_seg, load_wp, *load_wq, load_wo, load_text):
        load.start()

    barrier = pltpu.get_barrier_semaphore()

    def greet_llm(k):
        pl.semaphore_signal(
            barrier, inc=1, device_id=((llm + k) % N_LLM, enc), device_id_type=MESH
        )

    def greet_enc(k):
        pl.semaphore_signal(
            barrier, inc=1, device_id=(llm, (enc + k) % N_ENC), device_id_type=MESH
        )

    each(1, N_LLM, greet_llm)
    each(1, N_ENC, greet_enc)

    turned = jnp.where(core == 0, x, y)
    mate_llm, mate_enc = jnp.where(core == 0, y * 4 + z, z * 4 + x), turned * 2 + core

    @pl.when(turned != z)
    def _():
        pl.semaphore_signal(
            barrier, inc=1, device_id=(mate_llm, mate_enc), device_id_type=MESH
        )

    load_owner.wait()
    load_start.wait()
    start = first_row[0, 0]
    lane = iota((16, 256), 1)
    row = iota((16, 256), 0)

    def owner_rows(s):
        rank = owner[0, s * N_ENC + enc]
        hit = (lane == rank * 16 + row).astype(F32)
        perm[pl.ds(aligned(s * 16, 16), 16), :] = hit.astype(BF)

    each(0, N_LLM, owner_rows)

    load_mgrad.wait()
    take = (iota((ROWS, SEQ), 1) == iota((ROWS, SEQ), 0) + start).astype(F32).astype(BF)
    sent1[0, :, :] = mm(take, mgrad[...]).astype(BF)

    pl.semaphore_wait(barrier, N_LLM - 1 + N_ENC - 1 + (turned != z).astype(jnp.int32))

    def piece(ref, j):
        return ref.at[pl.ds(aligned(j // 2 * 16, 16), 16), pl.ds(aligned(j % 2 * HALF, 128), HALF)]

    def ahead(k):
        return (y + k // 4) % 4 * 4 + (x + k % 4) % 4

    def behind(k):
        return (y + 4 - k // 4) % 4 * 4 + (x + 4 - k % 4) % 4

    def scatter(way, k):
        to = ahead(k)
        return remote(
            piece(sent1.at[way], to), recv1.at[way, pl.ds(aligned(llm * 16, 16), 16)],
            ex_send.at[way, 0, k], ex_recv.at[way, 0, k], to, enc,
        )

    def scatter_arrival(way, k):
        source = behind(k)
        return remote(
            piece(sent1.at[way], llm), recv1.at[way, pl.ds(aligned(source * 16, 16), 16)],
            ex_send.at[way, 0, k], ex_recv.at[way, 0, k], ahead(k), enc,
        )

    def deliver(way, target, k):
        to = ahead(k)
        return remote(
            sent2.at[way, pl.ds(aligned(to * 16, 16), 16)], piece(target, llm),
            ex_send.at[way, 1, k], ex_recv.at[way, 1, k], to, enc,
        )

    def deliver_arrival(way, target, k):
        source = behind(k)
        return remote(
            sent2.at[way, pl.ds(aligned(llm * 16, 16), 16)], piece(target, source),
            ex_send.at[way, 1, k], ex_recv.at[way, 1, k], ahead(k), enc,
        )

    def own_piece(ref):
        return ref[pl.ds(aligned(llm // 2 * 16, 16), 16), pl.ds(aligned(llm % 2 * HALF, 128), HALF)]

    def exchange_first(way):
        each_peer(lambda k: scatter(way, k).start())
        arrivals["scatter", way] = lambda: each_peer(
            lambda k: scatter_arrival(way, k).wait_recv()
        )
        sends.append(lambda: each_peer(lambda k: scatter(way, k).wait_send()))
        recv1[way, pl.ds(aligned(llm * 16, 16), 16), :] = own_piece(sent1.at[way])

    def exchange_second(way, target, dims):
        arrivals.pop(("scatter", way))()
        sent2[way, :, :] = mm(perm[...], recv1[way], dims).astype(BF)
        each_peer(lambda k: deliver(way, target, k).start())
        arrivals["deliver", way] = lambda: each_peer(
            lambda k: deliver_arrival(way, target, k).wait_recv()
        )
        sends.append(lambda: each_peer(lambda k: deliver(way, target, k).wait_send()))
        target[pl.ds(aligned(llm // 2 * 16, 16), 16), pl.ds(aligned(llm % 2 * HALF, 128), HALF)] = (
            sent2[way, pl.ds(aligned(llm * 16, 16), 16), :]
        )

    exchange_first(0)
    other = enc + 1 - 2 * core

    def to_pair(slot, source, target):
        copy = remote(source, target, pair_send.at[slot], pair_recv.at[slot], llm, other)
        copy.start()
        arrivals["pair", slot] = copy.wait_recv
        sends.append(copy.wait_send)

    load_pat.wait()
    to_pair(
        0, pat.at[:, pl.ds(aligned((1 - core) * 512, 128), HALF)], aa.at[1, pl.ds(ROWS, ROWS)]
    )
    aa[1, pl.ds(0, ROWS), :] = pat[:, pl.ds(aligned(core * 512, 128), HALF)]

    load_wp.wait()

    for i in range(5):
        columns = pl.ds(256 * i, 256)
        res[:, columns] = mm(pat[...], wp[:, columns])
    for i in range(4):
        rows = pl.ds(32 * i, 32)
        values = res[rows, :]
        centred = values - jnp.mean(values, axis=1, keepdims=True)
        inverse = lax.rsqrt(jnp.mean(centred * centred, axis=1, keepdims=True) + 1e-6)
        nlow[rows, :] = (centred * inverse).astype(BF)

    for i in range(10):
        block = pl.ds(128 * i, 128)
        resT[block, :] = res[:, block].T
    mean = jnp.sum(resT[...], axis=0, keepdims=True) * (1.0 / D)
    centred = resT[...] - mean
    inverse = lax.rsqrt(jnp.sum(centred * centred, axis=0, keepdims=True) * (1.0 / D) + 1e-6)

    for i in range(15):
        if i % 5 == 0:
            load_wq[i // 5].wait()
        columns = pl.ds(256 * i, 256)
        tile = mm(nlow[...], wq[:, columns]).astype(BF)
        qkv[:, columns] = tile
        qkvT[columns, :] = tile.T

    exchange_second(0, up, NN)

    load_seg.wait()
    one_hot = (iota((8, ROWS), 0) == seg[...]).astype(F32).astype(BF)
    same_image = mm(one_hot, one_hot, TN) > 0.5

    def forward_heads(g):
        base = g * HALF
        for j in range(8):
            first, width, offset = head_window(j)
            head = pl.ds(aligned(base + 80 * j, 16), 80)
            block = pl.ds(aligned((g * 8 + j) * ROWS, ROWS), ROWS)
            keys = qkv[:, pl.ds(aligned(D + base + first, 128), width)]
            scores = mm(keys, padded(qkvT[head, :], offset, width)) * SCALE
            scores = jnp.where(same_image, scores, -1e30)
            weights = jnp.exp(scores - jnp.max(scores, axis=0, keepdims=True))
            probability = weights / jnp.sum(weights, axis=0, keepdims=True)
            low = probability.astype(BF)
            pT[block, :] = probability
            probs[block, :] = low.T
            values = qkvT[pl.ds(aligned(2 * D + base + 80 * j, 16), 80), :]
            attT[head, :] = mm(values, low).astype(BF)

    for g in range(2):
        forward_heads(g)

    for i in range(10):
        block = pl.ds(128 * i, 128)
        att[:, block] = attT[block, :].T
    to_pair(
        1, att.at[:, pl.ds(aligned((1 - core) * HALF, 128), HALF)], aa.at[0, pl.ds(ROWS, ROWS)]
    )
    aa[0, pl.ds(0, ROWS), :] = att[:, pl.ds(aligned(core * HALF, 128), HALF)]

    load_wo.wait()
    for i in range(5):
        columns = pl.ds(256 * i, 256)
        sent1[1, :, columns] = (res[:, columns] + mm(att[...], wo[:, columns])).astype(BF)

    arrivals.pop(("deliver", 0))()

    for i in range(10):
        block = pl.ds(128 * i, 128)
        upT[block, :] = up[:, block].T
    to_pair(2, upT, uu.at[0, :, pl.ds(ROWS, ROWS)])
    exchange_first(1)
    uu[0, :, pl.ds(0, ROWS)] = upT[...]

    for i in range(5):
        rows = pl.ds(256 * i, 256)
        gaT[rows, :] = mm(wo[rows, :], upT[...]).astype(BF)

    def by_core(run):
        for c in range(2):
            pl.when(core == c)(lambda c=c: run(c))

    def gradient(grad, index):
        columns = DOT_LANES[index]
        total = mm(uu[grad], aa[grad, :, columns])
        gt[grad, :, :, :, columns] = total.astype(BF).reshape(4, 4, 80, columns.size)

    def first_copy(grad, part, k):
        columns, kind = part
        if kind == 0:
            to = (y + k) % 4
            source, to_llm, to_enc = gt.at[grad, to, :, :, columns], to * 4 + x, enc
        elif kind == 1:
            to = (x + k) % 4
            source, to_llm, to_enc = gt.at[grad, :, to, :, columns], y * 4 + to, enc
        else:
            to = (z + k) % 4
            source = gt.at[grad, :, to, :, columns] if kind == 2 else gt.at[grad, to, :, :, columns]
            to_llm, to_enc = llm, to * 2 + core
        return remote(
            source, r1.at[grad, k - 1, :, :, columns],
            p1_send.at[grad, min(kind, 2), k - 1], p1_recv.at[grad, min(kind, 2), k - 1], to_llm, to_enc,
        )

    def second_copy(grad, part, k):
        columns, kind = part
        if kind in (0, 3):
            to = (x + k) % 4
            to_llm = y * 4 + to
        else:
            to = (y + k) % 4
            to_llm = to * 4 + x
        return remote(
            s1.at[grad, to, :, columns], r2.at[grad, k - 1, :, columns],
            p2_send.at[grad, min(kind, 2), k - 1], p2_recv.at[grad, min(kind, 2), k - 1], to_llm, enc,
        )

    def cross_copy(grad, part):
        columns, _ = part
        return remote(
            crossing.at[grad, :, columns], s2.at[grad, :, columns],
            p4_send.at[grad], p4_recv.at[grad], mate_llm, mate_enc,
        )

    def third_copy(grad, k):
        to = (enc + k) % N_ENC
        return remote(
            x3.at[grad, pl.ds(aligned(to * 16, 16), 16)], r3.at[grad, k - 1],
            p3_send.at[grad, k - 1], p3_recv.at[grad, k - 1], llm, to,
        )

    def three(grad, index, copy, act):
        def run(c):
            for k in (2, 1, 3):
                getattr(copy(grad, PARTS[grad][c][index], k), act)()

        by_core(run)

    def first_phase(grad, index):
        three(grad, index, first_copy, "start")
        arrivals["first", grad, index] = lambda: three(grad, index, first_copy, "wait_recv")
        sends.append(lambda: three(grad, index, first_copy, "wait_send"))

    def second_phase(grad, index):
        arrivals.pop(("first", grad, index))()

        def run(c):
            columns, kind = PARTS[grad][c][index]
            for i in range(4):
                if kind in (0, 3):
                    own = gt[grad, z if kind else y, i, :, columns]
                else:
                    own = gt[grad, i, x if kind == 1 else z, :, columns]
                total = own.astype(F32)
                for k in range(3):
                    total = total + r1[grad, k, i, :, columns].astype(F32)
                s1[grad, i, :, columns] = total.astype(BF)

        by_core(run)
        three(grad, index, second_copy, "start")
        arrivals["second", grad, index] = lambda: three(grad, index, second_copy, "wait_recv")
        sends.append(lambda: three(grad, index, second_copy, "wait_send"))

    spread_row = iota((ROWS, 80), 0)
    spread = jnp.logical_and(
        iota((ROWS, 80), 1) == spread_row // 16 * 10 + spread_row % 16, spread_row % 16 < 10
    )
    spread = spread.astype(F32).astype(BF)

    def cross(grad, act):
        def run(c):
            getattr(cross_copy(grad, PARTS[grad][c][0]), act)()

        pl.when(turned != z)(lambda: by_core(run))

    def third_sum(grad, index):
        arrivals.pop(("second", grad, index))()

        def run(c):
            columns, kind = PARTS[grad][c][index]
            total = s1[grad, x if kind in (0, 3) else y, :, columns].astype(F32)
            for k in range(3):
                total = total + r2[grad, k, :, columns].astype(F32)
            if kind < 2:
                s2[grad, :, columns] = total.astype(BF)
                return

            crossing[grad, :, columns] = total.astype(BF)

            @pl.when(turned == z)
            def _():
                s2[grad, :, columns] = crossing[grad, :, columns]

        by_core(run)
        if index == 0:
            cross(grad, "start")
            arrivals["cross", grad] = lambda: cross(grad, "wait_recv")
            sends.append(lambda: cross(grad, "wait_send"))

    def third_phase(grad):
        arrivals.pop(("cross", grad))()
        x3[grad, :, :] = mm(spread, s2[grad]).astype(BF)
        [third_copy(grad, k).start() for k in (4, 3, 5, 2, 6, 7, 1)]
        arrivals["third", grad] = lambda: each(
            1, N_ENC, lambda k: third_copy(grad, k).wait_recv()
        )
        sends.append(lambda: each(1, N_ENC, lambda k: third_copy(grad, k).wait_send()))

    def last_phase(grad, total, shift):
        arrivals.pop(("third", grad))()
        mine = x3[grad, pl.ds(aligned(enc * 16, 16), 16), :].astype(F32)
        for k in (2, 4, 6):
            mine = mine + r3[grad, k - 1].astype(F32)
        theirs = r3[grad, 0].astype(F32)
        for k in (3, 5, 7):
            theirs = theirs + r3[grad, k - 1].astype(F32)

        def put_halves(c):
            total[:, pl.ds(0, HALF)] = (mine if c == 0 else theirs)[:10, :]
            total[:, pl.ds(shift, HALF)] = (theirs if c == 0 else mine)[:10, :]

        by_core(put_halves)

    @pl.when(core == 0)
    def _():
        s2[1, :, pl.ds(512, 128)] = jnp.zeros((80, 128), BF)

    arrivals.pop(("pair", 1))()
    arrivals.pop(("pair", 2))()
    for index in range(3):
        gradient(0, index)
        first_phase(0, index)

    def backward_heads(g):
        base = g * HALF
        for j in range(8):
            first, width, offset = head_window(j)
            head = pl.ds(aligned(base + 80 * j, 16), 80)
            head_k = pl.ds(aligned(D + base + 80 * j, 16), 80)
            head_v = pl.ds(aligned(2 * D + base + 80 * j, 16), 80)
            block = pl.ds(aligned((g * 8 + j) * ROWS, ROWS), ROWS)
            values = qkv[:, pl.ds(aligned(2 * D + base + first, 128), width)]
            rows = gaT[head, :]
            grad_prob = mm(values, padded(rows, offset, width))
            probability = pT[block, :]
            weighted = jnp.sum(grad_prob * probability, axis=0, keepdims=True)
            low = (probability * (grad_prob - weighted) * SCALE).astype(BF)
            gqkvT[head, :] = mm(qkvT[head_k, :], low).astype(BF)
            gqkvT[head_k, :] = mm(qkvT[head, :], low, NT).astype(BF)
            gqkvT[head_v, :] = mm(rows, probs[block, :]).astype(BF)

    for g in range(2):
        backward_heads(g)


    mean_grad = jnp.zeros((1, ROWS), F32)
    mean_cross = jnp.zeros((1, ROWS), F32)
    for i in range(5):
        rows = pl.ds(256 * i, 256)
        tile = mm(wq[rows, :], gqkvT[...])
        gnT[rows, :] = tile
        normed = (resT[rows, :] - mean) * inverse
        mean_grad = mean_grad + jnp.sum(tile, axis=0, keepdims=True)
        mean_cross = mean_cross + jnp.sum(tile * normed, axis=0, keepdims=True)
    exchange_second(1, emb_in, TN)
    mean_grad = mean_grad * (1.0 / D)
    mean_cross = mean_cross * (1.0 / D)

    for i in range(5):
        rows = pl.ds(256 * i, 256)
        normed = (resT[rows, :] - mean) * inverse
        total = upT[rows, :].astype(F32) + inverse * (
            gnT[rows, :] - mean_grad - normed * mean_cross
        )
        uu[1, rows, pl.ds(0, ROWS)] = total.astype(BF)
    to_pair(3, uu.at[1, :, pl.ds(0, ROWS)], uu.at[1, :, pl.ds(ROWS, ROWS)])
    second_phase(0, 1)
    second_phase(0, 2)
    arrivals.pop(("pair", 0))()
    arrivals.pop(("pair", 3))()
    for index in range(3):
        gradient(1, index)
        first_phase(1, index)

    third_sum(0, 1)
    third_sum(0, 2)

    arrivals.pop(("deliver", 1))()
    load_text.wait()
    position = iota((SEQ, ROWS), 0)
    put = (position == iota((SEQ, ROWS), 1) + start).astype(F32).astype(BF)

    place = iota((SEQ, 256), 0)
    inside = jnp.logical_and(place >= start, place < start + ROWS)
    for i in range(5):
        columns = pl.ds(256 * i, 256)
        placed = mm(put, emb_in[:, columns])
        merged[:, columns] = jnp.where(inside, placed, text[:, columns].astype(F32)).astype(BF)
    store_merged = local(merged, merged_hbm, 9)
    store_merged.start()
    second_phase(0, 0)
    second_phase(1, 0)
    second_phase(1, 1)
    second_phase(1, 2)
    third_sum(0, 0)
    third_sum(1, 0)
    third_phase(0)
    third_sum(1, 1)
    third_sum(1, 2)
    third_phase(1)
    last_phase(0, gout, HALF)
    store_gout = local(gout, gout_hbm, 10)
    store_gout.start()
    last_phase(1, gpatch, 512)
    store_gpatch = local(gpatch, gpatch_hbm, 11)
    store_gpatch.start()

    for sent in sends:
        sent()
    store_merged.wait()
    store_gout.wait()
    store_gpatch.wait()


def finish_kernel(a, b, c, a_out, b_out, c_out, a_held, b_held, c_held, sem):
    arrays = ((a, a_held, a_out), (b, b_held, b_out), (c, c_held, c_out))
    loads = [pltpu.make_async_copy(v[0], v[1], sem.at[i]) for i, v in enumerate(arrays)]
    stores = [pltpu.make_async_copy(v[1], v[2], sem.at[3 + i]) for i, v in enumerate(arrays)]
    for load in loads:
        load.start()
    for load, store in zip(loads, stores):
        load.wait()
        store.start()
    for store in stores:
        store.wait()


def shards(
    patches, image_seg, owner_slot, place_start, text_embeds, merged_grad, w_patch, w_qkv, w_out
):
    anywhere = pl.BlockSpec(memory_space=pl.ANY)
    dma = pltpu.SemaphoreType.DMA
    merged, grad_patch, grad_out = pl.pallas_call(
        kernel,
        out_shape=(
            jax.ShapeDtypeStruct((SEQ, D), BF),
            jax.ShapeDtypeStruct((10, PIN), F32),
            jax.ShapeDtypeStruct((10, D), F32),
        ),
        in_specs=[anywhere] * 9,
        out_specs=(anywhere, anywhere, anywhere),
        scratch_shapes=[
            pltpu.SMEM((1, ROWS), jnp.int32),
            pltpu.SMEM((1, 1), jnp.int32),
            pltpu.VMEM((1, ROWS), jnp.int32),
            pltpu.VMEM((ROWS, PIN), BF),
            pltpu.VMEM((SEQ, D), BF),
            pltpu.VMEM((SEQ, D), BF),
            pltpu.VMEM((PIN, D), BF),
            pltpu.VMEM((D, 3 * D), BF),
            pltpu.VMEM((D, D), BF),
            pltpu.VMEM((256, 256), BF),
            pltpu.VMEM((2, ROWS, D), BF),
            pltpu.VMEM((2, 256, HALF), BF),
            pltpu.VMEM((2, 256, HALF), BF),
            pltpu.VMEM((ROWS, D), BF),
            pltpu.VMEM((ROWS, D), BF),
            pltpu.VMEM((ROWS, D), F32),
            pltpu.VMEM((ROWS, D), BF),
            pltpu.VMEM((D, ROWS), F32),
            pltpu.VMEM((ROWS, 3 * D), BF),
            pltpu.VMEM((3 * D, ROWS), BF),
            pltpu.VMEM((HEADS * ROWS, ROWS), F32),
            pltpu.VMEM((HEADS * ROWS, ROWS), BF),
            pltpu.VMEM((D, ROWS), BF),
            pltpu.VMEM((ROWS, D), BF),
            pltpu.VMEM((D, ROWS), BF),
            pltpu.VMEM((D, ROWS), BF),
            pltpu.VMEM((3 * D, ROWS), BF),
            pltpu.VMEM((D, ROWS), F32),
            pltpu.VMEM((SEQ, D), BF),
            pltpu.VMEM((10, PIN), F32),
            pltpu.VMEM((10, D), F32),
            pltpu.VMEM((2, D, 2 * ROWS), BF),
            pltpu.VMEM((2, 2 * ROWS, HALF), BF),
            pltpu.VMEM((2, 4, 4, 80, HALF), BF),
            pltpu.VMEM((2, 3, 4, 80, HALF), BF),
            pltpu.VMEM((2, 4, 80, HALF), BF),
            pltpu.VMEM((2, 3, 80, HALF), BF),
            pltpu.VMEM((2, 80, HALF), BF),
            pltpu.VMEM((2, 80, HALF), BF),
            pltpu.VMEM((2, ROWS, HALF), BF),
            pltpu.VMEM((2, 7, 16, HALF), BF),
            dma((14,)),
            dma((2, 2, N_LLM)),
            dma((2, 2, N_LLM)),
            dma((4,)),
            dma((4,)),
            dma((2, 3, 3)),
            dma((2, 3, 3)),
            dma((2, 3, 3)),
            dma((2, 3, 3)),
            dma((2, 7)),
            dma((2, 7)),
            dma((2,)),
            dma((2,)),
        ],
        compiler_params=pltpu.CompilerParams(
            collective_id=0, has_side_effects=True, vmem_limit_bytes=56 * 1024 * 1024
        ),
    )(
        owner_slot.reshape(1, 128), place_start, image_seg, patches, text_embeds, merged_grad,
        w_patch, w_qkv, w_out,
    )
    merged, grad_patch, grad_out = pl.pallas_call(
        finish_kernel,
        out_shape=(
            jax.ShapeDtypeStruct((SEQ, D), BF),
            jax.ShapeDtypeStruct((10, PIN), F32),
            jax.ShapeDtypeStruct((10, D), F32),
        ),
        in_specs=[anywhere] * 3,
        out_specs=(anywhere, anywhere, anywhere),
        scratch_shapes=[
            pltpu.VMEM((SEQ, D), BF),
            pltpu.VMEM((10, PIN), F32),
            pltpu.VMEM((10, D), F32),
            dma((6,)),
        ],
    )(merged, grad_patch, grad_out)
    return (merged, grad_patch.T, grad_out.T)


def solution(mesh):
    rows = P(("llm", "enc"), None)
    columns = P(None, ("llm", "enc"))
    return jax.shard_map(
        shards,
        mesh=mesh,
        in_specs=(rows, P(), P(), rows, rows, rows, P(), P(), P()),
        out_specs=(rows, columns, columns),
        check_vma=False,
    )
```

```python
import jax
import jax.numpy as jnp
from jax import lax
from jax.experimental import pallas as pl
from jax.experimental.pallas import tpu as pltpu
from jax.sharding import PartitionSpec as P

D = 1280
HEADS = 16
HEAD_DIM = 80
PIN = 1152
ROWS = 128
SEQ = 160
N_LLM = 16
N_ENC = 8
HALF = 640
SCALE = HEAD_DIM ** (-0.5)

OUT_PARTS = (
    ((pl.ds(384, 256), 2), (pl.ds(0, 256), 0), (pl.ds(256, 128), 1)),
    ((pl.ds(384, 256), 3), (pl.ds(0, 128), 0), (pl.ds(128, 256), 1)),
)
PATCH_PARTS = (
    ((pl.ds(384, 128), 2), (pl.ds(0, 256), 0), (pl.ds(256, 128), 1)),
    ((pl.ds(384, 256), 3), (pl.ds(0, 128), 0), (pl.ds(128, 256), 1)),
)
PARTS = (OUT_PARTS, PATCH_PARTS)
PEERS = (10, 6, 9, 11, 14, 2, 5, 7, 8, 13, 15, 1, 3, 4, 12)
DOT_LANES = (pl.ds(384, 256), pl.ds(0, 256), pl.ds(256, 128))

BF = jnp.bfloat16
F32 = jnp.float32
MESH = pl.DeviceIdType.MESH
NN = (((1,), (0,)), ((), ()))
NT = (((1,), (1,)), ((), ()))
TN = (((0,), (0,)), ((), ()))


def mm(a, b, dims=NN):
    return lax.dot_general(a, b, dims, preferred_element_type=F32)


def iota(shape, axis):
    return lax.broadcasted_iota(jnp.int32, shape, axis)


def aligned(value, unit):
    return value if isinstance(value, int) else pl.multiple_of(value, unit)


def each(low, high, body):
    for i in range(low, high):
        body(i)


def each_peer(body):
    for k in PEERS:
        body(k)


def head_window(j):
    first = 80 * j // 128 * 128
    last = -(-(80 * j + 80) // 128) * 128
    return first, last - first, 80 * j - first


def padded(rows, offset, width):
    pieces = []
    if offset:
        pieces.append(jnp.zeros((offset, ROWS), BF))
    pieces.append(rows)
    if width - offset - 80:
        pieces.append(jnp.zeros((width - offset - 80, ROWS), BF))
    return jnp.concatenate(pieces, axis=0)


def kernel(
    owner_hbm, start_hbm, seg_hbm, patches_hbm, text_hbm, mgrad_hbm, wp_hbm, wq_hbm, wo_hbm,
    merged_hbm, gpatch_hbm, gout_hbm,
    owner, first_row, seg, pat, text, mgrad, wp, wq, wo,
    perm, sent1, recv1, sent2, emb_in, up, res, nlow, resT, qkv, qkvT, pT, probs, attT, att,
    upT, gaT, gqkvT, gnT, merged, gpatch, gout, uu, aa, gt, r1, s1, r2, crossing, s2, x3, r3,
    local_sem, ex_send, ex_recv, pair_send, pair_recv, p1_send, p1_recv, p2_send, p2_recv,
    p3_send, p3_recv, p4_send, p4_recv,
):
    llm = lax.axis_index("llm")
    enc = lax.axis_index("enc")
    y, x = llm // 4, llm % 4
    z, core = enc // 2, enc % 2
    device = llm * N_ENC + enc
    arrivals, sends = {}, []

    def local(source, target, slot):
        return pltpu.make_async_copy(source, target, local_sem.at[slot])

    def remote(source, target, send, recv, to_llm, to_enc):
        return pltpu.make_async_remote_copy(
            src_ref=source, dst_ref=target, send_sem=send, recv_sem=recv,
            device_id=(to_llm, to_enc), device_id_type=MESH,
        )

    load_owner = local(owner_hbm, owner, 12)
    load_start = local(start_hbm, first_row, 13)
    load_mgrad = local(mgrad_hbm, mgrad, 0)
    load_pat = local(patches_hbm, pat, 1)
    load_seg = local(seg_hbm.at[device], seg, 2)
    load_wp = local(wp_hbm, wp, 3)
    load_wq = [
        local(wq_hbm.at[:, pl.ds(D * i, D)], wq.at[:, pl.ds(D * i, D)], 4 + i) for i in range(3)
    ]
    load_wo = local(wo_hbm, wo, 7)
    load_text = local(text_hbm, text, 8)
    for load in (load_owner, load_start, load_mgrad, load_pat, load_seg, load_wp, *load_wq, load_wo, load_text):
        load.start()

    barrier = pltpu.get_barrier_semaphore()

    def greet_llm(k):
        pl.semaphore_signal(
            barrier, inc=1, device_id=((llm + k) % N_LLM, enc), device_id_type=MESH
        )

    def greet_enc(k):
        pl.semaphore_signal(
            barrier, inc=1, device_id=(llm, (enc + k) % N_ENC), device_id_type=MESH
        )

    each(1, N_LLM, greet_llm)
    each(1, N_ENC, greet_enc)

    turned = jnp.where(core == 0, x, y)
    mate_llm, mate_enc = jnp.where(core == 0, y * 4 + z, z * 4 + x), turned * 2 + core

    @pl.when(turned != z)
    def _():
        pl.semaphore_signal(
            barrier, inc=1, device_id=(mate_llm, mate_enc), device_id_type=MESH
        )

    load_owner.wait()
    load_start.wait()
    start = first_row[0, 0]
    lane = iota((16, 256), 1)
    row = iota((16, 256), 0)

    def owner_rows(s):
        rank = owner[0, s * N_ENC + enc]
        hit = (lane == rank * 16 + row).astype(F32)
        perm[pl.ds(aligned(s * 16, 16), 16), :] = hit.astype(BF)

    each(0, N_LLM, owner_rows)

    load_mgrad.wait()
    take = (iota((ROWS, SEQ), 1) == iota((ROWS, SEQ), 0) + start).astype(F32).astype(BF)
    sent1[0, :, :] = mm(take, mgrad[...]).astype(BF)

    pl.semaphore_wait(barrier, N_LLM - 1 + N_ENC - 1 + (turned != z).astype(jnp.int32))

    def piece(ref, j):
        return ref.at[pl.ds(aligned(j // 2 * 16, 16), 16), pl.ds(aligned(j % 2 * HALF, 128), HALF)]

    def ahead(k):
        return (y + k // 4) % 4 * 4 + (x + k % 4) % 4

    def behind(k):
        return (y + 4 - k // 4) % 4 * 4 + (x + 4 - k % 4) % 4

    def scatter(way, k):
        to = ahead(k)
        return remote(
            piece(sent1.at[way], to), recv1.at[way, pl.ds(aligned(llm * 16, 16), 16)],
            ex_send.at[way, 0, k], ex_recv.at[way, 0, k], to, enc,
        )

    def scatter_arrival(way, k):
        source = behind(k)
        return remote(
            piece(sent1.at[way], llm), recv1.at[way, pl.ds(aligned(source * 16, 16), 16)],
            ex_send.at[way, 0, k], ex_recv.at[way, 0, k], ahead(k), enc,
        )

    def deliver(way, target, k):
        to = ahead(k)
        return remote(
            sent2.at[way, pl.ds(aligned(to * 16, 16), 16)], piece(target, llm),
            ex_send.at[way, 1, k], ex_recv.at[way, 1, k], to, enc,
        )

    def deliver_arrival(way, target, k):
        source = behind(k)
        return remote(
            sent2.at[way, pl.ds(aligned(llm * 16, 16), 16)], piece(target, source),
            ex_send.at[way, 1, k], ex_recv.at[way, 1, k], ahead(k), enc,
        )

    def own_piece(ref):
        return ref[pl.ds(aligned(llm // 2 * 16, 16), 16), pl.ds(aligned(llm % 2 * HALF, 128), HALF)]

    def exchange_first(way):
        each_peer(lambda k: scatter(way, k).start())
        arrivals["scatter", way] = lambda: each_peer(
            lambda k: scatter_arrival(way, k).wait_recv()
        )
        sends.append(lambda: each_peer(lambda k: scatter(way, k).wait_send()))
        recv1[way, pl.ds(aligned(llm * 16, 16), 16), :] = own_piece(sent1.at[way])

    def exchange_second(way, target, dims):
        arrivals.pop(("scatter", way))()
        sent2[way, :, :] = mm(perm[...], recv1[way], dims).astype(BF)
        each_peer(lambda k: deliver(way, target, k).start())
        arrivals["deliver", way] = lambda: each_peer(
            lambda k: deliver_arrival(way, target, k).wait_recv()
        )
        sends.append(lambda: each_peer(lambda k: deliver(way, target, k).wait_send()))
        target[pl.ds(aligned(llm // 2 * 16, 16), 16), pl.ds(aligned(llm % 2 * HALF, 128), HALF)] = (
            sent2[way, pl.ds(aligned(llm * 16, 16), 16), :]
        )

    exchange_first(0)
    other = enc + 1 - 2 * core

    def to_pair(slot, source, target):
        copy = remote(source, target, pair_send.at[slot], pair_recv.at[slot], llm, other)
        copy.start()
        arrivals["pair", slot] = copy.wait_recv
        sends.append(copy.wait_send)

    load_pat.wait()
    to_pair(
        0, pat.at[:, pl.ds(aligned((1 - core) * 512, 128), HALF)], aa.at[1, pl.ds(ROWS, ROWS)]
    )
    aa[1, pl.ds(0, ROWS), :] = pat[:, pl.ds(aligned(core * 512, 128), HALF)]

    load_wp.wait()

    for i in range(5):
        columns = pl.ds(256 * i, 256)
        res[:, columns] = mm(pat[...], wp[:, columns])
    for i in range(4):
        rows = pl.ds(32 * i, 32)
        values = res[rows, :]
        centred = values - jnp.mean(values, axis=1, keepdims=True)
        inverse = lax.rsqrt(jnp.mean(centred * centred, axis=1, keepdims=True) + 1e-6)
        nlow[rows, :] = (centred * inverse).astype(BF)

    for i in range(10):
        block = pl.ds(128 * i, 128)
        resT[block, :] = res[:, block].T
    mean = jnp.sum(resT[...], axis=0, keepdims=True) * (1.0 / D)
    centred = resT[...] - mean
    inverse = lax.rsqrt(jnp.sum(centred * centred, axis=0, keepdims=True) * (1.0 / D) + 1e-6)

    for i in range(15):
        if i % 5 == 0:
            load_wq[i // 5].wait()
        columns = pl.ds(256 * i, 256)
        tile = mm(nlow[...], wq[:, columns]).astype(BF)
        qkv[:, columns] = tile
        qkvT[columns, :] = tile.T

    exchange_second(0, up, NN)

    load_seg.wait()
    one_hot = (iota((8, ROWS), 0) == seg[...]).astype(F32).astype(BF)
    same_image = mm(one_hot, one_hot, TN) > 0.5

    def forward_heads(g):
        base = g * HALF
        for j in range(8):
            first, width, offset = head_window(j)
            head = pl.ds(aligned(base + 80 * j, 16), 80)
            block = pl.ds(aligned((g * 8 + j) * ROWS, ROWS), ROWS)
            keys = qkv[:, pl.ds(aligned(D + base + first, 128), width)]
            scores = mm(keys, padded(qkvT[head, :], offset, width)) * SCALE
            scores = jnp.where(same_image, scores, -1e30)
            weights = jnp.exp(scores - jnp.max(scores, axis=0, keepdims=True))
            probability = weights / jnp.sum(weights, axis=0, keepdims=True)
            low = probability.astype(BF)
            pT[block, :] = probability
            probs[block, :] = low.T
            values = qkvT[pl.ds(aligned(2 * D + base + 80 * j, 16), 80), :]
            attT[head, :] = mm(values, low).astype(BF)

    for g in range(2):
        forward_heads(g)

    for i in range(10):
        block = pl.ds(128 * i, 128)
        att[:, block] = attT[block, :].T
    to_pair(
        1, att.at[:, pl.ds(aligned((1 - core) * HALF, 128), HALF)], aa.at[0, pl.ds(ROWS, ROWS)]
    )
    aa[0, pl.ds(0, ROWS), :] = att[:, pl.ds(aligned(core * HALF, 128), HALF)]

    load_wo.wait()
    for i in range(5):
        columns = pl.ds(256 * i, 256)
        sent1[1, :, columns] = (res[:, columns] + mm(att[...], wo[:, columns])).astype(BF)

    arrivals.pop(("deliver", 0))()

    for i in range(10):
        block = pl.ds(128 * i, 128)
        upT[block, :] = up[:, block].T
    to_pair(2, upT, uu.at[0, :, pl.ds(ROWS, ROWS)])
    exchange_first(1)
    uu[0, :, pl.ds(0, ROWS)] = upT[...]

    for i in range(5):
        rows = pl.ds(256 * i, 256)
        gaT[rows, :] = mm(wo[rows, :], upT[...]).astype(BF)

    def by_core(run):
        for c in range(2):
            pl.when(core == c)(lambda c=c: run(c))

    def gradient(grad, index):
        columns = DOT_LANES[index]
        total = mm(uu[grad], aa[grad, :, columns])
        gt[grad, :, :, :, columns] = total.astype(BF).reshape(4, 4, 80, columns.size)

    def first_copy(grad, part, k):
        columns, kind = part
        if kind == 0:
            to = (y + k) % 4
            source, to_llm, to_enc = gt.at[grad, to, :, :, columns], to * 4 + x, enc
        elif kind == 1:
            to = (x + k) % 4
            source, to_llm, to_enc = gt.at[grad, :, to, :, columns], y * 4 + to, enc
        else:
            to = (z + k) % 4
            source = gt.at[grad, :, to, :, columns] if kind == 2 else gt.at[grad, to, :, :, columns]
            to_llm, to_enc = llm, to * 2 + core
        return remote(
            source, r1.at[grad, k - 1, :, :, columns],
            p1_send.at[grad, min(kind, 2), k - 1], p1_recv.at[grad, min(kind, 2), k - 1], to_llm, to_enc,
        )

    def second_copy(grad, part, k):
        columns, kind = part
        if kind in (0, 3):
            to = (x + k) % 4
            to_llm = y * 4 + to
        else:
            to = (y + k) % 4
            to_llm = to * 4 + x
        return remote(
            s1.at[grad, to, :, columns], r2.at[grad, k - 1, :, columns],
            p2_send.at[grad, min(kind, 2), k - 1], p2_recv.at[grad, min(kind, 2), k - 1], to_llm, enc,
        )

    def cross_copy(grad, part):
        columns, _ = part
        return remote(
            crossing.at[grad, :, columns], s2.at[grad, :, columns],
            p4_send.at[grad], p4_recv.at[grad], mate_llm, mate_enc,
        )

    def third_copy(grad, k):
        to = (enc + k) % N_ENC
        return remote(
            x3.at[grad, pl.ds(aligned(to * 16, 16), 16)], r3.at[grad, k - 1],
            p3_send.at[grad, k - 1], p3_recv.at[grad, k - 1], llm, to,
        )

    def three(grad, index, copy, act):
        def run(c):
            for k in (2, 1, 3):
                getattr(copy(grad, PARTS[grad][c][index], k), act)()

        by_core(run)

    def first_phase(grad, index):
        three(grad, index, first_copy, "start")
        arrivals["first", grad, index] = lambda: three(grad, index, first_copy, "wait_recv")
        sends.append(lambda: three(grad, index, first_copy, "wait_send"))

    def second_phase(grad, index):
        arrivals.pop(("first", grad, index))()

        def run(c):
            columns, kind = PARTS[grad][c][index]
            for i in range(4):
                if kind in (0, 3):
                    own = gt[grad, z if kind else y, i, :, columns]
                else:
                    own = gt[grad, i, x if kind == 1 else z, :, columns]
                total = own.astype(F32)
                for k in range(3):
                    total = total + r1[grad, k, i, :, columns].astype(F32)
                s1[grad, i, :, columns] = total.astype(BF)

        by_core(run)
        three(grad, index, second_copy, "start")
        arrivals["second", grad, index] = lambda: three(grad, index, second_copy, "wait_recv")
        sends.append(lambda: three(grad, index, second_copy, "wait_send"))

    spread_row = iota((ROWS, 80), 0)
    spread = jnp.logical_and(
        iota((ROWS, 80), 1) == spread_row // 16 * 10 + spread_row % 16, spread_row % 16 < 10
    )
    spread = spread.astype(F32).astype(BF)

    def cross(grad, act):
        def run(c):
            getattr(cross_copy(grad, PARTS[grad][c][0]), act)()

        pl.when(turned != z)(lambda: by_core(run))

    def third_sum(grad, index):
        arrivals.pop(("second", grad, index))()

        def run(c):
            columns, kind = PARTS[grad][c][index]
            total = s1[grad, x if kind in (0, 3) else y, :, columns].astype(F32)
            for k in range(3):
                total = total + r2[grad, k, :, columns].astype(F32)
            if kind < 2:
                s2[grad, :, columns] = total.astype(BF)
                return

            crossing[grad, :, columns] = total.astype(BF)

            @pl.when(turned == z)
            def _():
                s2[grad, :, columns] = crossing[grad, :, columns]

        by_core(run)
        if index == 0:
            cross(grad, "start")
            arrivals["cross", grad] = lambda: cross(grad, "wait_recv")
            sends.append(lambda: cross(grad, "wait_send"))

    def third_phase(grad):
        arrivals.pop(("cross", grad))()
        x3[grad, :, :] = mm(spread, s2[grad]).astype(BF)
        [third_copy(grad, k).start() for k in (4, 3, 5, 2, 6, 7, 1)]
        arrivals["third", grad] = lambda: each(
            1, N_ENC, lambda k: third_copy(grad, k).wait_recv()
        )
        sends.append(lambda: each(1, N_ENC, lambda k: third_copy(grad, k).wait_send()))

    def last_phase(grad, total, shift):
        arrivals.pop(("third", grad))()
        mine = x3[grad, pl.ds(aligned(enc * 16, 16), 16), :].astype(F32)
        for k in (2, 4, 6):
            mine = mine + r3[grad, k - 1].astype(F32)
        theirs = r3[grad, 0].astype(F32)
        for k in (3, 5, 7):
            theirs = theirs + r3[grad, k - 1].astype(F32)

        def put_halves(c):
            total[:, pl.ds(0, HALF)] = (mine if c == 0 else theirs)[:10, :]
            total[:, pl.ds(shift, HALF)] = (theirs if c == 0 else mine)[:10, :]

        by_core(put_halves)

    @pl.when(core == 0)
    def _():
        s2[1, :, pl.ds(512, 128)] = jnp.zeros((80, 128), BF)

    arrivals.pop(("pair", 1))()
    arrivals.pop(("pair", 2))()
    for index in range(3):
        gradient(0, index)
        first_phase(0, index)

    def backward_heads(g):
        base = g * HALF
        for j in range(8):
            first, width, offset = head_window(j)
            head = pl.ds(aligned(base + 80 * j, 16), 80)
            head_k = pl.ds(aligned(D + base + 80 * j, 16), 80)
            head_v = pl.ds(aligned(2 * D + base + 80 * j, 16), 80)
            block = pl.ds(aligned((g * 8 + j) * ROWS, ROWS), ROWS)
            values = qkv[:, pl.ds(aligned(2 * D + base + first, 128), width)]
            rows = gaT[head, :]
            grad_prob = mm(values, padded(rows, offset, width))
            probability = pT[block, :]
            weighted = jnp.sum(grad_prob * probability, axis=0, keepdims=True)
            low = (probability * (grad_prob - weighted) * SCALE).astype(BF)
            gqkvT[head, :] = mm(qkvT[head_k, :], low).astype(BF)
            gqkvT[head_k, :] = mm(qkvT[head, :], low, NT).astype(BF)
            gqkvT[head_v, :] = mm(rows, probs[block, :]).astype(BF)

    for g in range(2):
        backward_heads(g)


    exchange_second(1, emb_in, TN)
    mean_grad = jnp.zeros((1, ROWS), F32)
    mean_cross = jnp.zeros((1, ROWS), F32)
    for i in range(5):
        rows = pl.ds(256 * i, 256)
        tile = mm(wq[rows, :], gqkvT[...])
        gnT[rows, :] = tile
        normed = (resT[rows, :] - mean) * inverse
        mean_grad = mean_grad + jnp.sum(tile, axis=0, keepdims=True)
        mean_cross = mean_cross + jnp.sum(tile * normed, axis=0, keepdims=True)
    mean_grad = mean_grad * (1.0 / D)
    mean_cross = mean_cross * (1.0 / D)

    for i in range(5):
        rows = pl.ds(256 * i, 256)
        normed = (resT[rows, :] - mean) * inverse
        total = upT[rows, :].astype(F32) + inverse * (
            gnT[rows, :] - mean_grad - normed * mean_cross
        )
        uu[1, rows, pl.ds(0, ROWS)] = total.astype(BF)
    to_pair(3, uu.at[1, :, pl.ds(0, ROWS)], uu.at[1, :, pl.ds(ROWS, ROWS)])
    second_phase(0, 1)
    second_phase(0, 2)
    arrivals.pop(("pair", 0))()
    arrivals.pop(("pair", 3))()
    for index in range(3):
        gradient(1, index)
        first_phase(1, index)

    third_sum(0, 1)
    third_sum(0, 2)

    arrivals.pop(("deliver", 1))()
    load_text.wait()
    position = iota((SEQ, ROWS), 0)
    put = (position == iota((SEQ, ROWS), 1) + start).astype(F32).astype(BF)

    place = iota((SEQ, 256), 0)
    inside = jnp.logical_and(place >= start, place < start + ROWS)
    for i in range(5):
        columns = pl.ds(256 * i, 256)
        placed = mm(put, emb_in[:, columns])
        merged[:, columns] = jnp.where(inside, placed, text[:, columns].astype(F32)).astype(BF)
    store_merged = local(merged, merged_hbm, 9)
    store_merged.start()
    second_phase(0, 0)
    second_phase(1, 0)
    second_phase(1, 1)
    second_phase(1, 2)
    third_sum(0, 0)
    third_sum(1, 0)
    third_phase(0)
    third_sum(1, 1)
    third_sum(1, 2)
    third_phase(1)
    last_phase(0, gout, HALF)
    store_gout = local(gout, gout_hbm, 10)
    store_gout.start()
    last_phase(1, gpatch, 512)
    store_gpatch = local(gpatch, gpatch_hbm, 11)
    store_gpatch.start()

    for sent in sends:
        sent()
    store_merged.wait()
    store_gout.wait()
    store_gpatch.wait()


def finish_kernel(a, b, c, a_out, b_out, c_out, a_held, b_held, c_held, sem):
    arrays = ((a, a_held, a_out), (b, b_held, b_out), (c, c_held, c_out))
    loads = [pltpu.make_async_copy(v[0], v[1], sem.at[i]) for i, v in enumerate(arrays)]
    stores = [pltpu.make_async_copy(v[1], v[2], sem.at[3 + i]) for i, v in enumerate(arrays)]
    for load in loads:
        load.start()
    for load, store in zip(loads, stores):
        load.wait()
        store.start()
    for store in stores:
        store.wait()


def shards(
    patches, image_seg, owner_slot, place_start, text_embeds, merged_grad, w_patch, w_qkv, w_out
):
    anywhere = pl.BlockSpec(memory_space=pl.ANY)
    dma = pltpu.SemaphoreType.DMA
    merged, grad_patch, grad_out = pl.pallas_call(
        kernel,
        out_shape=(
            jax.ShapeDtypeStruct((SEQ, D), BF),
            jax.ShapeDtypeStruct((10, PIN), F32),
            jax.ShapeDtypeStruct((10, D), F32),
        ),
        in_specs=[anywhere] * 9,
        out_specs=(anywhere, anywhere, anywhere),
        scratch_shapes=[
            pltpu.SMEM((1, ROWS), jnp.int32),
            pltpu.SMEM((1, 1), jnp.int32),
            pltpu.VMEM((1, ROWS), jnp.int32),
            pltpu.VMEM((ROWS, PIN), BF),
            pltpu.VMEM((SEQ, D), BF),
            pltpu.VMEM((SEQ, D), BF),
            pltpu.VMEM((PIN, D), BF),
            pltpu.VMEM((D, 3 * D), BF),
            pltpu.VMEM((D, D), BF),
            pltpu.VMEM((256, 256), BF),
            pltpu.VMEM((2, ROWS, D), BF),
            pltpu.VMEM((2, 256, HALF), BF),
            pltpu.VMEM((2, 256, HALF), BF),
            pltpu.VMEM((ROWS, D), BF),
            pltpu.VMEM((ROWS, D), BF),
            pltpu.VMEM((ROWS, D), F32),
            pltpu.VMEM((ROWS, D), BF),
            pltpu.VMEM((D, ROWS), F32),
            pltpu.VMEM((ROWS, 3 * D), BF),
            pltpu.VMEM((3 * D, ROWS), BF),
            pltpu.VMEM((HEADS * ROWS, ROWS), F32),
            pltpu.VMEM((HEADS * ROWS, ROWS), BF),
            pltpu.VMEM((D, ROWS), BF),
            pltpu.VMEM((ROWS, D), BF),
            pltpu.VMEM((D, ROWS), BF),
            pltpu.VMEM((D, ROWS), BF),
            pltpu.VMEM((3 * D, ROWS), BF),
            pltpu.VMEM((D, ROWS), F32),
            pltpu.VMEM((SEQ, D), BF),
            pltpu.VMEM((10, PIN), F32),
            pltpu.VMEM((10, D), F32),
            pltpu.VMEM((2, D, 2 * ROWS), BF),
            pltpu.VMEM((2, 2 * ROWS, HALF), BF),
            pltpu.VMEM((2, 4, 4, 80, HALF), BF),
            pltpu.VMEM((2, 3, 4, 80, HALF), BF),
            pltpu.VMEM((2, 4, 80, HALF), BF),
            pltpu.VMEM((2, 3, 80, HALF), BF),
            pltpu.VMEM((2, 80, HALF), BF),
            pltpu.VMEM((2, 80, HALF), BF),
            pltpu.VMEM((2, ROWS, HALF), BF),
            pltpu.VMEM((2, 7, 16, HALF), BF),
            dma((14,)),
            dma((2, 2, N_LLM)),
            dma((2, 2, N_LLM)),
            dma((4,)),
            dma((4,)),
            dma((2, 3, 3)),
            dma((2, 3, 3)),
            dma((2, 3, 3)),
            dma((2, 3, 3)),
            dma((2, 7)),
            dma((2, 7)),
            dma((2,)),
            dma((2,)),
        ],
        compiler_params=pltpu.CompilerParams(
            collective_id=0, has_side_effects=True, vmem_limit_bytes=56 * 1024 * 1024
        ),
    )(
        owner_slot.reshape(1, 128), place_start, image_seg, patches, text_embeds, merged_grad,
        w_patch, w_qkv, w_out,
    )
    merged, grad_patch, grad_out = pl.pallas_call(
        finish_kernel,
        out_shape=(
            jax.ShapeDtypeStruct((SEQ, D), BF),
            jax.ShapeDtypeStruct((10, PIN), F32),
            jax.ShapeDtypeStruct((10, D), F32),
        ),
        in_specs=[anywhere] * 3,
        out_specs=(anywhere, anywhere, anywhere),
        scratch_shapes=[
            pltpu.VMEM((SEQ, D), BF),
            pltpu.VMEM((10, PIN), F32),
            pltpu.VMEM((10, D), F32),
            dma((6,)),
        ],
    )(merged, grad_patch, grad_out)
    return (merged, grad_patch.T, grad_out.T)


def solution(mesh):
    rows = P(("llm", "enc"), None)
    columns = P(None, ("llm", "enc"))
    return jax.shard_map(
        shards,
        mesh=mesh,
        in_specs=(rows, P(), P(), rows, rows, rows, P(), P(), P()),
        out_specs=(rows, columns, columns),
        check_vma=False,
    )
```
